32 devices in a mesh: section: 4 (over x, core), tensor: 2 (over y), dp: 4 (over z).
Axes of the slice: x: 2, y: 2, z: 4, core: 2. Of those that a mesh axis runs over, the one named last changes fastest.
Arguments:
- hidden_in: bfloat16 [1, 512, 16384], P(None, 'dp', 'tensor'), may hold values from -6 to 6
- norm_gain: bfloat16 [4, 16384], P('section', 'tensor'), may hold values from 0.099609375 to 1.8984375
- trainer_kv: bfloat16 [4, 16384, 2048], P('section', ('tensor', 'dp')), may hold values from -0.046875 to 0.046875
- queries: bfloat16 [4, 1, 512, 16384], P('section', None, 'dp', 'tensor'), may hold values from -120 to 120
- kv_cache: bfloat16 [4, 1, 512, 16, 4096], P('section', None, 'dp', None, 'tensor'), may hold values from -4 to 4, as said below
- cache_lengths: int32 [1, 512], P(None, 'dp'), may hold values from 1 to 16, as said below
Outputs:
- rollout_kv: bfloat16 [4, 16384, 2048], P('section', None, 'tensor')
- section_out: bfloat16 [4, 1, 512, 16384], P('section', None, 'dp', 'tensor')
The draws below stay inside these ranges and needn't reach their ends.
Inputs may be any that keep to these rules, and one draw needn't show every extreme that they name: `kv_cache`: the two copies c = 0 and c = 1 of each head's keys and values are equal. `cache_lengths`: valid cache positions of each row; in every aligned block of 128 rows one row has 16 and one has 1.
All inputs are finite; a program needn't handle non-finite values.
Results may differ from the reference program's by a relative error of at most 0.0035.
The reference program's roundings to bfloat16 on the way count: a program that leaves them out, or rounds other values in their place, can miss the bound.
Values may be sent and summed in bfloat16 or wider, within the bound.
No kernel may reach another device: no remote copies, remote signals or barrier semaphores. Data moves between devices by JAX's collectives and lax.ppermute only.
A program may use at most 384 MiB of HBM per device.

```python
import jax
import jax.numpy as jnp
from jax import lax

D = 16384
KVH = 8
HD = 128
GQ = 16
GROUP = 128
ROWS = 128
MB = 1
LMAX = 16
SECTIONS = 4
ROWS_ALL = 512
QH = 128
KVW = 2048
CW = 4096


def draw_queries(key, part):
    key = jax.random.fold_in(key, 11)
    shape = (SECTIONS, MB, ROWS_ALL, KVH, GQ, HD)
    values = jax.random.truncated_normal(key, -4.0, 4.0, shape, jnp.float32)
    return values.reshape(SECTIONS, MB, ROWS_ALL, QH * HD).astype(jnp.bfloat16)


def draw_kv_cache(key, part):
    key = jax.random.fold_in(key, 12)
    shape = (SECTIONS, MB, ROWS_ALL, LMAX, KVH, 2, HD)
    values = jax.random.truncated_normal(key, -4.0, 4.0, shape, jnp.float32)
    doubled = jnp.broadcast_to(values[:, :, :, :, :, None, :, :], (SECTIONS, MB, ROWS_ALL, LMAX, KVH, 2, 2, HD))
    return doubled.reshape(SECTIONS, MB, ROWS_ALL, LMAX, CW).astype(jnp.bfloat16)


def draw_cache_lengths(key, part):
    key = jax.random.fold_in(key, 13)
    drawn = jax.random.randint(key, (MB, ROWS_ALL), 1, LMAX + 1, jnp.int32)
    row_ids = (jnp.arange(ROWS_ALL) % ROWS)[None, :]
    drawn = jnp.where(row_ids == 0, LMAX, drawn)
    drawn = jnp.where(row_ids == 1, 1, drawn)
    return drawn.astype(jnp.int32)


def steps_of(stream_key, extent, split, low, largest):
    gain, own = 1.0, jax.random.fold_in(stream_key, 6)
    for dim, parts in split:
        draws = jnp.exp(jax.random.uniform(jax.random.fold_in(own, dim), (parts,), jnp.float32, low / len(split), largest / len(split)))
        gain = gain * jnp.repeat(draws, extent[dim] // parts).reshape([-1 if axis == dim else 1 for axis in range(len(extent))])
    return gain


def scatter_about(key, extent, deviation, reach, shards=(), held_as=jnp.bfloat16):
    loudness = steps_of(key, extent, shards, -0.22, 0.18) if shards else 1.0
    entries = jax.random.normal(key, extent, jnp.float32) * deviation * loudness
    return jnp.minimum(jnp.maximum(entries, -reach), reach).astype(held_as)


def setup_inputs(seed: int = 0) -> dict:
    key_of = jax.random.split(jax.random.key(seed), 7)
    hidden_in = scatter_about(key_of[0], (MB, ROWS_ALL, D), 1.0, 6.0, ((1, 4), (2, 2)))
    norm_gain = jnp.clip(1.0 + 0.18 * jax.random.normal(key_of[1], (SECTIONS, D), jnp.float32), 0.099609375, 1.8984375).astype(jnp.bfloat16)
    trainer_kv = scatter_about(key_of[2], (SECTIONS, D, KVW), D ** -0.5, 0.046875, ((0, 4), (1, 8)))
    queries = draw_queries(jax.random.fold_in(key_of[6], 71), 0)
    kv_cache = draw_kv_cache(jax.random.fold_in(key_of[6], 71), 0)
    cache_lengths = draw_cache_lengths(jax.random.fold_in(key_of[6], 71), 0)
    return dict(hidden_in=hidden_in, norm_gain=norm_gain, trainer_kv=trainer_kv, queries=queries, kv_cache=kv_cache, cache_lengths=cache_lengths)


epsilon = 1e-05
clip_ratio = 2.0

def requantize(weight_block):
    row_count, width = weight_block.shape
    grouped = weight_block.astype(jnp.float32).reshape(row_count // GROUP, GROUP, width)
    group_level = lax.optimization_barrier(jnp.mean(jnp.abs(grouped), axis=1, keepdims=True))
    limited = jnp.clip(grouped, -clip_ratio * group_level, clip_ratio * group_level)
    return limited.reshape(row_count, width).astype(jnp.bfloat16)

def layer_step(current, gain_row, weight_cols, query_rows, cache_rows, length_rows):
    row_count = current.shape[0]
    half_group = GQ // 2
    current_wide = current.astype(jnp.float32)
    inverse_rms = lax.rsqrt(lax.optimization_barrier(jnp.mean(current_wide * current_wide, axis=1)) + epsilon)
    normed = (current_wide * inverse_rms[:, None] * gain_row.astype(jnp.float32)).astype(jnp.bfloat16)
    fresh = jnp.dot(normed, weight_cols, preferred_element_type=jnp.float32).astype(jnp.bfloat16)
    fresh_wide = lax.optimization_barrier(fresh).astype(jnp.float32).reshape(row_count, KVH, 2, HD)
    query_heads = query_rows.astype(jnp.float32).reshape(row_count, KVH, 2, half_group, HD)
    cache_view = cache_rows.astype(jnp.float32).reshape(row_count, LMAX, KVH, 2, 2, HD)
    cache_keys = cache_view[:, :, :, :, 0]
    cache_values = cache_view[:, :, :, :, 1]
    score_scale = HD ** (-0.5)
    old_scores = jnp.einsum('rhcgd,rlhcd->rhcgl', query_heads, cache_keys) * score_scale
    new_scores = jnp.einsum('rhcgd,rhd->rhcg', query_heads, fresh_wide[:, :, 0]) * score_scale
    visible = (jnp.arange(LMAX)[None, :] < length_rows[:, None])[:, None, None, None, :]
    old_scores = jnp.where(visible, old_scores, -jnp.inf)
    highest = jnp.maximum(lax.optimization_barrier(jnp.max(old_scores, axis=-1)), new_scores)
    old_weights = jnp.where(visible, jnp.exp(old_scores - highest[..., None]), 0.0)
    new_weights = jnp.exp(new_scores - highest)
    denominator = lax.optimization_barrier(jnp.sum(old_weights, axis=-1)) + new_weights
    old_probs = (old_weights / denominator[..., None]).astype(jnp.bfloat16)
    new_probs = (new_weights / denominator).astype(jnp.bfloat16)
    old_probs = lax.optimization_barrier(old_probs).astype(jnp.float32)
    new_probs = lax.optimization_barrier(new_probs).astype(jnp.float32)
    mixed = jnp.einsum('rhcgl,rlhcd->rhcgd', old_probs, cache_values)
    mixed = mixed + new_probs[..., None] * fresh_wide[:, :, 1][:, :, None, None, :]
    return (current_wide + mixed.reshape(row_count, D)).astype(jnp.bfloat16)

def reference(hidden_in, norm_gain, trainer_kv, queries, kv_cache, cache_lengths):
    rollout = [requantize(trainer_kv[section_id]) for section_id in range(SECTIONS)]
    sectioned = []
    current = hidden_in
    for section_id in range(SECTIONS):
        produced = []
        for micro_id in range(MB):
            produced.append(layer_step(current[micro_id], norm_gain[section_id], rollout[section_id], queries[section_id, micro_id], kv_cache[section_id, micro_id], cache_lengths[micro_id]))
        current = jnp.stack(produced)
        sectioned.append(current)
    return (jnp.stack(rollout), jnp.stack(sectioned))
```

```python
import functools

import jax
import jax.numpy as jnp
from jax import lax
from jax.experimental import pallas as pl
from jax.experimental.pallas import tpu as pltpu
from jax.sharding import PartitionSpec as P

D = 16384
KVH = 8
HD = 128
GQ = 16
GROUP = 128
LMAX = 16
HALF = GQ // 2
PAIR = 2 * HD
ROW_TILE = 16

epsilon = 1e-05
clip_ratio = 2.0
MIB = 1 << 20


def requantize_kernel(column_ref, w_ref, o_ref):
    for group in range(w_ref.shape[0] // GROUP):
        rows = slice(group * GROUP, (group + 1) * GROUP)
        block = w_ref[rows, :].astype(jnp.float32)
        limit = clip_ratio * (jnp.sum(jnp.abs(block), axis=0, keepdims=True) * (1.0 / GROUP))
        o_ref[rows, :] = jnp.clip(block, -limit, limit).astype(jnp.bfloat16)


def requantize(weight, column_block, width):
    rows = weight.shape[0]
    tile = min(rows, 4 * GROUP)
    return pl.pallas_call(
        requantize_kernel,
        out_shape=jax.ShapeDtypeStruct((rows, width), jnp.bfloat16),
        grid_spec=pltpu.PrefetchScalarGridSpec(
            num_scalar_prefetch=1,
            grid=(rows // tile,),
            in_specs=[pl.BlockSpec((tile, width), lambda i, column: (i, column[0]))],
            out_specs=pl.BlockSpec((tile, width), lambda i, column: (i, 0)),
        ),
        compiler_params=pltpu.CompilerParams(vmem_limit_bytes=32 * MIB),
        cost_estimate=pl.CostEstimate(
            flops=4 * rows * width, bytes_accessed=4 * rows * width, transcendentals=0
        ),
    )(column_block.reshape(1), weight)


def partial_kernel(count, *refs):
    x_refs, (gain_ref, w_ref, o_ref, normed) = refs[:count], refs[count:]
    rows = x_refs[0].shape[0]

    @pl.when(pl.program_id(0) == 0)
    def _():
        gain = gain_ref[...].astype(jnp.float32)
        for b in range(count):
            scaled = x_refs[b][...].astype(jnp.float32) * gain
            normed[b * rows : (b + 1) * rows, :] = scaled.astype(jnp.bfloat16)

    o_ref[...] = jnp.dot(normed[...], w_ref[...], preferred_element_type=jnp.float32).astype(o_ref.dtype)


def partial_product(blocks, gain, weight, dtype):
    count = len(blocks)
    rows, depth = blocks[0].shape
    width = weight.shape[1]
    tile = min(width, 256)
    whole = pl.BlockSpec((rows, depth), lambda i: (0, 0))
    return pl.pallas_call(
        functools.partial(partial_kernel, count),
        out_shape=jax.ShapeDtypeStruct((count * rows, width), dtype),
        grid=(width // tile,),
        in_specs=[whole] * count
        + [pl.BlockSpec((1, depth), lambda i: (0, 0)), pl.BlockSpec((depth, tile), lambda i: (0, i))],
        out_specs=pl.BlockSpec((count * rows, tile), lambda i: (0, i)),
        scratch_shapes=[pltpu.VMEM((count * rows, depth), jnp.bfloat16)],
        compiler_params=pltpu.CompilerParams(vmem_limit_bytes=32 * MIB),
        cost_estimate=pl.CostEstimate(
            flops=2 * count * rows * depth * width,
            bytes_accessed=2 * depth * (width + count * rows) + 2 * count * rows * width,
            transcendentals=0,
        ),
    )(*blocks, gain, weight)


def attend_kernel(valid_ref, x_ref, q_ref, c_ref, f_ref, o_ref):
    heads = q_ref.shape[1] // HD
    query = jnp.concatenate([q_ref[:, i * HD : (i + 1) * HD] for i in range(heads)], axis=0)
    keys = c_ref[:, :, :HD].reshape(ROW_TILE * LMAX, HD)
    values = c_ref[:, :, HD:].reshape(ROW_TILE * LMAX, HD)
    fresh = f_ref[...].astype(jnp.float32)
    new_key = jnp.concatenate([fresh[:, :HD]] * heads, axis=0)
    new_value = jnp.concatenate([fresh[:, HD:]] * heads, axis=0)
    scale = HD ** (-0.5)
    shape = (heads * ROW_TILE, ROW_TILE * LMAX)
    owner = lax.rem(lax.broadcasted_iota(jnp.int32, shape, 0), ROW_TILE)
    column = lax.broadcasted_iota(jnp.int32, shape, 1)
    seen = (owner * LMAX <= column) & (column < owner * LMAX + valid_ref[0])
    old = lax.dot_general(query, keys, (((1,), (1,)), ((), ())), preferred_element_type=jnp.float32)
    old = jnp.where(seen, old * scale, -jnp.inf)
    new = jnp.sum(query.astype(jnp.float32) * new_key, axis=1, keepdims=True) * scale
    highest = jnp.maximum(jnp.max(old, axis=1, keepdims=True), new)
    old = jnp.where(seen, jnp.exp(old - highest), 0.0)
    new = jnp.exp(new - highest)
    inverse = 1.0 / (jnp.sum(old, axis=1, keepdims=True) + new)
    old = (old * inverse).astype(jnp.bfloat16)
    new = (new * inverse).astype(jnp.bfloat16).astype(jnp.float32)
    mixed = jnp.dot(old, values, preferred_element_type=jnp.float32) + new * new_value
    for i in range(heads):
        columns = slice(i * HD, (i + 1) * HD)
        total = x_ref[:, columns].astype(jnp.float32) + mixed[i * ROW_TILE : (i + 1) * ROW_TILE, :]
        o_ref[:, columns] = total.astype(jnp.bfloat16)


def attend(current, query, cache, length_columns, fresh):
    rows, width = query.shape
    pairs = width // (HALF * HD)
    share = min(2, pairs)
    heads = share * HALF
    wide = pl.BlockSpec((ROW_TILE, heads * HD), lambda i, g: (i, g))
    return pl.pallas_call(
        attend_kernel,
        out_shape=jax.ShapeDtypeStruct((rows, width), jnp.bfloat16),
        grid=(rows // ROW_TILE, pairs // share),
        in_specs=[
            pl.BlockSpec((1, 1, ROW_TILE * LMAX), lambda i, g: (i, 0, 0)),
            wide,
            wide,
            pl.BlockSpec((ROW_TILE, LMAX, PAIR), lambda i, g: (i, 0, share * g)),
            pl.BlockSpec((ROW_TILE, PAIR), lambda i, g: (i, g)),
        ],
        out_specs=wide,
        compiler_params=pltpu.CompilerParams(vmem_limit_bytes=32 * MIB),
        cost_estimate=pl.CostEstimate(
            flops=4 * rows * pairs * HALF * HD * ROW_TILE * LMAX,
            bytes_accessed=6 * rows * width + cache.size * 2 // share,
            transcendentals=rows * pairs * HALF * ROW_TILE * LMAX,
        ),
    )(length_columns, current, query, cache, fresh)


def body(hidden_in, norm_gain, trainer_kv, queries, kv_cache, cache_lengths):
    sections, tensors, dps = (lax.axis_size(axis) for axis in ("section", "tensor", "dp"))
    section, tensor, dp = (lax.axis_index(axis) for axis in ("section", "tensor", "dp"))
    rows, local_width = hidden_in.shape[1:]
    depth = trainer_kv.shape[1]
    own_width = 2 * KVH * HD // tensors
    served = max(own_width, PAIR)

    def over_dp(value, source_section, target_section, flip):
        pairs = [(source_section * dps + z, target_section * dps + (z ^ flip)) for z in range(dps)]
        return lax.ppermute(value, ("section", "dp"), pairs)

    def over_tensor(value, at_section, flip):
        pairs = [(at_section * tensors + t, at_section * tensors + (t ^ flip)) for t in range(tensors)]
        return lax.ppermute(value, ("section", "tensor"), pairs)

    def feature_block(value, flip):
        return lax.dynamic_slice_in_dim(value, (dp ^ flip) * depth, depth, 1)

    first = [feature_block(hidden_in[0], b) for b in range(dps)]
    weight, first = lax.optimization_barrier((trainer_kv[0], first))

    def kept_columns(j):
        return requantize(weight, (tensor ^ j) * own_width // served, served)

    def gather(part):
        return lax.all_gather(part, "dp", axis=0, tiled=False)

    kept = [kept_columns(0)]
    gathered = [(0, 0, gather(kept[0]))]
    for j in range(1, tensors):
        weight, _ = lax.optimization_barrier((weight, kept[-1]))
        kept.append(kept_columns(j))
    served_rows = [
        lax.ppermute(kept[j], "tensor", [(t, t ^ j) for t in range(tensors)]) for j in range(1, tensors)
    ]

    length = jnp.repeat(cache_lengths[0], LMAX).reshape(rows // ROW_TILE, 1, ROW_TILE * LMAX)
    gain = lax.dynamic_slice_in_dim(norm_gain, dp * depth, depth, 1)
    result = None
    for tick in range(sections):
        if tick == 0:
            current = hidden_in[0]
            blocks = first[:1] + [over_dp(first[b], 0, 0, b) for b in range(1, dps)]
        else:
            blocks = [over_dp(feature_block(carried, b), tick - 1, tick, b) for b in range(dps)]
            current = over_dp(carried, tick - 1, tick, 0)
        sent = [
            over_tensor(partial_product(blocks, gain, kept[j], jnp.bfloat16), tick, j)
            for j in range(1, tensors)
        ]
        total = partial_product(blocks, gain, kept[0], jnp.float32)
        wide = current.astype(jnp.float32)
        squares = jnp.sum(wide * wide, axis=1)
        for j in range(1, tensors):
            total = total + sent[j - 1].astype(jnp.float32)
        for j in (2**i for i in range(tensors.bit_length() - 1)):
            squares = squares + over_tensor(squares, tick, j)
        total = total.reshape(dps, rows, served)
        returned = [over_dp(total[b].astype(jnp.bfloat16), tick, tick, b) for b in range(1, dps)]
        inverse = lax.rsqrt(squares / D + epsilon)
        fresh = total[0]
        for part in returned:
            fresh = fresh + part.astype(jnp.float32)
        fresh = (fresh * inverse[:, None]).astype(jnp.bfloat16)
        carried = attend(current, queries[0, 0], kv_cache[0, 0], length, fresh)
        result = carried if result is None else jnp.where(section == tick, carried, result)
        if tick == 0:
            served_rows, carried = lax.optimization_barrier((served_rows, carried))
            for j in range(1, tensors):
                pieces = 2 if j == tensors - 1 else 1
                cut = depth // pieces
                for start in range(0, depth, cut):
                    gathered.append((j, start, gather(served_rows[j - 1][start : start + cut])))
        if tick == sections - 2:
            own_rows, carried = lax.optimization_barrier((gathered[0][2], carried))
            gathered[0] = (0, 0, own_rows)

    parts, result = lax.optimization_barrier(([part for _, _, part in gathered], result))
    rollout = jnp.zeros((tensors, dps, depth, own_width), jnp.bfloat16)
    for (j, start, _), part in zip(gathered, parts):
        if own_width < served:
            part = lax.dynamic_slice_in_dim(part, tensor * own_width % served, own_width, 2)
        rollout = lax.dynamic_update_slice(rollout, part[None], (tensor ^ j, 0, start, 0))
    return (rollout.reshape(1, D, own_width), result[None, None])


def solution(mesh):
    placed = (
        P(None, "dp", "tensor"),
        P("section", "tensor"),
        P("section", ("tensor", "dp"), None),
        P("section", None, "dp", "tensor"),
        P("section", None, "dp", None, "tensor"),
        P(None, "dp"),
    )
    return jax.shard_map(
        body,
        mesh=mesh,
        in_specs=placed,
        out_specs=(P("section", None, "tensor"), P("section", None, "dp", "tensor")),
        check_vma=False,
    )
```

```python
import functools

import jax
import jax.numpy as jnp
from jax import lax
from jax.experimental import pallas as pl
from jax.experimental.pallas import tpu as pltpu
from jax.sharding import PartitionSpec as P

D = 16384
KVH = 8
HD = 128
GQ = 16
GROUP = 128
LMAX = 16
HALF = GQ // 2
PAIR = 2 * HD
ROW_TILE = 16

epsilon = 1e-05
clip_ratio = 2.0
MIB = 1 << 20
SHORT = pl.CostEstimate(flops=0, bytes_accessed=0, transcendentals=0)


def requantize_kernel(column_ref, w_ref, o_ref):
    for group in range(w_ref.shape[0] // GROUP):
        rows = slice(group * GROUP, (group + 1) * GROUP)
        block = w_ref[rows, :].astype(jnp.float32)
        limit = clip_ratio * (jnp.sum(jnp.abs(block), axis=0, keepdims=True) * (1.0 / GROUP))
        o_ref[rows, :] = jnp.clip(block, -limit, limit).astype(jnp.bfloat16)


def requantize(weight, column_block, width):
    rows = weight.shape[0]
    tile = min(rows, 4 * GROUP)
    return pl.pallas_call(
        requantize_kernel,
        out_shape=jax.ShapeDtypeStruct((rows, width), jnp.bfloat16),
        grid_spec=pltpu.PrefetchScalarGridSpec(
            num_scalar_prefetch=1,
            grid=(rows // tile,),
            in_specs=[pl.BlockSpec((tile, width), lambda i, column: (i, column[0]))],
            out_specs=pl.BlockSpec((tile, width), lambda i, column: (i, 0)),
        ),
        compiler_params=pltpu.CompilerParams(vmem_limit_bytes=32 * MIB),
        cost_estimate=SHORT,
    )(column_block.reshape(1), weight)


def project_kernel(layout, lhs_count, has_total, offset_ref, *refs):
    lhs = refs[:lhs_count]
    blocks = refs[lhs_count : lhs_count + len(layout)]
    total = refs[lhs_count + len(layout)][...] if has_total else None
    i = 0
    for block, segments in zip(blocks, layout):
        for j, start, depth in segments:
            columns = pl.ds(pl.multiple_of(offset_ref[i], GROUP), depth)
            term = jnp.dot(
                lhs[j][:, columns], block[start : start + depth, :], preferred_element_type=jnp.float32
            )
            total = term if total is None else total + term
            i += 1
    refs[-1][...] = total


def project(lhs, terms, total=None):
    rows = lhs[0].shape[0]
    width = terms[0][0].shape[1]
    tile = min(width, 256)
    offsets = jnp.stack([jnp.asarray(offset, jnp.int32) for _, segments in terms for _, offset, _, _ in segments])
    layout = [[(j, start, depth) for j, _, start, depth in segments] for _, segments in terms]
    added = () if total is None else (total,)
    column = lambda i, offset: (0, i)
    return pl.pallas_call(
        functools.partial(project_kernel, layout, len(lhs), total is not None),
        out_shape=jax.ShapeDtypeStruct((rows, width), jnp.float32),
        grid_spec=pltpu.PrefetchScalarGridSpec(
            num_scalar_prefetch=1,
            grid=(width // tile,),
            in_specs=[pl.BlockSpec(part.shape, lambda i, offset: (0, 0)) for part in lhs]
            + [pl.BlockSpec((block.shape[0], tile), column) for block, _ in terms]
            + [pl.BlockSpec((rows, tile), column) for _ in added],
            out_specs=pl.BlockSpec((rows, tile), column),
        ),
        compiler_params=pltpu.CompilerParams(vmem_limit_bytes=48 * MIB),
        cost_estimate=SHORT,
    )(offsets, *lhs, *[block for block, _ in terms], *added)


def place_kernel(layout, width, where_ref, *refs):
    blocks, out, sems = refs[: len(layout)], refs[-2], refs[-1]

    @pl.when(where_ref[0] == 1)
    def _():
        copies = []
        for block, segments in zip(blocks, layout):
            for start, depth in segments:
                i = len(copies)
                rows = pl.ds(pl.multiple_of(where_ref[2 + i], GROUP), depth)
                columns = pl.ds(0, width)
                if width < block.shape[1]:
                    columns = pl.ds(pl.multiple_of(where_ref[1], HD), width)
                copies.append(
                    pltpu.make_async_copy(block.at[pl.ds(start, depth), columns], out.at[rows], sems.at[i])
                )
        for copy in copies:
            copy.start()
        for copy in copies:
            copy.wait()


def place(rollout, width, active, column, terms, waits=()):
    rows = [row for _, segments in terms for row, _, _ in segments]
    layout = [[(start, depth) for _, start, depth in segments] for _, segments in terms]
    where = jnp.stack([jnp.asarray(v, jnp.int32) for v in (active, column, *rows)])
    held = tuple(waits) if rollout is None else (*waits, rollout)
    anywhere = pl.BlockSpec(memory_space=pl.ANY)
    return pl.pallas_call(
        functools.partial(place_kernel, layout, width),
        out_shape=jax.ShapeDtypeStruct((D, width), jnp.bfloat16),
        grid_spec=pltpu.PrefetchScalarGridSpec(
            num_scalar_prefetch=1,
            grid=(1,),
            in_specs=[anywhere] * (len(terms) + len(held)),
            out_specs=anywhere,
            scratch_shapes=[pltpu.SemaphoreType.DMA((len(rows),))],
        ),
        input_output_aliases={} if rollout is None else {len(terms) + len(held): 0},
        cost_estimate=SHORT,
    )(where, *[block for block, _ in terms], *held)


def attend_kernel(valid_ref, x_ref, q_ref, c_ref, f_ref, o_ref):
    heads = q_ref.shape[1] // HD
    query = jnp.concatenate([q_ref[:, i * HD : (i + 1) * HD] for i in range(heads)], axis=0)
    keys = c_ref[:, :, :HD].reshape(ROW_TILE * LMAX, HD)
    values = c_ref[:, :, HD:].reshape(ROW_TILE * LMAX, HD)
    fresh = f_ref[...].astype(jnp.float32)
    new_key = jnp.concatenate([fresh[:, :HD]] * heads, axis=0)
    new_value = jnp.concatenate([fresh[:, HD:]] * heads, axis=0)
    scale = HD ** (-0.5)
    shape = (heads * ROW_TILE, ROW_TILE * LMAX)
    owner = lax.rem(lax.broadcasted_iota(jnp.int32, shape, 0), ROW_TILE)
    column = lax.broadcasted_iota(jnp.int32, shape, 1)
    seen = (owner * LMAX <= column) & (column < owner * LMAX + valid_ref[0])
    old = lax.dot_general(query, keys, (((1,), (1,)), ((), ())), preferred_element_type=jnp.float32)
    old = jnp.where(seen, old * scale, -jnp.inf)
    new = jnp.sum(query.astype(jnp.float32) * new_key, axis=1, keepdims=True) * scale
    highest = jnp.maximum(jnp.max(old, axis=1, keepdims=True), new)
    old = jnp.where(seen, jnp.exp(old - highest), 0.0)
    new = jnp.exp(new - highest)
    inverse = 1.0 / (jnp.sum(old, axis=1, keepdims=True) + new)
    old = (old * inverse).astype(jnp.bfloat16)
    new = (new * inverse).astype(jnp.bfloat16).astype(jnp.float32)
    mixed = jnp.dot(old, values, preferred_element_type=jnp.float32) + new * new_value
    for i in range(heads):
        columns = slice(i * HD, (i + 1) * HD)
        total = x_ref[:, columns].astype(jnp.float32) + mixed[i * ROW_TILE : (i + 1) * ROW_TILE, :]
        o_ref[:, columns] = total.astype(jnp.bfloat16)


def attend(current, query, cache, length_columns, fresh):
    rows, width = query.shape
    pairs = width // (HALF * HD)
    share = min(2, pairs)
    heads = share * HALF
    wide = pl.BlockSpec((ROW_TILE, heads * HD), lambda i, g: (i, g))
    return pl.pallas_call(
        attend_kernel,
        out_shape=jax.ShapeDtypeStruct((rows, width), jnp.bfloat16),
        grid=(rows // ROW_TILE, pairs // share),
        in_specs=[
            pl.BlockSpec((1, 1, ROW_TILE * LMAX), lambda i, g: (i, 0, 0)),
            wide,
            wide,
            pl.BlockSpec((ROW_TILE, LMAX, PAIR), lambda i, g: (i, 0, share * g)),
            pl.BlockSpec((ROW_TILE, PAIR), lambda i, g: (i, g)),
        ],
        out_specs=wide,
        compiler_params=pltpu.CompilerParams(vmem_limit_bytes=32 * MIB),
        cost_estimate=SHORT,
    )(length_columns, current, query, cache, fresh)


def together(*values):
    return lax.optimization_barrier(values)


def body(hidden_in, norm_gain, trainer_kv, queries, kv_cache, cache_lengths):
    sections, tensors, dps = (lax.axis_size(axis) for axis in ("section", "tensor", "dp"))
    section, tensor, dp = (lax.axis_index(axis) for axis in ("section", "tensor", "dp"))
    rows = hidden_in.shape[1]
    depth = trainer_kv.shape[1]
    own_width = 2 * KVH * HD // tensors
    served = max(own_width, PAIR)
    early, late = (1, 2), (0, 3)
    everyone = tuple(range(sections))
    is_early = ((section == 1) | (section == 2)).astype(jnp.int32)
    inner = (dp == 1) | (dp == 2)

    def over(axis, count, value, routes):
        pairs = [(a * count + i, b * count + j) for a, b, i, j in routes]
        return lax.ppermute(value, ("section", axis), pairs)

    def over_dp(value, at, target):
        return over("dp", dps, value, [(s, s, z, target[z]) for s in at for z in range(dps)])

    def over_tensor(value, at, flip, step=0):
        return over("tensor", tensors, value, [(s, s + step, t, t ^ flip) for s in at for t in range(tensors)])

    def flipped(b):
        return [z ^ b for z in range(dps)]

    def feature_block(value, b):
        return lax.dynamic_slice_in_dim(value, (dp ^ b) * depth, depth, 1)

    def normed_of(parts, inverse, gains):
        return [
            (part.astype(jnp.float32) * inverse[:, None] * gain.astype(jnp.float32)).astype(jnp.bfloat16)
            for part, gain in zip(parts, gains)
        ]

    def square_sum(part):
        wide = part.astype(jnp.float32)
        return jnp.sum(wide * wide, axis=1)

    length = jnp.repeat(cache_lengths[0], LMAX).reshape(rows // ROW_TILE, 1, ROW_TILE * LMAX)

    def attended(current, fresh):
        return attend(current, queries[0, 0], kv_cache[0, 0], length, fresh.astype(jnp.bfloat16))

    def hop(value, tick):
        return [over_tensor(value, (tick - 1,), j, 1) for j in range(tensors)]

    def prepared(parts):
        inverse = lax.rsqrt(sum(square_sum(part) for part in parts) / D + epsilon)
        return normed_of(parts, inverse, gains)

    halves = [[(0, 0)], [(j, (j - 1) * depth) for j in range(1, tensors)]]

    def straight(at, block):
        return {0: block, 3: over_dp(block, at, flipped(3)), 1: over_dp(block, at, flipped(1))}

    def relayed(at, blocks):
        return over_dp(jnp.where(inner, blocks[3], blocks[0]), at, (2, 0, 3, 1))

    def terms_of(half, blocks, which):
        return [
            (blocks[b], [(j, (dp ^ b) * depth, start, depth) for j, start in halves[half]]) for b in which
        ]

    def put(rollout, active, half, blocks, which, waits=()):
        places = [
            (blocks[b], [(((tensor ^ j) * dps + (dp ^ b)) * depth, start, depth) for j, start in halves[half]])
            for b in which
        ]
        return place(rollout, own_width, active, tensor * own_width % served, places, waits)

    weight, hidden, kept = trainer_kv[0], hidden_in[0], []
    for j in range(tensors):
        kept.append(requantize(weight, (tensor ^ j) * own_width // served, served))
        weight, hidden, kept[-1] = together(weight, hidden, kept[-1])

    squares = square_sum(hidden)
    for j in (2**i for i in range(tensors.bit_length() - 1)):
        squares = squares + over_tensor(squares, (0,), j)
    (normed,) = normed_of([hidden], lax.rsqrt(squares / D + epsilon), [norm_gain])
    first = [feature_block(normed, b) for b in range(dps)]
    first[1:] = [over_dp(first[b], (0,), flipped(b)) for b in range(1, dps)]
    gains = [norm_gain] + [over_tensor(norm_gain, everyone, j) for j in range(1, tensors)]

    def others(at, kept):
        received = [over_tensor(kept[j], at, j) for j in range(1, tensors)]
        return received[0] if len(received) == 1 else jnp.concatenate(received, axis=0)

    early_own = straight(early, kept[0])

    lhs = [jnp.concatenate(first, axis=0)]
    partial = [project(lhs, [(kept[j], [(0, 0, 0, depth)])]) for j in range(tensors)]
    partial, kept = together(partial, kept)
    early_rest = others(early, kept)
    total = partial[0]
    for j in range(1, tensors):
        total = total + over_tensor(partial[j], (0,), j)
    total = total.reshape(dps, rows, served)
    returned = [over_dp(total[b].astype(jnp.bfloat16), (0,), flipped(b)) for b in range(1, dps)]
    fresh = total[0]
    for part in returned:
        fresh = fresh + part.astype(jnp.float32)
    result = carried = attended(hidden, fresh)

    early_own, early_rest, carried, kept = together(early_own, early_rest, carried, kept)
    moved = hop(carried, 1)
    early_other = straight(early, early_rest)
    early_own[2] = relayed(early, early_own)
    late_rest = others(late, kept)

    early_own, early_other, late_rest = together(early_own, early_other, late_rest)
    early_other[2] = relayed(early, early_other)
    token = over("dp", dps, early_other[3][:ROW_TILE, :HD], [(a, b, z, z) for a, b in ((1, 0), (2, 3)) for z in range(dps)])
    rollout = put(None, 1, 0, {0: kept[0]}, (0,), (token,))
    late_block, rollout = together(kept[0], rollout)
    late_own = straight(late, late_block)
    rollout = put(rollout, is_early, 0, early_own, (1, 2, 3))
    moved, rollout, early_other = together(moved, rollout, early_other)
    rollout = put(rollout, is_early, 1, early_other, (0, 1, 2, 3))

    terms = terms_of(0, early_own, range(dps)) + terms_of(1, early_other, range(dps))
    carried = attended(moved[0], project(prepared(moved), terms))
    result = jnp.where(section == 1, carried, result)

    late_own, carried, rollout = together(late_own, carried, rollout)
    moved = hop(carried, 2)
    late_other = straight(late, late_rest)
    late_own[2] = relayed(late, late_own)
    carried = attended(moved[0], project(prepared(moved), terms))
    result = jnp.where(section == 2, carried, result)
    moved = hop(carried, 3)

    normed = prepared(moved)
    late_other, late_own, normed, result = together(late_other, late_own, normed, result)
    late_other[2] = relayed(late, late_other)
    fresh = project(normed, terms_of(0, late_own, range(dps)) + terms_of(1, late_other, (0, 1, 3)))
    rollout = put(rollout, 1 - is_early, 0, late_own, (1, 2, 3))
    rollout = put(rollout, 1 - is_early, 1, late_other, (0, 1, 3))
    fresh, rollout, last = together(fresh, rollout, late_other[2])
    late_other[2] = last
    fresh = project(normed, terms_of(1, late_other, (2,)), fresh)
    rollout = put(rollout, 1 - is_early, 1, late_other, (2,))
    result = jnp.where(section == 3, attended(moved[0], fresh), result)
    return (rollout[None], result[None, None])


def solution(mesh):
    placed = (
        P(None, "dp", "tensor"),
        P("section", "tensor"),
        P("section", ("tensor", "dp"), None),
        P("section", None, "dp", "tensor"),
        P("section", None, "dp", None, "tensor"),
        P(None, "dp"),
    )
    return jax.shard_map(
        body,
        mesh=mesh,
        in_specs=placed,
        out_specs=(P("section", None, "tensor"), P("section", None, "dp", "tensor")),
        check_vma=False,
    )
```

```python
import functools

import jax
import jax.numpy as jnp
from jax import lax
from jax.experimental import pallas as pl
from jax.experimental.pallas import tpu as pltpu
from jax.sharding import PartitionSpec as P

D = 16384
KVH = 8
HD = 128
GQ = 16
GROUP = 128
LMAX = 16
HALF = GQ // 2
PAIR = 2 * HD
ROW_TILE = 16

epsilon = 1e-05
clip_ratio = 2.0
VMEM = 60 << 20
SHORT = pl.CostEstimate(flops=0, bytes_accessed=0, transcendentals=0)


def requantize_kernel(column_ref, w_ref, *o_refs):
    width = o_refs[0].shape[1]
    for j, o_ref in enumerate(o_refs):
        columns = pl.ds(pl.multiple_of(column_ref[j], HD), width)
        for start in range(0, w_ref.shape[0], GROUP):
            block = w_ref[start : start + GROUP, columns].astype(jnp.float32)
            limit = clip_ratio * (jnp.sum(jnp.abs(block), axis=0, keepdims=True) * (1.0 / GROUP))
            o_ref[start : start + GROUP, :] = jnp.clip(block, -limit, limit).astype(jnp.bfloat16)


def requantize(weight, columns, width):
    rows, whole = weight.shape
    tile = min(rows, 2 * GROUP)
    return pl.pallas_call(
        requantize_kernel,
        out_shape=[jax.ShapeDtypeStruct((rows, width), jnp.bfloat16)] * len(columns),
        grid_spec=pltpu.PrefetchScalarGridSpec(
            num_scalar_prefetch=1,
            grid=(rows // tile,),
            in_specs=[pl.BlockSpec((tile, whole), lambda i, columns: (i, 0))],
            out_specs=[pl.BlockSpec((tile, width), lambda i, columns: (i, 0))] * len(columns),
        ),
        compiler_params=pltpu.CompilerParams(vmem_limit_bytes=VMEM),
        cost_estimate=SHORT,
    )(jnp.stack(columns), weight)


def project_kernel(layout, lhs_count, has_total, has_held, placed, where_ref, *refs):
    lhs = refs[:lhs_count]
    blocks = refs[lhs_count : lhs_count + len(layout)]
    rest = list(refs[lhs_count + len(layout) :])
    total = rest.pop(0)[...] if has_total else None
    if has_held:
        rest.pop(0)
    o_ref = rest.pop(0)
    segments = [(block, *segment) for block, of_block in zip(blocks, layout) for segment in of_block]

    def copies():
        out, sems = rest
        width = min(out.shape[1], o_ref.shape[1])
        for i, (block, _, start, depth) in enumerate(segments):
            rows = pl.ds(pl.multiple_of(where_ref[2 + 2 * i + 1], GROUP), depth)
            columns = pl.ds(pl.multiple_of(pl.program_id(0) * width, HD), width)
            source = block.at[pl.ds(start, depth)]
            if width < block.shape[1]:
                source = block.at[pl.ds(start, depth), pl.ds(pl.multiple_of(where_ref[1], HD), width)]
            yield pltpu.make_async_copy(source, out.at[rows, columns], sems.at[i])

    if placed:

        @pl.when(where_ref[0] == 1)
        def _():
            for copy in copies():
                copy.start()

    for i, (block, j, start, depth) in enumerate(segments):
        columns = pl.ds(pl.multiple_of(where_ref[2 + 2 * i], GROUP), depth)
        term = jnp.dot(lhs[j][:, columns], block[start : start + depth, :], preferred_element_type=jnp.float32)
        total = term if total is None else total + term
    o_ref[...] = total

    if placed:

        @pl.when(where_ref[0] == 1)
        def _():
            for copy in copies():
                copy.wait()


def project(lhs, terms, total=None, placing=None, rollout=None):
    rows = lhs[0].shape[0]
    served = terms[0][0].shape[1]
    tile = min(served, 256)
    active, first_column, width = placing or (0, 0, 0)
    where = [active, first_column]
    for _, segments in terms:
        for _, offset, row, _, _ in segments:
            where += [offset, row]
    layout = [[(j, start, depth) for j, _, _, start, depth in segments] for _, segments in terms]
    count = sum(len(segments) for segments in layout)
    added = () if total is None else (total,)
    held = () if rollout is None else (rollout,)
    column = lambda i, where: (0, i)
    anywhere = pl.BlockSpec(memory_space=pl.ANY)
    fresh_shape, fresh_spec = jax.ShapeDtypeStruct((rows, served), jnp.float32), pl.BlockSpec((rows, tile), column)
    return pl.pallas_call(
        functools.partial(project_kernel, layout, len(lhs), bool(added), bool(held), placing is not None),
        out_shape=[fresh_shape, jax.ShapeDtypeStruct((D, width), jnp.bfloat16)] if placing else fresh_shape,
        grid_spec=pltpu.PrefetchScalarGridSpec(
            num_scalar_prefetch=1,
            grid=(served // tile,),
            in_specs=[pl.BlockSpec(part.shape, lambda i, where: (0, 0)) for part in lhs]
            + [pl.BlockSpec((block.shape[0], tile), column) for block, _ in terms]
            + [fresh_spec for _ in added]
            + [anywhere for _ in held],
            out_specs=[fresh_spec, anywhere] if placing else fresh_spec,
            scratch_shapes=[pltpu.SemaphoreType.DMA((count,))] if placing else [],
        ),
        input_output_aliases={1 + len(lhs) + len(terms) + len(added): 1} if held else {},
        compiler_params=pltpu.CompilerParams(vmem_limit_bytes=VMEM),
        cost_estimate=SHORT,
    )(jnp.stack([jnp.asarray(v, jnp.int32) for v in where]), *lhs, *[block for block, _ in terms], *added, *held)


def attend_kernel(share, bias_ref, x_ref, q_ref, c_ref, f_ref, o_ref):
    heads = share * HALF
    bias = bias_ref[0]
    scale = HD ** (-0.5)
    for g in range(q_ref.shape[1] // (heads * HD)):
        lanes = [slice((g * heads + i) * HD, (g * heads + i + 1) * HD) for i in range(heads)]
        query = jnp.concatenate([q_ref[:, lane] for lane in lanes], axis=0)
        at = g * share * PAIR
        keys = c_ref[:, :, at : at + HD].reshape(ROW_TILE * LMAX, HD)
        values = c_ref[:, :, at + HD : at + PAIR].reshape(ROW_TILE * LMAX, HD)
        fresh = f_ref[:, g * PAIR : (g + 1) * PAIR].astype(jnp.bfloat16).astype(jnp.float32)
        new_key = jnp.concatenate([fresh[:, :HD]] * heads, axis=0)
        new_value = jnp.concatenate([fresh[:, HD:]] * heads, axis=0)
        old = lax.dot_general(query, keys, (((1,), (1,)), ((), ())), preferred_element_type=jnp.float32)
        old = old * scale + bias
        new = jnp.sum(query.astype(jnp.float32) * new_key, axis=1, keepdims=True) * scale
        highest = jnp.maximum(jnp.max(old, axis=1, keepdims=True), new)
        old = jnp.exp(old - highest)
        new = jnp.exp(new - highest)
        inverse = 1.0 / (jnp.sum(old, axis=1, keepdims=True) + new)
        old = (old * inverse).astype(jnp.bfloat16)
        new = (new * inverse).astype(jnp.bfloat16).astype(jnp.float32)
        mixed = jnp.dot(old, values, preferred_element_type=jnp.float32) + new * new_value
        for i, lane in enumerate(lanes):
            total = x_ref[:, lane].astype(jnp.float32) + mixed[i * ROW_TILE : (i + 1) * ROW_TILE, :]
            o_ref[:, lane] = total.astype(jnp.bfloat16)


def seen_bias(lengths, heads):
    owner = jnp.arange(ROW_TILE)
    own = (owner[:, None, None] == owner[None, :, None]) & jnp.ones((1, 1, LMAX), bool)
    seen = jnp.arange(LMAX)[None, None, None, :] < lengths.reshape(-1, ROW_TILE, 1, 1)
    bias = jnp.where(own[None] & seen, 0.0, -jnp.inf).astype(jnp.float32)
    bias = jnp.broadcast_to(bias[:, None], (bias.shape[0], heads, ROW_TILE, ROW_TILE, LMAX))
    return bias.reshape(-1, heads * ROW_TILE, ROW_TILE * LMAX)


def attend(current, query, cache, bias, fresh):
    rows, width = query.shape
    share = min(2, width // (HALF * HD))
    wide = pl.BlockSpec((ROW_TILE, width), lambda i: (i, 0))
    return pl.pallas_call(
        functools.partial(attend_kernel, share),
        out_shape=jax.ShapeDtypeStruct((rows, width), jnp.bfloat16),
        grid=(rows // ROW_TILE,),
        in_specs=[
            pl.BlockSpec((1, *bias.shape[1:]), lambda i: (i, 0, 0)),
            wide,
            wide,
            pl.BlockSpec((ROW_TILE, LMAX, cache.shape[2]), lambda i: (i, 0, 0)),
            pl.BlockSpec((ROW_TILE, fresh.shape[1]), lambda i: (i, 0)),
        ],
        out_specs=wide,
        compiler_params=pltpu.CompilerParams(vmem_limit_bytes=VMEM),
        cost_estimate=SHORT,
    )(bias, current, query, cache, fresh)


def together(*values):
    return lax.optimization_barrier(values)


def body(hidden_in, norm_gain, trainer_kv, queries, kv_cache, cache_lengths):
    sections, tensors, dps = (lax.axis_size(axis) for axis in ("section", "tensor", "dp"))
    section, tensor, dp = (lax.axis_index(axis) for axis in ("section", "tensor", "dp"))
    rows = hidden_in.shape[1]
    depth = trainer_kv.shape[1]
    own_width = 2 * KVH * HD // tensors
    served = max(own_width, PAIR)
    early, late = (1, 2), (0, 3)
    everyone = tuple(range(sections))
    is_early = ((section == 1) | (section == 2)).astype(jnp.int32)
    inner = (dp == 1) | (dp == 2)

    def over(axis, count, value, routes):
        pairs = [(a * count + i, b * count + j) for a, b, i, j in routes]
        return lax.ppermute(value, ("section", axis), pairs)

    def over_dp(value, at, target):
        return over("dp", dps, value, [(s, s, z, target[z]) for s in at for z in range(dps)])

    def over_tensor(value, at, flip, step=0):
        return over("tensor", tensors, value, [(s, s + step, t, t ^ flip) for s in at for t in range(tensors)])

    def flipped(b):
        return [z ^ b for z in range(dps)]

    def feature_block(value, b):
        return lax.dynamic_slice_in_dim(value, (dp ^ b) * depth, depth, 1)

    def normed_of(parts, inverse, gains):
        return [
            (part.astype(jnp.float32) * inverse[:, None] * gain.astype(jnp.float32)).astype(jnp.bfloat16)
            for part, gain in zip(parts, gains)
        ]

    def square_sum(part):
        wide = part.astype(jnp.float32)
        return jnp.sum(wide * wide, axis=1)

    bias = seen_bias(cache_lengths[0], min(2, hidden_in.shape[2] // (HALF * HD)) * HALF)

    def attended(current, fresh):
        return attend(current, queries[0, 0], kv_cache[0, 0], bias, fresh)

    def hop(value, tick):
        return [over_tensor(value, (tick - 1,), j, 1) for j in range(tensors)]

    def prepared(parts):
        inverse = lax.rsqrt(sum(square_sum(part) for part in parts) / D + epsilon)
        return normed_of(parts, inverse, gains)

    halves = [[(0, 0)], [(j, (j - 1) * depth) for j in range(1, tensors)]]

    def straight(at, block):
        return {0: block, 3: over_dp(block, at, flipped(3)), 1: over_dp(block, at, flipped(1))}

    def relayed(at, blocks):
        return over_dp(jnp.where(inner, blocks[3], blocks[0]), at, (2, 0, 3, 1))

    def terms_of(half, blocks, which, shift=0):
        return [
            (
                blocks[b],
                [
                    (j, (dp ^ b) * depth + shift, ((tensor ^ j) * dps + (dp ^ b)) * depth, start, depth)
                    for j, start in halves[half]
                ],
            )
            for b in which
        ]

    def placing(active):
        return (active, tensor * own_width % served, own_width)

    kept = requantize(trainer_kv[0], [(tensor ^ j) * own_width // served * served for j in range(tensors)], served)
    hidden, kept = together(hidden_in[0], kept)

    squares = square_sum(hidden)
    for j in (2**i for i in range(tensors.bit_length() - 1)):
        squares = squares + over_tensor(squares, (0,), j)
    (normed,) = normed_of([hidden], lax.rsqrt(squares / D + epsilon), [norm_gain])
    first = [feature_block(normed, b) for b in range(dps)]
    first[1:] = [over_dp(first[b], (0,), flipped(b)) for b in range(1, dps)]
    gains = [norm_gain] + [over_tensor(norm_gain, everyone, j) for j in range(1, tensors)]

    def others(at, kept):
        received = [over_tensor(kept[j], at, j) for j in range(1, tensors)]
        return received[0] if len(received) == 1 else jnp.concatenate(received, axis=0)

    early_own = straight(early, kept[0])

    lhs = [jnp.concatenate(first, axis=0)]
    partial = [project(lhs, [(kept[j], [(0, 0, 0, 0, depth)])]) for j in range(tensors)]
    partial, kept = together(partial, kept)
    early_rest = others(early, kept)
    total = partial[0]
    for j in range(1, tensors):
        total = total + over_tensor(partial[j], (0,), j)
    total = total.reshape(dps, rows, served)
    returned = [over_dp(total[b].astype(jnp.bfloat16), (0,), flipped(b)) for b in range(1, dps)]
    fresh = total[0]
    for part in returned:
        fresh = fresh + part.astype(jnp.float32)
    result = carried = attended(hidden, fresh)

    early_other = straight(early, early_rest)
    early_own, carried, kept = together(early_own, carried, kept)
    early_own[2] = relayed(early, early_own)
    moved = hop(carried, 1)
    late_rest = others(late, kept)

    early_own, early_other, late_rest = together(early_own, early_other, late_rest)
    early_other[2] = relayed(early, early_other)
    token = over("dp", dps, early_other[3][:ROW_TILE, :HD], [(a, b, z, z) for a, b in ((1, 0), (2, 3)) for z in range(dps)])
    token, late_block = together(token, kept[0])
    shift = jnp.isnan(token[0, 0]).astype(jnp.int32)
    late_own = straight(late, late_block)

    terms = terms_of(0, early_own, range(dps)) + terms_of(1, early_other, range(dps))
    fresh, rollout = project(prepared(moved), terms, None, placing(is_early))
    carried = attended(moved[0], fresh)
    result = jnp.where(section == 1, carried, result)

    late_rest, carried = together(late_rest, carried)
    late_other = straight(late, late_rest)
    moved = hop(carried, 2)
    late_own, moved = together(late_own, moved)
    late_own[2] = relayed(late, late_own)
    carried = attended(moved[0], project(prepared(moved), terms))
    result = jnp.where(section == 2, carried, result)
    moved = hop(carried, 3)

    normed = prepared(moved)
    late_other, late_own, normed, result = together(late_other, late_own, normed, result)
    late_other[2] = relayed(late, late_other)
    terms = terms_of(0, late_own, range(dps), shift) + terms_of(1, late_other, (0, 1, 3))
    fresh, rollout = project(normed, terms, None, placing(1 - is_early), rollout)
    fresh, rollout, last = together(fresh, rollout, late_other[2])
    fresh, rollout = project(normed, terms_of(1, {2: last}, (2,)), fresh, placing(1 - is_early), rollout)
    result = jnp.where(section == 3, attended(moved[0], fresh), result)
    return (rollout[None], result[None, None])


def solution(mesh):
    placed = (
        P(None, "dp", "tensor"),
        P("section", "tensor"),
        P("section", ("tensor", "dp"), None),
        P("section", None, "dp", "tensor"),
        P("section", None, "dp", None, "tensor"),
        P(None, "dp"),
    )
    return jax.shard_map(
        body,
        mesh=mesh,
        in_specs=placed,
        out_specs=(P("section", None, "tensor"), P("section", None, "dp", "tensor")),
        check_vma=False,
    )
```

```python
import functools

import jax
import jax.numpy as jnp
from jax import lax
from jax.experimental import pallas as pl
from jax.experimental.pallas import tpu as pltpu
from jax.sharding import PartitionSpec as P

D = 16384
KVH = 8
HD = 128
GQ = 16
GROUP = 128
LMAX = 16
HALF = GQ // 2
PAIR = 2 * HD
ROW_TILE = 16

epsilon = 1e-05
clip_ratio = 2.0
FIXED = 4
VMEM = 60 << 20
SHORT = pl.CostEstimate(flops=0, bytes_accessed=0, transcendentals=0)


def requantize_kernel(column_ref, w_ref, *o_refs):
    width = o_refs[0].shape[1]
    ones = jnp.ones((ROW_TILE, GROUP), jnp.bfloat16)
    for j, o_ref in enumerate(o_refs):
        columns = pl.ds(pl.multiple_of(column_ref[j], HD), width)
        for start in range(0, w_ref.shape[0], GROUP):
            block = w_ref[start : start + GROUP, columns]
            total = jnp.dot(ones, jnp.abs(block), preferred_element_type=jnp.float32)[:1]
            limit = (total * (clip_ratio / GROUP)).astype(jnp.bfloat16)
            o_ref[start : start + GROUP, :] = jnp.minimum(jnp.maximum(block, -limit), limit)


def requantize(weight, columns, width):
    rows, whole = weight.shape
    tile = min(rows, 2 * GROUP)
    return pl.pallas_call(
        requantize_kernel,
        out_shape=[jax.ShapeDtypeStruct((rows, width), jnp.bfloat16)] * len(columns),
        grid_spec=pltpu.PrefetchScalarGridSpec(
            num_scalar_prefetch=1,
            grid=(rows // tile,),
            in_specs=[pl.BlockSpec((tile, whole), lambda i, columns: (i, 0))],
            out_specs=[pl.BlockSpec((tile, width), lambda i, columns: (i, 0))] * len(columns),
        ),
        compiler_params=pltpu.CompilerParams(vmem_limit_bytes=VMEM),
        cost_estimate=SHORT,
    )(jnp.stack(columns), weight)


def project_kernel(layout, lhs_count, has_total, has_held, placed, where_ref, *refs):
    lhs = refs[:lhs_count]
    blocks = refs[lhs_count : lhs_count + len(layout)]
    rest = list(refs[lhs_count + len(layout) :])
    total_ref = rest.pop(0) if has_total else None
    if has_held:
        rest.pop(0)
    o_ref = rest.pop(0)
    segments = [(block, *segment) for block, of_block in zip(blocks, layout) for segment in of_block]

    def copies():
        out, sems = rest
        width = min(out.shape[1], o_ref.shape[1])
        for i, (block, _, start, depth) in enumerate(segments):
            rows = pl.ds(pl.multiple_of(where_ref[FIXED + 2 * i + 1], GROUP), depth)
            columns = pl.ds(pl.multiple_of(pl.program_id(0) * width, HD), width)
            source = block.at[pl.ds(start, depth)]
            if width < block.shape[1]:
                source = block.at[pl.ds(start, depth), pl.ds(pl.multiple_of(where_ref[2], HD), width)]
            yield pltpu.make_async_copy(source, out.at[rows, columns], sems.at[i])

    if placed:

        @pl.when(where_ref[1] == 1)
        def _():
            for copy in copies():
                copy.start()

    @pl.when(where_ref[0] == 1)
    def _():
        total = total_ref[...] if has_total else None
        for i, (block, j, start, depth) in enumerate(segments):
            columns = pl.ds(pl.multiple_of(where_ref[FIXED + 2 * i], GROUP), depth)
            term = jnp.dot(
                lhs[j][:, columns], block[start : start + depth, :], preferred_element_type=jnp.float32
            )
            total = term if total is None else total + term
        o_ref[...] = total

    @pl.when(where_ref[0] == 0)
    def _():
        o_ref[...] = jnp.zeros(o_ref.shape, jnp.float32)

    if placed:

        @pl.when(where_ref[1] == 1)
        def _():
            for copy in copies():
                copy.wait()


def project(active, lhs, terms, total=None, placing=None, rollout=None):
    used = sorted({segment[0] for _, segments in terms for segment in segments})
    lhs = [lhs[j] for j in used]
    rows = lhs[0].shape[0]
    served = terms[0][0].shape[1]
    tile = min(served, 256)
    places, first_column, width = placing or (0, 0, 0)
    where = [active, places, first_column, active | places]
    for _, segments in terms:
        for _, offset, row, _, _ in segments:
            where += [offset, row]
    layout = [[(used.index(j), start, depth) for j, _, _, start, depth in segments] for _, segments in terms]
    count = sum(len(segments) for segments in layout)
    added = () if total is None else (total,)
    held = () if rollout is None else (rollout,)
    column = lambda i, where: (0, i)
    read = lambda i, where: (0, i * where[3])
    anywhere = pl.BlockSpec(memory_space=pl.ANY)
    fresh_shape, fresh_spec = jax.ShapeDtypeStruct((rows, served), jnp.float32), pl.BlockSpec((rows, tile), column)
    return pl.pallas_call(
        functools.partial(project_kernel, layout, len(lhs), bool(added), bool(held), placing is not None),
        out_shape=[fresh_shape, jax.ShapeDtypeStruct((D, width), jnp.bfloat16)] if placing else fresh_shape,
        grid_spec=pltpu.PrefetchScalarGridSpec(
            num_scalar_prefetch=1,
            grid=(served // tile,),
            in_specs=[pl.BlockSpec(part.shape, lambda i, where: (0, 0)) for part in lhs]
            + [pl.BlockSpec((block.shape[0], tile), read) for block, _ in terms]
            + [fresh_spec for _ in added]
            + [anywhere for _ in held],
            out_specs=[fresh_spec, anywhere] if placing else fresh_spec,
            scratch_shapes=[pltpu.SemaphoreType.DMA((count,))] if placing else [],
        ),
        input_output_aliases={1 + len(lhs) + len(terms) + len(added): 1} if held else {},
        compiler_params=pltpu.CompilerParams(vmem_limit_bytes=VMEM),
        cost_estimate=SHORT,
    )(jnp.stack([jnp.asarray(v, jnp.int32) for v in where]), *lhs, *[block for block, _ in terms], *added, *held)


def attend_kernel(share, active_ref, bias_ref, x_ref, q_ref, c_ref, f_ref, held_ref, o_ref):
    heads = share * HALF
    scale = HD ** (-0.5)

    @pl.when(active_ref[0] == 0)
    def _():
        o_ref[...] = held_ref[...]

    @pl.when(active_ref[0] == 1)
    def _():
        bias = jnp.concatenate([bias_ref[0]] * heads, axis=0)
        for g in range(q_ref.shape[1] // (heads * HD)):
            lanes = [slice((g * heads + i) * HD, (g * heads + i + 1) * HD) for i in range(heads)]
            query = jnp.concatenate([q_ref[:, lane] for lane in lanes], axis=0)
            at = g * share * PAIR
            keys = c_ref[:, :, at : at + HD].reshape(ROW_TILE * LMAX, HD)
            values = c_ref[:, :, at + HD : at + PAIR].reshape(ROW_TILE * LMAX, HD)
            fresh = f_ref[:, g * PAIR : (g + 1) * PAIR].astype(jnp.bfloat16).astype(jnp.float32)
            new_key = jnp.concatenate([fresh[:, :HD]] * heads, axis=0)
            new_value = jnp.concatenate([fresh[:, HD:]] * heads, axis=0)
            old = lax.dot_general(query, keys, (((1,), (1,)), ((), ())), preferred_element_type=jnp.float32)
            old = old * scale + bias
            new = jnp.sum(query.astype(jnp.float32) * new_key, axis=1, keepdims=True) * scale
            highest = jnp.maximum(jnp.max(old, axis=1, keepdims=True), new)
            old = jnp.exp(old - highest)
            new = jnp.exp(new - highest)
            inverse = 1.0 / (jnp.sum(old, axis=1, keepdims=True) + new)
            old = (old * inverse).astype(jnp.bfloat16)
            new = (new * inverse).astype(jnp.bfloat16).astype(jnp.float32)
            mixed = jnp.dot(old, values, preferred_element_type=jnp.float32) + new * new_value
            for i, lane in enumerate(lanes):
                total = x_ref[:, lane].astype(jnp.float32) + mixed[i * ROW_TILE : (i + 1) * ROW_TILE, :]
                o_ref[:, lane] = total.astype(jnp.bfloat16)


def seen_bias(lengths):
    column = jnp.arange(ROW_TILE * LMAX)
    own = jnp.arange(ROW_TILE)[:, None] == column[None, :] // LMAX
    seen = own[None] & ((column % LMAX)[None, None, :] < lengths.reshape(-1, ROW_TILE, 1))
    return jnp.where(seen, 0.0, -jnp.inf).astype(jnp.float32)


def attend(active, current, query, cache, bias, fresh, held):
    rows, width = query.shape
    share = min(2, width // (HALF * HD))
    wide = pl.BlockSpec((ROW_TILE, width), lambda i, active: (i, 0))
    return pl.pallas_call(
        functools.partial(attend_kernel, share),
        out_shape=jax.ShapeDtypeStruct((rows, width), jnp.bfloat16),
        grid_spec=pltpu.PrefetchScalarGridSpec(
            num_scalar_prefetch=1,
            grid=(rows // ROW_TILE,),
            in_specs=[
                pl.BlockSpec((1, *bias.shape[1:]), lambda i, active: (i, 0, 0)),
                wide,
                wide,
                pl.BlockSpec((ROW_TILE, LMAX, cache.shape[2]), lambda i, active: (i, 0, 0)),
                pl.BlockSpec((ROW_TILE, fresh.shape[1]), lambda i, active: (i, 0)),
                wide,
            ],
            out_specs=wide,
        ),
        compiler_params=pltpu.CompilerParams(vmem_limit_bytes=VMEM),
        cost_estimate=SHORT,
    )(active.reshape(1), bias, current, query, cache, fresh, held)


def together(*values):
    return lax.optimization_barrier(values)


def body(hidden_in, norm_gain, trainer_kv, queries, kv_cache, cache_lengths):
    sections, tensors, dps = (lax.axis_size(axis) for axis in ("section", "tensor", "dp"))
    section, tensor, dp = (lax.axis_index(axis) for axis in ("section", "tensor", "dp"))
    rows = hidden_in.shape[1]
    depth = trainer_kv.shape[1]
    own_width = 2 * KVH * HD // tensors
    served = max(own_width, PAIR)
    early, late = (1, 2), (0, 3)
    everyone = tuple(range(sections))
    is_early = ((section == 1) | (section == 2)).astype(jnp.int32)
    inner = (dp == 1) | (dp == 2)

    def over(axis, count, value, routes):
        pairs = [(a * count + i, b * count + j) for a, b, i, j in routes]
        return lax.ppermute(value, ("section", axis), pairs)

    def over_dp(value, at, target):
        return over("dp", dps, value, [(s, s, z, target[z]) for s in at for z in range(dps)])

    def over_tensor(value, at, flip, step=0):
        return over("tensor", tensors, value, [(s, s + step, t, t ^ flip) for s in at for t in range(tensors)])

    def flipped(b):
        return [z ^ b for z in range(dps)]

    def feature_block(value, b):
        return lax.dynamic_slice_in_dim(value, (dp ^ b) * depth, depth, 1)

    def normed_of(parts, inverse, gains):
        return [
            (part.astype(jnp.float32) * inverse[:, None] * gain.astype(jnp.float32)).astype(jnp.bfloat16)
            for part, gain in zip(parts, gains)
        ]

    def square_sum(part):
        wide = part.astype(jnp.float32)
        return jnp.sum(wide * wide, axis=1)

    bias = seen_bias(cache_lengths[0])
    turn = [(section == tick).astype(jnp.int32) for tick in range(sections)]

    def attended(tick, current, fresh, held):
        return attend(turn[tick], current, queries[0, 0], kv_cache[0, 0], bias, fresh, held)

    def hop(value, tick):
        return [over_tensor(value, (tick - 1,), j, 1) for j in range(tensors)]

    def prepared(parts):
        inverse = lax.rsqrt(sum(square_sum(part) for part in parts) / D + epsilon)
        return normed_of(parts, inverse, gains)

    halves = [[(0, 0)], [(j, (j - 1) * depth) for j in range(1, tensors)]]

    def relay(blocks):
        return jnp.where(inner, blocks[3], blocks[0])

    relay_to = (2, 0, 3, 1)

    def terms_of(half, blocks, which, shift=0):
        return [
            (
                blocks[b],
                [
                    (j, (dp ^ b) * depth + shift, ((tensor ^ j) * dps + (dp ^ b)) * depth, start, depth)
                    for j, start in halves[half]
                ],
            )
            for b in which
        ]

    def placing(active):
        return (active, tensor * own_width % served, own_width)

    kept = requantize(trainer_kv[0], [(tensor ^ j) * own_width // served * served for j in range(tensors)], served)
    hidden, kept = together(hidden_in[0], kept)

    squares = square_sum(hidden)
    for j in (2**i for i in range(tensors.bit_length() - 1)):
        squares = squares + over_tensor(squares, (0,), j)
    (normed,) = normed_of([hidden], lax.rsqrt(squares / D + epsilon), [norm_gain])
    first = [feature_block(normed, b) for b in range(dps)]
    first[1:] = [over_dp(first[b], (0,), flipped(b)) for b in range(1, dps)]
    gains = [norm_gain] + [over_tensor(norm_gain, everyone, j) for j in range(1, tensors)]

    def others(at, kept):
        received = [over_tensor(kept[j], at, j) for j in range(1, tensors)]
        return received[0] if len(received) == 1 else jnp.concatenate(received, axis=0)

    own = {0: kept[0], 3: over_dp(kept[0], early, flipped(3)), 1: over_dp(kept[0], early, flipped(1))}

    lhs = [jnp.concatenate(first, axis=0)]
    partial = [project(turn[0], lhs, [(kept[j], [(0, 0, 0, 0, depth)])]) for j in range(tensors)]
    partial, kept = together(partial, kept)
    rest = {0: others(early, kept)}
    total = partial[0]
    for j in range(1, tensors):
        total = total + over_tensor(partial[j], (0,), j)
    total = total.reshape(dps, rows, served)
    returned = [over_dp(total[b].astype(jnp.bfloat16), (0,), flipped(b)) for b in range(1, dps)]
    fresh = total[0]
    for part in returned:
        fresh = fresh + part.astype(jnp.float32)
    result = attended(0, hidden, fresh, hidden)

    rest[3], rest[1] = over_dp(rest[0], early, flipped(3)), over_dp(rest[0], early, flipped(1))
    own, result, kept = together(own, result, kept)
    own[2] = over_dp(relay(own), early, relay_to)
    own[2], rest = together(own[2], rest)
    handed = relay(rest)
    rest[2] = over_dp(handed, early, relay_to)
    token = over("dp", dps, handed[:ROW_TILE, :HD], [(a, b, z, z) for a, b in ((1, 0), (2, 3)) for z in range(dps)])
    token, late_block, result, kept = together(token, kept[0], result, kept)
    shift = jnp.isnan(token[0, 0]).astype(jnp.int32)
    late_own = {0: late_block, 3: over_dp(late_block, late, flipped(3)), 1: over_dp(late_block, late, flipped(1))}
    moved = hop(result, 1)
    late_rest = {0: others(late, kept)}

    terms = terms_of(0, own, range(dps)) + terms_of(1, rest, range(dps))
    fresh, rollout = project(turn[1], prepared(moved), terms, None, placing(is_early))
    result = attended(1, moved[0], fresh, result)

    late_rest[0], result = together(late_rest[0], result)
    late_rest[3], late_rest[1] = over_dp(late_rest[0], late, flipped(3)), over_dp(late_rest[0], late, flipped(1))
    moved = hop(result, 2)
    late_own, moved = together(late_own, moved)
    late_own[2] = over_dp(relay(late_own), late, relay_to)
    result = attended(2, moved[0], project(turn[2], prepared(moved), terms), result)
    moved = hop(result, 3)

    normed = prepared(moved)
    late_own, late_rest, normed = together(late_own, late_rest, normed)
    late_rest[2] = over_dp(relay(late_rest), late, relay_to)
    terms = terms_of(0, late_own, range(dps), shift) + terms_of(1, late_rest, (0, 1, 3))
    fresh, rollout = project(turn[3], normed, terms, None, placing(1 - is_early), rollout)
    fresh, rollout, late_rest[2] = together(fresh, rollout, late_rest[2])
    fresh, rollout = project(turn[3], normed, terms_of(1, late_rest, (2,)), fresh, placing(1 - is_early), rollout)
    result = attended(3, moved[0], fresh, result)
    return (rollout[None], result[None, None])


def solution(mesh):
    placed = (
        P(None, "dp", "tensor"),
        P("section", "tensor"),
        P("section", ("tensor", "dp"), None),
        P("section", None, "dp", "tensor"),
        P("section", None, "dp", None, "tensor"),
        P(None, "dp"),
    )
    return jax.shard_map(
        body,
        mesh=mesh,
        in_specs=placed,
        out_specs=(P("section", None, "tensor"), P("section", None, "dp", "tensor")),
        check_vma=False,
    )
```

```python
import functools

import jax
import jax.numpy as jnp
from jax import lax
from jax.experimental import pallas as pl
from jax.experimental.pallas import tpu as pltpu
from jax.sharding import PartitionSpec as P

D = 16384
KVH = 8
HD = 128
GQ = 16
GROUP = 128
LMAX = 16
HALF = GQ // 2
PAIR = 2 * HD
ROW_TILE = 16

epsilon = 1e-05
clip_ratio = 2.0
FAR, RELAYED = 4, 5
FIXED = 4
VMEM = 60 << 20
SHORT = pl.CostEstimate(flops=0, bytes_accessed=0, transcendentals=0)


def requantize_kernel(column_ref, w_ref, *o_refs):
    width = o_refs[0].shape[1]
    ones = jnp.ones((ROW_TILE, GROUP), jnp.bfloat16)
    for j, o_ref in enumerate(o_refs):
        columns = pl.ds(pl.multiple_of(column_ref[j], HD), width)
        for start in range(0, w_ref.shape[0], GROUP):
            block = w_ref[start : start + GROUP, columns]
            total = jnp.dot(ones, jnp.abs(block), preferred_element_type=jnp.float32)[:1]
            limit = (total * (clip_ratio / GROUP)).astype(jnp.bfloat16)
            o_ref[start : start + GROUP, :] = jnp.minimum(jnp.maximum(block, -limit), limit)


def requantize(weight, columns, width):
    rows, whole = weight.shape
    tile = min(rows, 2 * GROUP)
    return pl.pallas_call(
        requantize_kernel,
        out_shape=[jax.ShapeDtypeStruct((rows, width), jnp.bfloat16)] * len(columns),
        grid_spec=pltpu.PrefetchScalarGridSpec(
            num_scalar_prefetch=1,
            grid=(rows // tile,),
            in_specs=[pl.BlockSpec((tile, whole), lambda i, columns: (i, 0))],
            out_specs=[pl.BlockSpec((tile, width), lambda i, columns: (i, 0))] * len(columns),
        ),
        compiler_params=pltpu.CompilerParams(vmem_limit_bytes=VMEM),
        cost_estimate=SHORT,
    )(jnp.stack(columns), weight)


def project_kernel(layout, lhs_count, has_total, has_held, placed, where_ref, *refs):
    lhs = refs[:lhs_count]
    blocks = refs[lhs_count : lhs_count + len(layout)]
    rest = list(refs[lhs_count + len(layout) :])
    total_ref = rest.pop(0) if has_total else None
    if has_held:
        rest.pop(0)
    o_ref = rest.pop(0)
    segments = [(n, *segment) for n, (_, of_block) in enumerate(layout) for segment in of_block]

    def copy(i):
        n, _, start, depth = segments[i]
        out, sems = rest
        width = min(out.shape[1], o_ref.shape[1])
        rows = pl.ds(pl.multiple_of(where_ref[FIXED + len(layout) + 2 * i + 1], GROUP), depth)
        columns = pl.ds(pl.multiple_of(pl.program_id(0) * width, HD), width)
        source = blocks[n].at[pl.ds(start, depth)]
        if width < blocks[n].shape[1]:
            source = blocks[n].at[pl.ds(start, depth), pl.ds(pl.multiple_of(where_ref[2], HD), width)]
        return pltpu.make_async_copy(source, out.at[rows, columns], sems.at[i])

    def add(which):
        total = o_ref[...]
        for i in which:
            n, j, start, depth = segments[i]
            columns = pl.ds(pl.multiple_of(where_ref[FIXED + len(layout) + 2 * i], GROUP), depth)
            rows = blocks[n][start : start + depth, :]
            total += jnp.dot(lhs[j][:, columns], rows, preferred_element_type=jnp.float32)
        o_ref[...] = total

    def start(which):
        for i in which:
            copy(i).start()

    def wait(which):
        for i in which:
            copy(i).wait()

    groups = [(None, [i for i, segment in enumerate(segments) if not layout[segment[0]][0]])]
    for n, (gated, _) in enumerate(layout):
        if gated:
            groups.append((n, [i for i, segment in enumerate(segments) if segment[0] == n]))

    for n, which in groups:
        has = 1 if n is None else where_ref[FIXED + n]

        if placed and which:
            pl.when(where_ref[1] * has == 1)(functools.partial(start, which))

    o_ref[...] = total_ref[...] if has_total else jnp.zeros(o_ref.shape, jnp.float32)
    for n, which in groups:
        if which:
            has = 1 if n is None else where_ref[FIXED + n]
            pl.when(where_ref[0] * has == 1)(functools.partial(add, which))

    for n, which in groups:
        has = 1 if n is None else where_ref[FIXED + n]

        if placed and which:
            pl.when(where_ref[1] * has == 1)(functools.partial(wait, which))


def project(active, lhs, terms, total=None, placing=None, rollout=None):
    used = sorted({segment[0] for _, _, segments in terms for segment in segments})
    lhs = [lhs[j] for j in used]
    rows = lhs[0].shape[0]
    served = terms[0][0].shape[1]
    tile = min(served, 256)
    places, first_column, width = placing or (0, 0, 0)
    where = [active, places, first_column, active | places]
    where += [1 if has is None else has for _, has, _ in terms]
    for _, _, segments in terms:
        for _, offset, row, _, _ in segments:
            where += [offset, row]
    layout = [
        (has is not None, [(used.index(j), start, depth) for j, _, _, start, depth in segments])
        for _, has, segments in terms
    ]
    count = sum(len(segments) for _, segments in layout)
    added = () if total is None else (total,)
    held = () if rollout is None else (rollout,)
    column = lambda i, where: (0, i)

    def read(n):
        return lambda i, where: (0, i * where[3] * where[FIXED + n])

    anywhere = pl.BlockSpec(memory_space=pl.ANY)
    fresh_shape, fresh_spec = jax.ShapeDtypeStruct((rows, served), jnp.float32), pl.BlockSpec((rows, tile), column)
    placed = int(placing is not None)
    return pl.pallas_call(
        functools.partial(project_kernel, layout, len(lhs), bool(added), bool(held), placed),
        out_shape=[fresh_shape, jax.ShapeDtypeStruct((D, width), jnp.bfloat16)] if placing else fresh_shape,
        grid_spec=pltpu.PrefetchScalarGridSpec(
            num_scalar_prefetch=1,
            grid=(served // tile,),
            in_specs=[pl.BlockSpec(part.shape, lambda i, where: (0, 0)) for part in lhs]
            + [pl.BlockSpec((term[0].shape[0], tile), read(n)) for n, term in enumerate(terms)]
            + [fresh_spec for _ in added]
            + [anywhere for _ in held],
            out_specs=[fresh_spec, anywhere] if placing else fresh_spec,
            scratch_shapes=[pltpu.SemaphoreType.DMA((count,))] if placing else [],
        ),
        input_output_aliases={1 + len(lhs) + len(terms) + len(added): 1} if held else {},
        compiler_params=pltpu.CompilerParams(vmem_limit_bytes=VMEM),
        cost_estimate=SHORT,
    )(jnp.stack([jnp.asarray(v, jnp.int32) for v in where]), *lhs, *[term[0] for term in terms], *added, *held)


def attend_kernel(share, active_ref, bias_ref, x_ref, q_ref, c_ref, f_ref, held_ref, o_ref):
    heads = share * HALF
    scale = HD ** (-0.5)

    @pl.when((active_ref[0] == 0) & (pl.program_id(0) == 0))
    def _():
        o_ref[...] = held_ref[...]

    @pl.when(active_ref[0] == 1)
    def _():
        bias = jnp.concatenate([bias_ref[0]] * heads, axis=0)
        for g in range(q_ref.shape[1] // (heads * HD)):
            lanes = [slice((g * heads + i) * HD, (g * heads + i + 1) * HD) for i in range(heads)]
            query = jnp.concatenate([q_ref[:, lane] for lane in lanes], axis=0)
            at = g * share * PAIR
            keys = c_ref[:, :, at : at + HD].reshape(ROW_TILE * LMAX, HD)
            values = c_ref[:, :, at + HD : at + PAIR].reshape(ROW_TILE * LMAX, HD)
            fresh = f_ref[:, g * PAIR : (g + 1) * PAIR].astype(jnp.bfloat16).astype(jnp.float32)
            new_key = jnp.concatenate([fresh[:, :HD]] * heads, axis=0)
            new_value = jnp.concatenate([fresh[:, HD:]] * heads, axis=0)
            old = lax.dot_general(query, keys, (((1,), (1,)), ((), ())), preferred_element_type=jnp.float32)
            old = old * scale + bias
            new = jnp.sum(query.astype(jnp.float32) * new_key, axis=1, keepdims=True) * scale
            highest = jnp.maximum(jnp.max(old, axis=1, keepdims=True), new)
            old = jnp.exp(old - highest)
            new = jnp.exp(new - highest)
            inverse = 1.0 / (jnp.sum(old, axis=1, keepdims=True) + new)
            old = (old * inverse).astype(jnp.bfloat16)
            new = (new * inverse).astype(jnp.bfloat16).astype(jnp.float32)
            mixed = jnp.dot(old, values, preferred_element_type=jnp.float32) + new * new_value
            for i, lane in enumerate(lanes):
                total = x_ref[:, lane].astype(jnp.float32) + mixed[i * ROW_TILE : (i + 1) * ROW_TILE, :]
                o_ref[:, lane] = total.astype(jnp.bfloat16)


def seen_bias(lengths):
    column = jnp.arange(ROW_TILE * LMAX)
    own = jnp.arange(ROW_TILE)[:, None] == column[None, :] // LMAX
    seen = own[None] & ((column % LMAX)[None, None, :] < lengths.reshape(-1, ROW_TILE, 1))
    return jnp.where(seen, 0.0, -jnp.inf).astype(jnp.float32)


def attend(active, current, query, cache, bias, fresh, held):
    rows, width = query.shape
    share = min(2, width // (HALF * HD))
    wide = pl.BlockSpec((ROW_TILE, width), lambda i, active: (i * active[0], 0))
    return pl.pallas_call(
        functools.partial(attend_kernel, share),
        out_shape=jax.ShapeDtypeStruct((rows, width), jnp.bfloat16),
        grid_spec=pltpu.PrefetchScalarGridSpec(
            num_scalar_prefetch=1,
            grid=(rows // ROW_TILE,),
            in_specs=[
                pl.BlockSpec((1, *bias.shape[1:]), lambda i, active: (i * active[0], 0, 0)),
                wide,
                wide,
                pl.BlockSpec((ROW_TILE, LMAX, cache.shape[2]), lambda i, active: (i * active[0], 0, 0)),
                pl.BlockSpec((ROW_TILE, fresh.shape[1]), lambda i, active: (i * active[0], 0)),
                pl.BlockSpec((ROW_TILE, width), lambda i, active: (0, 0)),
            ],
            out_specs=wide,
        ),
        input_output_aliases={6: 0},
        compiler_params=pltpu.CompilerParams(vmem_limit_bytes=VMEM),
        cost_estimate=SHORT,
    )(active.reshape(1), bias, current, query, cache, fresh, held)


def together(*values):
    return lax.optimization_barrier(values)


def body(hidden_in, norm_gain, trainer_kv, queries, kv_cache, cache_lengths):
    sections, tensors, dps = (lax.axis_size(axis) for axis in ("section", "tensor", "dp"))
    section, tensor, dp = (lax.axis_index(axis) for axis in ("section", "tensor", "dp"))
    rows = hidden_in.shape[1]
    depth = trainer_kv.shape[1]
    own_width = 2 * KVH * HD // tensors
    served = max(own_width, PAIR)
    early, late = (1, 2), (0, 3)
    everyone = tuple(range(sections))
    is_early = ((section == 1) | (section == 2)).astype(jnp.int32)
    inner = ((dp == 1) | (dp == 2)).astype(jnp.int32)

    def over(axis, count, value, routes):
        pairs = [(a * count + i, b * count + j) for a, b, i, j in routes]
        return lax.ppermute(value, ("section", axis), pairs)

    def over_dp(value, at, target):
        return over("dp", dps, value, [(s, s, z, target[z]) for s in at for z in range(dps)])

    def over_tensor(value, at, flip, step=0):
        return over("tensor", tensors, value, [(s, s + step, t, t ^ flip) for s in at for t in range(tensors)])

    def flipped(b):
        return [z ^ b for z in range(dps)]

    def feature_block(value, b):
        return lax.dynamic_slice_in_dim(value, (dp ^ b) * depth, depth, 1)

    def normed_of(parts, inverse, gains):
        return [
            (part.astype(jnp.float32) * inverse[:, None] * gain.astype(jnp.float32)).astype(jnp.bfloat16)
            for part, gain in zip(parts, gains)
        ]

    def square_sum(part):
        wide = part.astype(jnp.float32)
        return jnp.sum(wide * wide, axis=1)

    bias = seen_bias(cache_lengths[0])
    turn = [(section == tick).astype(jnp.int32) for tick in range(sections)]

    def attended(tick, current, fresh, held):
        return attend(turn[tick], current, queries[0, 0], kv_cache[0, 0], bias, fresh, held)

    def hop(value, tick):
        return [over_tensor(value, (tick - 1,), j, 1) for j in range(tensors)]

    def prepared(parts):
        inverse = lax.rsqrt(sum(square_sum(part) for part in parts) / D + epsilon)
        return normed_of(parts, inverse, gains)

    halves = [[(0, 0)], [(j, (j - 1) * depth) for j in range(1, tensors)]]

    def far(at, blocks):
        return over("dp", dps, blocks[0], [(s, s, a, b) for s in at for a, b in ((0, 2), (3, 1))])

    def relayed(at, blocks):
        return over("dp", dps, blocks[3], [(s, s, a, b) for s in at for a, b in ((2, 3), (1, 0))])

    def around(at, blocks):
        return over_dp(jnp.where(inner == 1, blocks[3], blocks[0]), at, (2, 0, 3, 1))

    def terms_of(half, blocks, which, shift=0):
        terms = []
        for name in which:
            b, has = {FAR: (2, inner), RELAYED: (2, 1 - inner)}.get(name, (name, None))
            source = dp ^ b
            terms.append((blocks[name], has, [
                (j, source * depth + shift, ((tensor ^ j) * dps + source) * depth, start, depth)
                for j, start in halves[half]
            ]))
        return terms

    everything = (0, 1, 3, FAR, RELAYED)

    def placing(active):
        return (active, tensor * own_width % served, own_width)

    kept = requantize(trainer_kv[0], [(tensor ^ j) * own_width // served * served for j in range(tensors)], served)
    hidden, kept = together(hidden_in[0], kept)

    squares = square_sum(hidden)
    for j in (2**i for i in range(tensors.bit_length() - 1)):
        squares = squares + over_tensor(squares, (0,), j)
    (normed,) = normed_of([hidden], lax.rsqrt(squares / D + epsilon), [norm_gain])
    first = [feature_block(normed, b) for b in range(dps)]
    first[1:] = [over_dp(first[b], (0,), flipped(b)) for b in range(1, dps)]
    gains = [norm_gain] + [over_tensor(norm_gain, everyone, j) for j in range(1, tensors)]

    def others(at, kept):
        received = [over_tensor(kept[j], at, j) for j in range(1, tensors)]
        return received[0] if len(received) == 1 else jnp.concatenate(received, axis=0)

    own = {0: kept[0], 3: over_dp(kept[0], early, flipped(3)), 1: over_dp(kept[0], early, flipped(1))}

    lhs = [jnp.concatenate(first, axis=0)]
    partial = [project(turn[0], lhs, [(kept[j], None, [(0, 0, 0, 0, depth)])]) for j in range(tensors)]
    partial, kept = together(partial, kept)
    rest = {0: others(early, kept)}
    total = partial[0]
    for j in range(1, tensors):
        total = total + over_tensor(partial[j], (0,), j)
    total = total.reshape(dps, rows, served)
    returned = [over_dp(total[b].astype(jnp.bfloat16), (0,), flipped(b)) for b in range(1, dps)]
    fresh = total[0]
    for part in returned:
        fresh = fresh + part.astype(jnp.float32)
    result = attended(0, hidden, fresh, hidden)

    rest[3], rest[1] = over_dp(rest[0], early, flipped(3)), over_dp(rest[0], early, flipped(1))
    own, result, kept, gains = together(own, result, kept, gains)
    own[RELAYED], own[FAR] = relayed(early, own), far(early, own)
    own, rest = together(own, rest)
    rest[RELAYED], rest[FAR] = relayed(early, rest), far(early, rest)
    token = over("dp", dps, rest[3][:ROW_TILE, :HD], [(a, b, z, z) for a, b in ((1, 0), (2, 3)) for z in range(dps)])
    token, late_block, result, kept = together(token, kept[0], result, kept)
    shift = jnp.isnan(token[0, 0]).astype(jnp.int32)
    late_own = {0: late_block, 3: over_dp(late_block, late, flipped(3)), 1: over_dp(late_block, late, flipped(1))}
    moved = hop(result, 1)
    moved, rest, kept = together(moved, rest, kept)
    late_rest = {0: others(late, kept)}

    terms = terms_of(0, own, everything) + terms_of(1, rest, everything)
    fresh, rollout = project(turn[1], prepared(moved), terms, None, placing(is_early))
    result = attended(1, moved[0], fresh, result)

    moved = hop(result, 2)
    result = attended(2, moved[0], project(turn[2], prepared(moved), terms), result)
    late_own, late_rest[0], result = together(late_own, late_rest[0], result)
    late_rest[3], late_rest[1] = over_dp(late_rest[0], late, flipped(3)), over_dp(late_rest[0], late, flipped(1))
    late_own[2] = around(late, late_own)
    moved = hop(result, 3)

    normed = prepared(moved)
    late_own, late_rest, normed = together(late_own, late_rest, normed)
    late_rest[RELAYED], late_rest[FAR] = relayed(late, late_rest), far(late, late_rest)
    terms = terms_of(0, late_own, range(dps), shift) + terms_of(1, late_rest, (0, 1, 3))
    fresh, rollout = project(turn[3], normed, terms, None, placing(1 - is_early), rollout)
    fresh, rollout, late_rest = together(fresh, rollout, late_rest)
    terms = terms_of(1, late_rest, (FAR, RELAYED))
    fresh, rollout = project(turn[3], normed, terms, fresh, placing(1 - is_early), rollout)
    result = attended(3, moved[0], fresh, result)
    return (rollout[None], result[None, None])


def solution(mesh):
    placed = (
        P(None, "dp", "tensor"),
        P("section", "tensor"),
        P("section", ("tensor", "dp"), None),
        P("section", None, "dp", "tensor"),
        P("section", None, "dp", None, "tensor"),
        P(None, "dp"),
    )
    return jax.shard_map(
        body,
        mesh=mesh,
        in_specs=placed,
        out_specs=(P("section", None, "tensor"), P("section", None, "dp", "tensor")),
        check_vma=False,
    )
```

```python
import functools

import jax
import jax.numpy as jnp
from jax import lax
from jax.experimental import pallas as pl
from jax.experimental.pallas import tpu as pltpu
from jax.sharding import PartitionSpec as P

D = 16384
KVH = 8
HD = 128
GQ = 16
GROUP = 128
LMAX = 16
HALF = GQ // 2
PAIR = 2 * HD
ROW_TILE = 16

epsilon = 1e-05
clip_ratio = 2.0
FAR, RELAYED = 4, 5
FIXED = 4
VMEM = 60 << 20
SHORT = pl.CostEstimate(flops=0, bytes_accessed=0, transcendentals=0)


def requantize_kernel(column_ref, w_ref, o_ref):
    ones = jnp.ones((ROW_TILE, GROUP), jnp.bfloat16)
    for start in range(0, w_ref.shape[0], GROUP):
        block = w_ref[start : start + GROUP, :]
        total = jnp.dot(ones, jnp.abs(block), preferred_element_type=jnp.float32)[:1]
        limit = (total * (clip_ratio / GROUP)).astype(jnp.bfloat16)
        o_ref[start : start + GROUP, :] = jnp.minimum(jnp.maximum(block, -limit), limit)


def requantize(weight, indices, own_width, width):
    rows = weight.shape[0]
    tile = min(rows, 4 * GROUP)
    return [
        pl.pallas_call(
            requantize_kernel,
            out_shape=jax.ShapeDtypeStruct((rows, width), jnp.bfloat16),
            grid_spec=pltpu.PrefetchScalarGridSpec(
                num_scalar_prefetch=1,
                grid=(rows // tile,),
                in_specs=[pl.BlockSpec((tile, width), lambda i, column: (i, column[0]))],
                out_specs=pl.BlockSpec((tile, width), lambda i, column: (i, 0)),
            ),
            compiler_params=pltpu.CompilerParams(vmem_limit_bytes=VMEM),
            cost_estimate=SHORT,
        )((index * own_width // width).reshape(1), weight)
        for index in indices
    ]


def project_kernel(layout, lhs_count, has_total, has_held, placed, where_ref, *refs):
    lhs = refs[:lhs_count]
    blocks = refs[lhs_count : lhs_count + len(layout)]
    rest = list(refs[lhs_count + len(layout) :])
    total_ref = rest.pop(0) if has_total else None
    if has_held:
        rest.pop(0)
    o_ref = rest.pop(0)
    segments = [(n, *segment) for n, (_, of_block) in enumerate(layout) for segment in of_block]

    def copy(i):
        n, _, start, depth = segments[i]
        out, sems = rest
        width = min(out.shape[1], o_ref.shape[1])
        rows = pl.ds(pl.multiple_of(where_ref[FIXED + len(layout) + 2 * i + 1], GROUP), depth)
        columns = pl.ds(pl.multiple_of(pl.program_id(0) * width, HD), width)
        source = blocks[n].at[pl.ds(start, depth)]
        if width < blocks[n].shape[1]:
            source = blocks[n].at[pl.ds(start, depth), pl.ds(pl.multiple_of(where_ref[2], HD), width)]
        return pltpu.make_async_copy(source, out.at[rows, columns], sems.at[i])

    def add(which):
        total = o_ref[...]
        for i in which:
            n, j, start, depth = segments[i]
            columns = pl.ds(pl.multiple_of(where_ref[FIXED + len(layout) + 2 * i], GROUP), depth)
            rows = blocks[n][start : start + depth, :]
            total += jnp.dot(lhs[j][:, columns], rows, preferred_element_type=jnp.float32)
        o_ref[...] = total

    def start(which):
        for i in which:
            copy(i).start()

    def wait(which):
        for i in which:
            copy(i).wait()

    groups = [(None, [i for i, segment in enumerate(segments) if not layout[segment[0]][0]])]
    for n, (gated, _) in enumerate(layout):
        if gated:
            groups.append((n, [i for i, segment in enumerate(segments) if segment[0] == n]))

    for n, which in groups:
        has = 1 if n is None else where_ref[FIXED + n]

        if placed and which:
            pl.when(where_ref[1] * has == 1)(functools.partial(start, which))

    o_ref[...] = total_ref[...] if has_total else jnp.zeros(o_ref.shape, jnp.float32)
    for n, which in groups:
        if which:
            has = 1 if n is None else where_ref[FIXED + n]
            pl.when(where_ref[0] * has == 1)(functools.partial(add, which))

    for n, which in groups:
        has = 1 if n is None else where_ref[FIXED + n]

        if placed and which:
            pl.when(where_ref[1] * has == 1)(functools.partial(wait, which))


def project(active, lhs, terms, total=None, placing=None, rollout=None):
    used = sorted({segment[0] for _, _, segments in terms for segment in segments})
    lhs = [lhs[j] for j in used]
    rows = lhs[0].shape[0]
    served = terms[0][0].shape[1]
    tile = min(served, 256)
    places, first_column, width = placing or (0, 0, 0)
    where = [active, places, first_column, active | places]
    where += [1 if has is None else has for _, has, _ in terms]
    for _, _, segments in terms:
        for _, offset, row, _, _ in segments:
            where += [offset, row]
    layout = [
        (has is not None, [(used.index(j), start, depth) for j, _, _, start, depth in segments])
        for _, has, segments in terms
    ]
    count = sum(len(segments) for _, segments in layout)
    added = () if total is None else (total,)
    held = () if rollout is None else (rollout,)
    column = lambda i, where: (0, i)

    def read(n):
        return lambda i, where: (0, i * where[3] * where[FIXED + n])

    anywhere = pl.BlockSpec(memory_space=pl.ANY)
    fresh_shape, fresh_spec = jax.ShapeDtypeStruct((rows, served), jnp.float32), pl.BlockSpec((rows, tile), column)
    placed = int(placing is not None)
    return pl.pallas_call(
        functools.partial(project_kernel, layout, len(lhs), bool(added), bool(held), placed),
        out_shape=[fresh_shape, jax.ShapeDtypeStruct((D, width), jnp.bfloat16)] if placing else fresh_shape,
        grid_spec=pltpu.PrefetchScalarGridSpec(
            num_scalar_prefetch=1,
            grid=(served // tile,),
            in_specs=[pl.BlockSpec(part.shape, lambda i, where: (0, 0)) for part in lhs]
            + [pl.BlockSpec((term[0].shape[0], tile), read(n)) for n, term in enumerate(terms)]
            + [fresh_spec for _ in added]
            + [anywhere for _ in held],
            out_specs=[fresh_spec, anywhere] if placing else fresh_spec,
            scratch_shapes=[pltpu.SemaphoreType.DMA((count,))] if placing else [],
        ),
        input_output_aliases={1 + len(lhs) + len(terms) + len(added): 1} if held else {},
        compiler_params=pltpu.CompilerParams(vmem_limit_bytes=VMEM),
        cost_estimate=SHORT,
    )(jnp.stack([jnp.asarray(v, jnp.int32) for v in where]), *lhs, *[term[0] for term in terms], *added, *held)


def attend_kernel(share, active_ref, bias_ref, x_ref, q_ref, c_ref, f_ref, held_ref, o_ref):
    heads = share * HALF
    scale = HD ** (-0.5)

    @pl.when((active_ref[0] == 0) & (pl.program_id(0) == 0))
    def _():
        o_ref[...] = held_ref[...]

    @pl.when(active_ref[0] == 1)
    def _():
        bias = jnp.concatenate([bias_ref[0]] * heads, axis=0)
        for g in range(q_ref.shape[1] // (heads * HD)):
            lanes = [slice((g * heads + i) * HD, (g * heads + i + 1) * HD) for i in range(heads)]
            query = jnp.concatenate([q_ref[:, lane] for lane in lanes], axis=0)
            at = g * share * PAIR
            keys = c_ref[:, :, at : at + HD].reshape(ROW_TILE * LMAX, HD)
            values = c_ref[:, :, at + HD : at + PAIR].reshape(ROW_TILE * LMAX, HD)
            fresh = f_ref[:, g * PAIR : (g + 1) * PAIR].astype(jnp.bfloat16).astype(jnp.float32)
            new_key = jnp.concatenate([fresh[:, :HD]] * heads, axis=0)
            new_value = jnp.concatenate([fresh[:, HD:]] * heads, axis=0)
            old = lax.dot_general(query, keys, (((1,), (1,)), ((), ())), preferred_element_type=jnp.float32)
            old = old * scale + bias
            new = jnp.sum(query.astype(jnp.float32) * new_key, axis=1, keepdims=True) * scale
            highest = jnp.maximum(jnp.max(old, axis=1, keepdims=True), new)
            old = jnp.exp(old - highest)
            new = jnp.exp(new - highest)
            inverse = 1.0 / (jnp.sum(old, axis=1, keepdims=True) + new)
            old = (old * inverse).astype(jnp.bfloat16)
            new = (new * inverse).astype(jnp.bfloat16).astype(jnp.float32)
            mixed = jnp.dot(old, values, preferred_element_type=jnp.float32) + new * new_value
            for i, lane in enumerate(lanes):
                total = x_ref[:, lane].astype(jnp.float32) + mixed[i * ROW_TILE : (i + 1) * ROW_TILE, :]
                o_ref[:, lane] = total.astype(jnp.bfloat16)


def seen_bias(lengths):
    column = jnp.arange(ROW_TILE * LMAX)
    own = jnp.arange(ROW_TILE)[:, None] == column[None, :] // LMAX
    seen = own[None] & ((column % LMAX)[None, None, :] < lengths.reshape(-1, ROW_TILE, 1))
    return jnp.where(seen, 0.0, -jnp.inf).astype(jnp.float32)


def attend(active, current, query, cache, bias, fresh, held):
    rows, width = query.shape
    share = min(2, width // (HALF * HD))
    wide = pl.BlockSpec((ROW_TILE, width), lambda i, active: (i * active[0], 0))
    return pl.pallas_call(
        functools.partial(attend_kernel, share),
        out_shape=jax.ShapeDtypeStruct((rows, width), jnp.bfloat16),
        grid_spec=pltpu.PrefetchScalarGridSpec(
            num_scalar_prefetch=1,
            grid=(rows // ROW_TILE,),
            in_specs=[
                pl.BlockSpec((1, *bias.shape[1:]), lambda i, active: (i * active[0], 0, 0)),
                wide,
                wide,
                pl.BlockSpec((ROW_TILE, LMAX, cache.shape[2]), lambda i, active: (i * active[0], 0, 0)),
                pl.BlockSpec((ROW_TILE, fresh.shape[1]), lambda i, active: (i * active[0], 0)),
                pl.BlockSpec((ROW_TILE, width), lambda i, active: (0, 0)),
            ],
            out_specs=wide,
        ),
        input_output_aliases={6: 0},
        compiler_params=pltpu.CompilerParams(vmem_limit_bytes=VMEM),
        cost_estimate=SHORT,
    )(active.reshape(1), bias, current, query, cache, fresh, held)


def together(*values):
    return lax.optimization_barrier(values)


def body(hidden_in, norm_gain, trainer_kv, queries, kv_cache, cache_lengths):
    sections, tensors, dps = (lax.axis_size(axis) for axis in ("section", "tensor", "dp"))
    section, tensor, dp = (lax.axis_index(axis) for axis in ("section", "tensor", "dp"))
    rows = hidden_in.shape[1]
    depth = trainer_kv.shape[1]
    own_width = 2 * KVH * HD // tensors
    served = max(own_width, PAIR)
    early, late = (1, 2), (0, 3)
    everyone = tuple(range(sections))
    is_early = ((section == 1) | (section == 2)).astype(jnp.int32)
    inner = ((dp == 1) | (dp == 2)).astype(jnp.int32)

    def over(axis, count, value, routes):
        pairs = [(a * count + i, b * count + j) for a, b, i, j in routes]
        return lax.ppermute(value, ("section", axis), pairs)

    def over_dp(value, at, target):
        return over("dp", dps, value, [(s, s, z, target[z]) for s in at for z in range(dps)])

    def over_tensor(value, at, flip, step=0):
        return over("tensor", tensors, value, [(s, s + step, t, t ^ flip) for s in at for t in range(tensors)])

    def flipped(b):
        return [z ^ b for z in range(dps)]

    def feature_block(value, b):
        return lax.dynamic_slice_in_dim(value, (dp ^ b) * depth, depth, 1)

    def normed_of(parts, inverse, gains):
        return [
            (part.astype(jnp.float32) * inverse[:, None] * gain.astype(jnp.float32)).astype(jnp.bfloat16)
            for part, gain in zip(parts, gains)
        ]

    def square_sum(part):
        wide = part.astype(jnp.float32)
        return jnp.sum(wide * wide, axis=1)

    bias = seen_bias(cache_lengths[0])
    turn = [(section == tick).astype(jnp.int32) for tick in range(sections)]

    def attended(tick, current, fresh, held):
        return attend(turn[tick], current, queries[0, 0], kv_cache[0, 0], bias, fresh, held)

    def hop(value, tick):
        return over_tensor(value, (tick - 1,), 0, 1)

    def both(part, tick):
        return [part] + [over_tensor(part, (tick,), j) for j in range(1, tensors)]

    def prepared(parts):
        inverse = lax.rsqrt(sum(square_sum(part) for part in parts) / D + epsilon)
        return normed_of(parts, inverse, gains)

    halves = [[(0, 0)], [(j, (j - 1) * depth) for j in range(1, tensors)], [(j, j * depth) for j in range(tensors)]]

    def far(at, blocks):
        return over("dp", dps, blocks[0], [(s, s, a, b) for s in at for a, b in ((0, 2), (3, 1))])

    def relayed(at, blocks):
        return over("dp", dps, blocks[3], [(s, s, a, b) for s in at for a, b in ((2, 3), (1, 0))])

    def around(at, blocks):
        return over_dp(jnp.where(inner == 1, blocks[3], blocks[0]), at, (2, 0, 3, 1))

    def terms_of(half, blocks, which, shift=0):
        terms = []
        for name in which:
            b, has = {FAR: (2, inner), RELAYED: (2, 1 - inner)}.get(name, (name, None))
            source = dp ^ b
            terms.append((blocks[name], has, [
                (j, source * depth + shift, ((tensor ^ j) * dps + source) * depth, start, depth)
                for j, start in halves[half]
            ]))
        return terms

    everything = (0, 1, 3, FAR, RELAYED)

    def placing(active):
        return (active, tensor * own_width % served, own_width)

    weight, hidden, first_kept = together(trainer_kv[0], hidden_in[0], requantize(trainer_kv[0], [tensor], own_width, served))

    squares = square_sum(hidden)
    for j in (2**i for i in range(tensors.bit_length() - 1)):
        squares = squares + over_tensor(squares, (0,), j)
    (normed,) = normed_of([hidden], lax.rsqrt(squares / D + epsilon), [norm_gain])
    first = [feature_block(normed, b) for b in range(dps)]
    weight, first = together(weight, first)
    kept = first_kept + requantize(weight, [tensor ^ j for j in range(1, tensors)], own_width, served)
    first[1:] = [over_dp(first[b], (0,), flipped(b)) for b in range(1, dps)]
    gains = [norm_gain] + [over_tensor(norm_gain, everyone, j) for j in range(1, tensors)]

    def others(at, kept):
        received = [over_tensor(kept[j], at, j) for j in range(1, tensors)]
        return received[0] if len(received) == 1 else jnp.concatenate(received, axis=0)

    own = {0: kept[0], 3: over_dp(kept[0], early, flipped(3)), 1: over_dp(kept[0], early, flipped(1))}

    lhs = [jnp.concatenate(first, axis=0)]
    partial = [project(turn[0], lhs, [(kept[j], None, [(0, 0, 0, 0, depth)])]) for j in range(tensors)]
    partial, kept = together(partial, kept)
    rest = {0: others(early, kept)}
    total = partial[0]
    for j in range(1, tensors):
        total = total + over_tensor(partial[j], (0,), j)
    total = total.reshape(dps, rows, served)
    returned = [over_dp(total[b].astype(jnp.bfloat16), (0,), flipped(b)) for b in range(1, dps)]
    fresh = total[0]
    for part in returned:
        fresh = fresh + part.astype(jnp.float32)
    result = attended(0, hidden, fresh, hidden)

    rest[3], rest[1] = over_dp(rest[0], early, flipped(3)), over_dp(rest[0], early, flipped(1))
    own, result, kept, gains = together(own, result, kept, gains)
    whole = jnp.concatenate([kept[0], others(late, kept)], axis=0)
    own[RELAYED], own[FAR] = relayed(early, own), far(early, own)
    own, rest, whole = together(own, rest, whole)
    rest[2] = around(early, rest)
    token = over("dp", dps, rest[3][:ROW_TILE, :HD], [(a, b, z, z) for a, b in ((1, 0), (2, 3)) for z in range(dps)])
    token, whole, result = together(token, whole, result)
    shift = jnp.isnan(token[0, 0]).astype(jnp.int32)
    last = {0: whole, 3: over_dp(whole, late, flipped(3)), 1: over_dp(whole, late, flipped(1))}

    moved, rest = together(both(hop(result, 1), 1), rest)
    terms = terms_of(0, own, everything) + terms_of(1, rest, range(dps))
    fresh, rollout = project(turn[1], prepared(moved), terms, None, placing(is_early))
    result = attended(1, moved[0], fresh, result)

    moved, last = together(both(hop(result, 2), 2), last)
    last[RELAYED], last[FAR] = relayed(late, last), far(late, last)
    result = attended(2, moved[0], project(turn[2], prepared(moved), terms), result)
    moved = both(hop(result, 3), 3)
    normed = prepared(moved)
    fresh, rollout = project(turn[3], normed, terms_of(2, last, (0, 1, 3), shift), None, placing(1 - is_early), rollout)
    fresh, rollout, last = together(fresh, rollout, last)
    fresh, rollout = project(turn[3], normed, terms_of(2, last, (FAR, RELAYED)), fresh, placing(1 - is_early), rollout)
    result = attended(3, moved[0], fresh, result)
    return (rollout[None], result[None, None])


def solution(mesh):
    placed = (
        P(None, "dp", "tensor"),
        P("section", "tensor"),
        P("section", ("tensor", "dp"), None),
        P("section", None, "dp", "tensor"),
        P("section", None, "dp", None, "tensor"),
        P(None, "dp"),
    )
    return jax.shard_map(
        body,
        mesh=mesh,
        in_specs=placed,
        out_specs=(P("section", None, "tensor"), P("section", None, "dp", "tensor")),
        check_vma=False,
    )
```

```python
import functools

import jax
import jax.numpy as jnp
from jax import lax
from jax.experimental import pallas as pl
from jax.experimental.pallas import tpu as pltpu
from jax.sharding import PartitionSpec as P

D = 16384
KVH = 8
HD = 128
GQ = 16
GROUP = 128
LMAX = 16
HALF = GQ // 2
PAIR = 2 * HD
ROW_TILE = 16

epsilon = 1e-05
clip_ratio = 2.0
FAR, RELAYED = 4, 5
FIXED = 4
VMEM = 60 << 20
SHORT = pl.CostEstimate(flops=0, bytes_accessed=0, transcendentals=0)


def requantize_kernel(column_ref, w_ref, o_ref):
    ones = jnp.ones((ROW_TILE, GROUP), jnp.bfloat16)
    for start in range(0, w_ref.shape[0], GROUP):
        block = w_ref[start : start + GROUP, :]
        total = jnp.dot(ones, jnp.abs(block), preferred_element_type=jnp.float32)[:1]
        limit = (total * (clip_ratio / GROUP)).astype(jnp.bfloat16)
        o_ref[start : start + GROUP, :] = jnp.minimum(jnp.maximum(block, -limit), limit)


def requantize(weight, indices, own_width, width):
    rows = weight.shape[0]
    tile = min(rows, 4 * GROUP)
    return [
        pl.pallas_call(
            requantize_kernel,
            out_shape=jax.ShapeDtypeStruct((rows, width), jnp.bfloat16),
            grid_spec=pltpu.PrefetchScalarGridSpec(
                num_scalar_prefetch=1,
                grid=(rows // tile,),
                in_specs=[pl.BlockSpec((tile, width), lambda i, column: (i, column[0]))],
                out_specs=pl.BlockSpec((tile, width), lambda i, column: (i, 0)),
            ),
            compiler_params=pltpu.CompilerParams(vmem_limit_bytes=VMEM),
            cost_estimate=SHORT,
        )((index * own_width // width).reshape(1), weight)
        for index in indices
    ]


def project_kernel(layout, lhs_count, has_total, has_held, placed, where_ref, *refs):
    lhs = refs[:lhs_count]
    blocks = refs[lhs_count : lhs_count + len(layout)]
    rest = list(refs[lhs_count + len(layout) :])
    total_ref = rest.pop(0) if has_total else None
    if has_held:
        rest.pop(0)
    o_ref = rest.pop(0)
    segments = [(n, *segment) for n, (_, of_block) in enumerate(layout) for segment in of_block]

    def copy(i):
        n, _, start, depth = segments[i]
        out, sems = rest
        width = min(out.shape[1], o_ref.shape[1])
        rows = pl.ds(pl.multiple_of(where_ref[FIXED + len(layout) + 2 * i + 1], GROUP), depth)
        columns = pl.ds(pl.multiple_of(pl.program_id(0) * width, HD), width)
        source = blocks[n].at[pl.ds(start, depth)]
        if width < blocks[n].shape[1]:
            source = blocks[n].at[pl.ds(start, depth), pl.ds(pl.multiple_of(where_ref[2], HD), width)]
        return pltpu.make_async_copy(source, out.at[rows, columns], sems.at[i])

    def add(which):
        total = o_ref[...]
        for i in which:
            n, j, start, depth = segments[i]
            columns = pl.ds(pl.multiple_of(where_ref[FIXED + len(layout) + 2 * i], GROUP), depth)
            rows = blocks[n][start : start + depth, :]
            total += jnp.dot(lhs[j][:, columns], rows, preferred_element_type=jnp.float32)
        o_ref[...] = total

    def start(which):
        for i in which:
            copy(i).start()

    def wait(which):
        for i in which:
            copy(i).wait()

    groups = [(None, [i for i, segment in enumerate(segments) if not layout[segment[0]][0]])]
    for n, (gated, _) in enumerate(layout):
        if gated:
            groups.append((n, [i for i, segment in enumerate(segments) if segment[0] == n]))

    for n, which in groups:
        has = 1 if n is None else where_ref[FIXED + n]

        if placed and which:
            pl.when(where_ref[1] * has == 1)(functools.partial(start, which))

    o_ref[...] = total_ref[...] if has_total else jnp.zeros(o_ref.shape, jnp.float32)
    for n, which in groups:
        if which:
            has = 1 if n is None else where_ref[FIXED + n]
            pl.when(where_ref[0] * has == 1)(functools.partial(add, which))

    for n, which in groups:
        has = 1 if n is None else where_ref[FIXED + n]

        if placed and which:
            pl.when(where_ref[1] * has == 1)(functools.partial(wait, which))


def project(active, lhs, terms, total=None, placing=None, rollout=None):
    used = sorted({segment[0] for _, _, segments in terms for segment in segments})
    lhs = [lhs[j] for j in used]
    rows = lhs[0].shape[0]
    served = terms[0][0].shape[1]
    tile = min(served, 256)
    places, first_column, width = placing or (0, 0, 0)
    where = [active, places, first_column, active | places]
    where += [1 if has is None else has for _, has, _ in terms]
    for _, _, segments in terms:
        for _, offset, row, _, _ in segments:
            where += [offset, row]
    layout = [
        (has is not None, [(used.index(j), start, depth) for j, _, _, start, depth in segments])
        for _, has, segments in terms
    ]
    count = sum(len(segments) for _, segments in layout)
    added = () if total is None else (total,)
    held = () if rollout is None else (rollout,)
    column = lambda i, where: (0, i)

    def read(n):
        return lambda i, where: (0, i * where[3] * where[FIXED + n])

    anywhere = pl.BlockSpec(memory_space=pl.ANY)
    fresh_shape, fresh_spec = jax.ShapeDtypeStruct((rows, served), jnp.float32), pl.BlockSpec((rows, tile), column)
    placed = int(placing is not None)
    return pl.pallas_call(
        functools.partial(project_kernel, layout, len(lhs), bool(added), bool(held), placed),
        out_shape=[fresh_shape, jax.ShapeDtypeStruct((D, width), jnp.bfloat16)] if placing else fresh_shape,
        grid_spec=pltpu.PrefetchScalarGridSpec(
            num_scalar_prefetch=1,
            grid=(served // tile,),
            in_specs=[pl.BlockSpec(part.shape, lambda i, where: (0, 0)) for part in lhs]
            + [pl.BlockSpec((term[0].shape[0], tile), read(n)) for n, term in enumerate(terms)]
            + [fresh_spec for _ in added]
            + [anywhere for _ in held],
            out_specs=[fresh_spec, anywhere] if placing else fresh_spec,
            scratch_shapes=[pltpu.SemaphoreType.DMA((count,))] if placing else [],
        ),
        input_output_aliases={1 + len(lhs) + len(terms) + len(added): 1} if held else {},
        compiler_params=pltpu.CompilerParams(vmem_limit_bytes=VMEM),
        cost_estimate=SHORT,
    )(jnp.stack([jnp.asarray(v, jnp.int32) for v in where]), *lhs, *[term[0] for term in terms], *added, *held)


def attend_kernel(share, active_ref, bias_ref, x_ref, q_ref, c_ref, f_ref, held_ref, o_ref):
    heads = share * HALF
    scale = HD ** (-0.5)

    @pl.when((active_ref[0] == 0) & (pl.program_id(0) == 0))
    def _():
        o_ref[...] = held_ref[...]

    @pl.when(active_ref[0] == 1)
    def _():
        bias = jnp.concatenate([bias_ref[0]] * heads, axis=0)
        for g in range(q_ref.shape[1] // (heads * HD)):
            lanes = [slice((g * heads + i) * HD, (g * heads + i + 1) * HD) for i in range(heads)]
            query = jnp.concatenate([q_ref[:, lane] for lane in lanes], axis=0)
            at = g * share * PAIR
            keys = c_ref[:, :, at : at + HD].reshape(ROW_TILE * LMAX, HD)
            values = c_ref[:, :, at + HD : at + PAIR].reshape(ROW_TILE * LMAX, HD)
            fresh = f_ref[:, g * PAIR : (g + 1) * PAIR].astype(jnp.bfloat16).astype(jnp.float32)
            new_key = jnp.concatenate([fresh[:, :HD]] * heads, axis=0)
            new_value = jnp.concatenate([fresh[:, HD:]] * heads, axis=0)
            old = lax.dot_general(query, keys, (((1,), (1,)), ((), ())), preferred_element_type=jnp.float32)
            old = old * scale + bias
            new = jnp.sum(query.astype(jnp.float32) * new_key, axis=1, keepdims=True) * scale
            highest = jnp.maximum(jnp.max(old, axis=1, keepdims=True), new)
            old = jnp.exp(old - highest)
            new = jnp.exp(new - highest)
            inverse = 1.0 / (jnp.sum(old, axis=1, keepdims=True) + new)
            old = (old * inverse).astype(jnp.bfloat16)
            new = (new * inverse).astype(jnp.bfloat16).astype(jnp.float32)
            mixed = jnp.dot(old, values, preferred_element_type=jnp.float32) + new * new_value
            for i, lane in enumerate(lanes):
                total = x_ref[:, lane].astype(jnp.float32) + mixed[i * ROW_TILE : (i + 1) * ROW_TILE, :]
                o_ref[:, lane] = total.astype(jnp.bfloat16)


def seen_bias(lengths):
    column = jnp.arange(ROW_TILE * LMAX)
    own = jnp.arange(ROW_TILE)[:, None] == column[None, :] // LMAX
    seen = own[None] & ((column % LMAX)[None, None, :] < lengths.reshape(-1, ROW_TILE, 1))
    return jnp.where(seen, 0.0, -jnp.inf).astype(jnp.float32)


def attend(active, current, query, cache, bias, fresh, held):
    rows, width = query.shape
    share = min(2, width // (HALF * HD))
    wide = pl.BlockSpec((ROW_TILE, width), lambda i, active: (i * active[0], 0))
    return pl.pallas_call(
        functools.partial(attend_kernel, share),
        out_shape=jax.ShapeDtypeStruct((rows, width), jnp.bfloat16),
        grid_spec=pltpu.PrefetchScalarGridSpec(
            num_scalar_prefetch=1,
            grid=(rows // ROW_TILE,),
            in_specs=[
                pl.BlockSpec((1, *bias.shape[1:]), lambda i, active: (i * active[0], 0, 0)),
                wide,
                wide,
                pl.BlockSpec((ROW_TILE, LMAX, cache.shape[2]), lambda i, active: (i * active[0], 0, 0)),
                pl.BlockSpec((ROW_TILE, fresh.shape[1]), lambda i, active: (i * active[0], 0)),
                pl.BlockSpec((ROW_TILE, width), lambda i, active: (0, 0)),
            ],
            out_specs=wide,
        ),
        input_output_aliases={6: 0},
        compiler_params=pltpu.CompilerParams(vmem_limit_bytes=VMEM),
        cost_estimate=SHORT,
    )(active.reshape(1), bias, current, query, cache, fresh, held)


def together(*values):
    return lax.optimization_barrier(values)


def body(hidden_in, norm_gain, trainer_kv, queries, kv_cache, cache_lengths):
    sections, tensors, dps = (lax.axis_size(axis) for axis in ("section", "tensor", "dp"))
    section, tensor, dp = (lax.axis_index(axis) for axis in ("section", "tensor", "dp"))
    rows = hidden_in.shape[1]
    depth = trainer_kv.shape[1]
    own_width = 2 * KVH * HD // tensors
    served = max(own_width, PAIR)
    early, late = (1, 2), (0, 3)
    everyone = tuple(range(sections))
    is_early = ((section == 1) | (section == 2)).astype(jnp.int32)
    inner = ((dp == 1) | (dp == 2)).astype(jnp.int32)

    def over(axis, count, value, routes):
        pairs = [(a * count + i, b * count + j) for a, b, i, j in routes]
        return lax.ppermute(value, ("section", axis), pairs)

    def over_dp(value, at, target):
        return over("dp", dps, value, [(s, s, z, target[z]) for s in at for z in range(dps)])

    def over_tensor(value, at, flip, step=0):
        return over("tensor", tensors, value, [(s, s + step, t, t ^ flip) for s in at for t in range(tensors)])

    def flipped(b):
        return [z ^ b for z in range(dps)]

    def feature_block(value, b):
        return lax.dynamic_slice_in_dim(value, (dp ^ b) * depth, depth, 1)

    def normed_of(parts, inverse, gains):
        return [
            (part.astype(jnp.float32) * inverse[:, None] * gain.astype(jnp.float32)).astype(jnp.bfloat16)
            for part, gain in zip(parts, gains)
        ]

    def square_sum(part):
        wide = part.astype(jnp.float32)
        return jnp.sum(wide * wide, axis=1)

    bias = seen_bias(cache_lengths[0])
    turn = [(section == tick).astype(jnp.int32) for tick in range(sections)]

    def attended(tick, current, fresh, held):
        return attend(turn[tick], current, queries[0, 0], kv_cache[0, 0], bias, fresh, held)

    def hop(value, tick):
        return over_tensor(value, (tick - 1,), 0, 1)

    def both(part, tick):
        return [part] + [over_tensor(part, (tick,), j) for j in range(1, tensors)]

    def prepared(parts):
        inverse = lax.rsqrt(sum(square_sum(part) for part in parts) / D + epsilon)
        return normed_of(parts, inverse, gains)

    halves = [[(0, 0)], [(j, (j - 1) * depth) for j in range(1, tensors)], [(j, j * depth) for j in range(tensors)]]

    def far(at, blocks):
        return over("dp", dps, blocks[0], [(s, s, a, b) for s in at for a, b in ((0, 2), (3, 1))])

    def relayed(at, blocks):
        return over("dp", dps, blocks[3], [(s, s, a, b) for s in at for a, b in ((2, 3), (1, 0))])

    def around(at, blocks):
        return over_dp(jnp.where(inner == 1, blocks[3], blocks[0]), at, (2, 0, 3, 1))

    def terms_of(half, blocks, which, shift=0):
        terms = []
        for name in which:
            b, has = {FAR: (2, inner), RELAYED: (2, 1 - inner)}.get(name, (name, None))
            source = dp ^ b
            terms.append((blocks[name], has, [
                (j, source * depth + shift, ((tensor ^ j) * dps + source) * depth, start, depth)
                for j, start in halves[half]
            ]))
        return terms

    everything = (0, 1, 3, FAR, RELAYED)

    def placing(active):
        return (active, tensor * own_width % served, own_width)

    weight, hidden, first_kept = together(trainer_kv[0], hidden_in[0], requantize(trainer_kv[0], [tensor], own_width, served))

    squares = square_sum(hidden)
    for j in (2**i for i in range(tensors.bit_length() - 1)):
        squares = squares + over_tensor(squares, (0,), j)
    (normed,) = normed_of([hidden], lax.rsqrt(squares / D + epsilon), [norm_gain])
    first = [feature_block(normed, b) for b in range(dps)]
    weight, first = together(weight, first)
    kept = first_kept + requantize(weight, [tensor ^ j for j in range(1, tensors)], own_width, served)
    first[1:] = [over_dp(first[b], (0,), flipped(b)) for b in range(1, dps)]
    gains = [norm_gain] + [over_tensor(norm_gain, everyone, j) for j in range(1, tensors)]

    def others(at, kept):
        received = [over_tensor(kept[j], at, j) for j in range(1, tensors)]
        return received[0] if len(received) == 1 else jnp.concatenate(received, axis=0)

    own = {0: kept[0], 3: over_dp(kept[0], early, flipped(3)), 1: over_dp(kept[0], early, flipped(1))}

    lhs = [jnp.concatenate(first, axis=0)]
    partial = [project(turn[0], lhs, [(kept[j], None, [(0, 0, 0, 0, depth)])]) for j in range(tensors)]
    partial, kept = together(partial, kept)
    rest = {0: others(everyone, kept)}
    total = partial[0]
    for j in range(1, tensors):
        total = total + over_tensor(partial[j].astype(jnp.bfloat16), (0,), j).astype(jnp.float32)
    total = total.reshape(dps, rows, served)
    returned = [over_dp(total[b].astype(jnp.bfloat16), (0,), flipped(b)) for b in range(1, dps)]
    fresh = total[0]
    for part in returned:
        fresh = fresh + part.astype(jnp.float32)
    result = attended(0, hidden, fresh, hidden)

    rest[3], rest[1] = over_dp(rest[0], early, flipped(3)), over_dp(rest[0], early, flipped(1))
    own, result, gains = together(own, result, gains)
    kept_back, rest[0] = together(own, rest[0])
    own[RELAYED], own[FAR] = relayed(early, kept_back), far(early, kept_back)
    own, rest = together(own, rest)
    rest[RELAYED], rest[FAR] = relayed(early, rest), far(early, rest)
    token = over("dp", dps, rest[3][:ROW_TILE, :HD], [(a, b, z, z) for a, b in ((1, 0), (2, 3)) for z in range(dps)])
    token, whole, result = together(token, [kept[0], rest[0]], result)
    whole = jnp.concatenate(whole, axis=0)
    shift = jnp.isnan(token[0, 0]).astype(jnp.int32)
    last = {0: whole, 3: over_dp(whole, late, flipped(3)), 1: over_dp(whole, late, flipped(1))}

    moved, rest = together(both(hop(result, 1), 1), rest)
    terms = terms_of(0, own, everything) + terms_of(1, rest, everything)
    fresh, rollout = project(turn[1], prepared(moved), terms, None, placing(is_early))
    result = attended(1, moved[0], fresh, result)

    moved, last = together(both(hop(result, 2), 2), last)
    last[RELAYED], last[FAR] = relayed(late, last), far(late, last)
    result = attended(2, moved[0], project(turn[2], prepared(moved), terms), result)
    moved = both(hop(result, 3), 3)
    normed = prepared(moved)
    fresh, rollout = project(turn[3], normed, terms_of(2, last, (0, 1, 3), shift), None, placing(1 - is_early), rollout)
    fresh, rollout, last = together(fresh, rollout, last)
    fresh, rollout = project(turn[3], normed, terms_of(2, last, (FAR, RELAYED)), fresh, placing(1 - is_early), rollout)
    result = attended(3, moved[0], fresh, result)
    return (rollout[None], result[None, None])


def solution(mesh):
    placed = (
        P(None, "dp", "tensor"),
        P("section", "tensor"),
        P("section", ("tensor", "dp"), None),
        P("section", None, "dp", "tensor"),
        P("section", None, "dp", None, "tensor"),
        P(None, "dp"),
    )
    return jax.shard_map(
        body,
        mesh=mesh,
        in_specs=placed,
        out_specs=(P("section", None, "tensor"), P("section", None, "dp", "tensor")),
        check_vma=False,
    )
```

```python
import functools

import jax
import jax.numpy as jnp
from jax import lax
from jax.experimental import pallas as pl
from jax.experimental.pallas import tpu as pltpu
from jax.sharding import PartitionSpec as P

D = 16384
KVH = 8
HD = 128
GQ = 16
GROUP = 128
LMAX = 16
HALF = GQ // 2
PAIR = 2 * HD
ROW_TILE = 16

epsilon = 1e-05
clip_ratio = 2.0
FAR, RELAYED = 4, 5
FIXED = 4
VMEM = 60 << 20
SHORT = pl.CostEstimate(flops=0, bytes_accessed=0, transcendentals=0)


def requantize_kernel(column_ref, w_ref, o_ref):
    ones = jnp.ones((ROW_TILE, GROUP), jnp.bfloat16)
    for start in range(0, w_ref.shape[0], GROUP):
        block = w_ref[start : start + GROUP, :]
        total = jnp.dot(ones, jnp.abs(block), preferred_element_type=jnp.float32)[:1]
        limit = (total * (clip_ratio / GROUP)).astype(jnp.bfloat16)
        o_ref[start : start + GROUP, :] = jnp.minimum(jnp.maximum(block, -limit), limit)


def requantize(weight, indices, own_width, width):
    rows = weight.shape[0]
    tile = min(rows, 4 * GROUP)
    return [
        pl.pallas_call(
            requantize_kernel,
            out_shape=jax.ShapeDtypeStruct((rows, width), jnp.bfloat16),
            grid_spec=pltpu.PrefetchScalarGridSpec(
                num_scalar_prefetch=1,
                grid=(rows // tile,),
                in_specs=[pl.BlockSpec((tile, width), lambda i, column: (i, column[0]))],
                out_specs=pl.BlockSpec((tile, width), lambda i, column: (i, 0)),
            ),
            compiler_params=pltpu.CompilerParams(vmem_limit_bytes=VMEM),
            cost_estimate=SHORT,
        )((index * own_width // width).reshape(1), weight)
        for index in indices
    ]


def project_kernel(layout, lhs_count, has_total, has_held, placed, where_ref, *refs):
    lhs = refs[:lhs_count]
    blocks = refs[lhs_count : lhs_count + len(layout)]
    rest = list(refs[lhs_count + len(layout) :])
    total_ref = rest.pop(0) if has_total else None
    if has_held:
        rest.pop(0)
    o_ref = rest.pop(0)
    segments = [(n, *segment) for n, (_, of_block) in enumerate(layout) for segment in of_block]

    def copy(i):
        n, _, start, depth = segments[i]
        out, sems = rest
        width = min(out.shape[1], o_ref.shape[1])
        rows = pl.ds(pl.multiple_of(where_ref[FIXED + len(layout) + 2 * i + 1], GROUP), depth)
        columns = pl.ds(pl.multiple_of(pl.program_id(0) * width, HD), width)
        source = blocks[n].at[pl.ds(start, depth)]
        if width < blocks[n].shape[1]:
            source = blocks[n].at[pl.ds(start, depth), pl.ds(pl.multiple_of(where_ref[2], HD), width)]
        return pltpu.make_async_copy(source, out.at[rows, columns], sems.at[i])

    def add(which):
        total = o_ref[...]
        for i in which:
            n, j, start, depth = segments[i]
            columns = pl.ds(pl.multiple_of(where_ref[FIXED + len(layout) + 2 * i], GROUP), depth)
            rows = blocks[n][start : start + depth, :]
            total += jnp.dot(lhs[j][:, columns], rows, preferred_element_type=jnp.float32)
        o_ref[...] = total

    def start(which):
        for i in which:
            copy(i).start()

    def wait(which):
        for i in which:
            copy(i).wait()

    groups = [(None, [i for i, segment in enumerate(segments) if not layout[segment[0]][0]])]
    for n, (gated, _) in enumerate(layout):
        if gated:
            groups.append((n, [i for i, segment in enumerate(segments) if segment[0] == n]))

    for n, which in groups:
        has = 1 if n is None else where_ref[FIXED + n]

        if placed and which:
            pl.when(where_ref[1] * has == 1)(functools.partial(start, which))

    o_ref[...] = total_ref[...] if has_total else jnp.zeros(o_ref.shape, jnp.float32)
    for n, which in groups:
        if which:
            has = 1 if n is None else where_ref[FIXED + n]
            pl.when(where_ref[0] * has == 1)(functools.partial(add, which))

    for n, which in groups:
        has = 1 if n is None else where_ref[FIXED + n]

        if placed and which:
            pl.when(where_ref[1] * has == 1)(functools.partial(wait, which))


def project(active, lhs, terms, total=None, placing=None, rollout=None):
    used = sorted({segment[0] for _, _, segments in terms for segment in segments})
    lhs = [lhs[j] for j in used]
    rows = lhs[0].shape[0]
    served = terms[0][0].shape[1]
    tile = min(served, 256)
    places, first_column, width = placing or (0, 0, 0)
    where = [active, places, first_column, active | places]
    where += [1 if has is None else has for _, has, _ in terms]
    for _, _, segments in terms:
        for _, offset, row, _, _ in segments:
            where += [offset, row]
    layout = [
        (has is not None, [(used.index(j), start, depth) for j, _, _, start, depth in segments])
        for _, has, segments in terms
    ]
    count = sum(len(segments) for _, segments in layout)
    added = () if total is None else (total,)
    held = () if rollout is None else (rollout,)
    column = lambda i, where: (0, i)

    def read(n):
        return lambda i, where: (0, i * where[3] * where[FIXED + n])

    anywhere = pl.BlockSpec(memory_space=pl.ANY)
    fresh_shape, fresh_spec = jax.ShapeDtypeStruct((rows, served), jnp.float32), pl.BlockSpec((rows, tile), column)
    placed = int(placing is not None)
    return pl.pallas_call(
        functools.partial(project_kernel, layout, len(lhs), bool(added), bool(held), placed),
        out_shape=[fresh_shape, jax.ShapeDtypeStruct((D, width), jnp.bfloat16)] if placing else fresh_shape,
        grid_spec=pltpu.PrefetchScalarGridSpec(
            num_scalar_prefetch=1,
            grid=(served // tile,),
            in_specs=[pl.BlockSpec(part.shape, lambda i, where: (0, 0)) for part in lhs]
            + [pl.BlockSpec((term[0].shape[0], tile), read(n)) for n, term in enumerate(terms)]
            + [fresh_spec for _ in added]
            + [anywhere for _ in held],
            out_specs=[fresh_spec, anywhere] if placing else fresh_spec,
            scratch_shapes=[pltpu.SemaphoreType.DMA((count,))] if placing else [],
        ),
        input_output_aliases={1 + len(lhs) + len(terms) + len(added): 1} if held else {},
        compiler_params=pltpu.CompilerParams(vmem_limit_bytes=VMEM),
        cost_estimate=SHORT,
    )(jnp.stack([jnp.asarray(v, jnp.int32) for v in where]), *lhs, *[term[0] for term in terms], *added, *held)


def attend_kernel(share, active_ref, bias_ref, x_ref, q_ref, c_ref, f_ref, held_ref, o_ref):
    heads = share * HALF
    scale = HD ** (-0.5)

    @pl.when((active_ref[0] == 0) & (pl.program_id(0) == 0))
    def _():
        o_ref[...] = held_ref[...]

    @pl.when(active_ref[0] == 1)
    def _():
        bias = jnp.concatenate([bias_ref[0]] * heads, axis=0)
        for g in range(q_ref.shape[1] // (heads * HD)):
            lanes = [slice((g * heads + i) * HD, (g * heads + i + 1) * HD) for i in range(heads)]
            query = jnp.concatenate([q_ref[:, lane] for lane in lanes], axis=0)
            at = g * share * PAIR
            keys = c_ref[:, :, at : at + HD].reshape(ROW_TILE * LMAX, HD)
            values = c_ref[:, :, at + HD : at + PAIR].reshape(ROW_TILE * LMAX, HD)
            fresh = f_ref[:, g * PAIR : (g + 1) * PAIR].astype(jnp.bfloat16).astype(jnp.float32)
            new_key = jnp.concatenate([fresh[:, :HD]] * heads, axis=0)
            new_value = jnp.concatenate([fresh[:, HD:]] * heads, axis=0)
            old = lax.dot_general(query, keys, (((1,), (1,)), ((), ())), preferred_element_type=jnp.float32)
            old = old * scale + bias
            new = jnp.sum(query.astype(jnp.float32) * new_key, axis=1, keepdims=True) * scale
            highest = jnp.maximum(jnp.max(old, axis=1, keepdims=True), new)
            old = jnp.exp(old - highest)
            new = jnp.exp(new - highest)
            inverse = 1.0 / (jnp.sum(old, axis=1, keepdims=True) + new)
            old = (old * inverse).astype(jnp.bfloat16)
            new = (new * inverse).astype(jnp.bfloat16).astype(jnp.float32)
            mixed = jnp.dot(old, values, preferred_element_type=jnp.float32) + new * new_value
            for i, lane in enumerate(lanes):
                total = x_ref[:, lane].astype(jnp.float32) + mixed[i * ROW_TILE : (i + 1) * ROW_TILE, :]
                o_ref[:, lane] = total.astype(jnp.bfloat16)


def seen_bias(lengths):
    column = jnp.arange(ROW_TILE * LMAX)
    own = jnp.arange(ROW_TILE)[:, None] == column[None, :] // LMAX
    seen = own[None] & ((column % LMAX)[None, None, :] < lengths.reshape(-1, ROW_TILE, 1))
    return jnp.where(seen, 0.0, -jnp.inf).astype(jnp.float32)


def attend(active, current, query, cache, bias, fresh, held):
    rows, width = query.shape
    share = min(2, width // (HALF * HD))
    wide = pl.BlockSpec((ROW_TILE, width), lambda i, active: (i * active[0], 0))
    return pl.pallas_call(
        functools.partial(attend_kernel, share),
        out_shape=jax.ShapeDtypeStruct((rows, width), jnp.bfloat16),
        grid_spec=pltpu.PrefetchScalarGridSpec(
            num_scalar_prefetch=1,
            grid=(rows // ROW_TILE,),
            in_specs=[
                pl.BlockSpec((1, *bias.shape[1:]), lambda i, active: (i * active[0], 0, 0)),
                wide,
                wide,
                pl.BlockSpec((ROW_TILE, LMAX, cache.shape[2]), lambda i, active: (i * active[0], 0, 0)),
                pl.BlockSpec((ROW_TILE, fresh.shape[1]), lambda i, active: (i * active[0], 0)),
                pl.BlockSpec((ROW_TILE, width), lambda i, active: (0, 0)),
            ],
            out_specs=wide,
        ),
        input_output_aliases={6: 0},
        compiler_params=pltpu.CompilerParams(vmem_limit_bytes=VMEM),
        cost_estimate=SHORT,
    )(active.reshape(1), bias, current, query, cache, fresh, held)


def together(*values):
    return lax.optimization_barrier(values)


def body(hidden_in, norm_gain, trainer_kv, queries, kv_cache, cache_lengths):
    sections, tensors, dps = (lax.axis_size(axis) for axis in ("section", "tensor", "dp"))
    section, tensor, dp = (lax.axis_index(axis) for axis in ("section", "tensor", "dp"))
    rows = hidden_in.shape[1]
    depth = trainer_kv.shape[1]
    own_width = 2 * KVH * HD // tensors
    served = max(own_width, PAIR)
    early, late = (1, 2), (0, 3)
    everyone = tuple(range(sections))
    is_early = ((section == 1) | (section == 2)).astype(jnp.int32)
    inner = ((dp == 1) | (dp == 2)).astype(jnp.int32)

    def over(axis, count, value, routes):
        pairs = [(a * count + i, b * count + j) for a, b, i, j in routes]
        return lax.ppermute(value, ("section", axis), pairs)

    def over_dp(value, at, target):
        return over("dp", dps, value, [(s, s, z, target[z]) for s in at for z in range(dps)])

    def over_tensor(value, at, flip, step=0):
        return over("tensor", tensors, value, [(s, s + step, t, t ^ flip) for s in at for t in range(tensors)])

    def flipped(b):
        return [z ^ b for z in range(dps)]

    def feature_block(value, b):
        return lax.dynamic_slice_in_dim(value, (dp ^ b) * depth, depth, 1)

    def normed_of(parts, inverse, gains):
        return [
            (part.astype(jnp.float32) * inverse[:, None] * gain.astype(jnp.float32)).astype(jnp.bfloat16)
            for part, gain in zip(parts, gains)
        ]

    def square_sum(part):
        wide = part.astype(jnp.float32)
        return jnp.sum(wide * wide, axis=1)

    bias = seen_bias(cache_lengths[0])
    turn = [(section == tick).astype(jnp.int32) for tick in range(sections)]

    def attended(tick, current, fresh, held):
        return attend(turn[tick], current, queries[0, 0], kv_cache[0, 0], bias, fresh, held)

    def hop(value, tick):
        return over_tensor(value, (tick - 1,), 0, 1)

    def both(part, tick):
        return [part] + [over_tensor(part, (tick,), j) for j in range(1, tensors)]

    def prepared(parts):
        inverse = lax.rsqrt(sum(square_sum(part) for part in parts) / D + epsilon)
        return normed_of(parts, inverse, gains)

    halves = [[(0, 0)], [(j, (j - 1) * depth) for j in range(1, tensors)], [(j, j * depth) for j in range(tensors)]]

    def far(at, blocks):
        return over("dp", dps, blocks[0], [(s, s, a, b) for s in at for a, b in ((0, 2), (3, 1))])

    def relayed(at, blocks):
        return over("dp", dps, blocks[3], [(s, s, a, b) for s in at for a, b in ((2, 3), (1, 0))])

    def around(at, blocks):
        return over_dp(jnp.where(inner == 1, blocks[3], blocks[0]), at, (2, 0, 3, 1))

    def terms_of(half, blocks, which, shift=0):
        terms = []
        for name in which:
            b, has = {FAR: (2, inner), RELAYED: (2, 1 - inner)}.get(name, (name, None))
            source = dp ^ b
            terms.append((blocks[name], has, [
                (j, source * depth + shift, ((tensor ^ j) * dps + source) * depth, start, depth)
                for j, start in halves[half]
            ]))
        return terms

    everything = (0, 1, 3, FAR, RELAYED)

    def placing(active):
        return (active, tensor * own_width % served, own_width)

    weight, hidden, first_kept = together(trainer_kv[0], hidden_in[0], requantize(trainer_kv[0], [tensor], own_width, served))

    squares = square_sum(hidden)
    for j in (2**i for i in range(tensors.bit_length() - 1)):
        squares = squares + over_tensor(squares, (0,), j)
    (normed,) = normed_of([hidden], lax.rsqrt(squares / D + epsilon), [norm_gain])
    first = [feature_block(normed, b) for b in range(dps)]
    weight, first = together(weight, first)
    kept = first_kept + requantize(weight, [tensor ^ j for j in range(1, tensors)], own_width, served)
    first[1:] = [over_dp(first[b], (0,), flipped(b)) for b in range(1, dps)]
    first, gain = together(first, norm_gain)
    gains = [gain] + [over_tensor(gain, everyone, j) for j in range(1, tensors)]

    def others(at, kept):
        received = [over_tensor(kept[j], at, j) for j in range(1, tensors)]
        return received[0] if len(received) == 1 else jnp.concatenate(received, axis=0)

    own = {0: kept[0], 3: over_dp(kept[0], early, flipped(3)), 1: over_dp(kept[0], early, flipped(1))}

    lhs = [jnp.concatenate(first, axis=0)]
    partial = [project(turn[0], lhs, [(kept[j], None, [(0, 0, 0, 0, depth)])]) for j in range(tensors)]
    partial, kept, gains = together(partial, kept, gains)
    rest = {0: others(early, kept)}
    total = partial[0]
    for j in range(1, tensors):
        total = total + over_tensor(partial[j].astype(jnp.bfloat16), (0,), j).astype(jnp.float32)
    total = total.reshape(dps, rows, served)
    returned = [over_dp(total[b].astype(jnp.bfloat16), (0,), flipped(b)) for b in range(1, dps)]
    fresh = total[0]
    for part in returned:
        fresh = fresh + part.astype(jnp.float32)
    result = attended(0, hidden, fresh, hidden)

    rest[3], rest[1] = over_dp(rest[0], early, flipped(3)), over_dp(rest[0], early, flipped(1))
    own, result, kept = together(own, result, kept)
    late_rest = others(late, kept)
    kept_back, rest[0] = together(own, rest[0])
    own[RELAYED], own[FAR] = relayed(early, kept_back), far(early, kept_back)
    own, rest = together(own, rest)
    rest[RELAYED], rest[FAR] = relayed(early, rest), far(early, rest)
    token = over("dp", dps, rest[3][:ROW_TILE, :HD], [(a, b, z, z) for a, b in ((1, 0), (2, 3)) for z in range(dps)])
    token, late_own, result = together(token, kept[0], result)
    whole = jnp.concatenate([late_own, late_rest], axis=0)
    shift = jnp.isnan(token[0, 0]).astype(jnp.int32)
    last = {0: whole, 3: over_dp(whole, late, flipped(3)), 1: over_dp(whole, late, flipped(1))}

    moved = both(hop(result, 1), 1)
    normed = prepared(moved)
    terms = terms_of(0, own, everything) + terms_of(1, rest, (0, 1, 3))
    fresh, rollout = project(turn[1], normed, terms, None, placing(is_early))
    fresh, rollout, rest = together(fresh, rollout, rest)
    fresh, rollout = project(turn[1], normed, terms_of(1, rest, (FAR, RELAYED)), fresh, placing(is_early), rollout)
    result = attended(1, moved[0], fresh, result)

    terms = terms_of(0, own, everything) + terms_of(1, rest, everything)
    moved, last = together(both(hop(result, 2), 2), last)
    last[RELAYED], last[FAR] = relayed(late, last), far(late, last)
    result = attended(2, moved[0], project(turn[2], prepared(moved), terms), result)
    moved = both(hop(result, 3), 3)
    normed = prepared(moved)
    fresh, rollout = project(turn[3], normed, terms_of(2, last, (0, 1, 3), shift), None, placing(1 - is_early), rollout)
    fresh, rollout, last = together(fresh, rollout, last)
    fresh, rollout = project(turn[3], normed, terms_of(2, last, (FAR, RELAYED)), fresh, placing(1 - is_early), rollout)
    result = attended(3, moved[0], fresh, result)
    return (rollout[None], result[None, None])


def solution(mesh):
    placed = (
        P(None, "dp", "tensor"),
        P("section", "tensor"),
        P("section", ("tensor", "dp"), None),
        P("section", None, "dp", "tensor"),
        P("section", None, "dp", None, "tensor"),
        P(None, "dp"),
    )
    return jax.shard_map(
        body,
        mesh=mesh,
        in_specs=placed,
        out_specs=(P("section", None, "tensor"), P("section", None, "dp", "tensor")),
        check_vma=False,
    )
```

```python
import functools

import jax
import jax.numpy as jnp
from jax import lax
from jax.experimental import pallas as pl
from jax.experimental.pallas import tpu as pltpu
from jax.sharding import PartitionSpec as P

D = 16384
KVH = 8
HD = 128
GQ = 16
GROUP = 128
LMAX = 16
HALF = GQ // 2
PAIR = 2 * HD
ROW_TILE = 16

epsilon = 1e-05
clip_ratio = 2.0
FAR, RELAYED = 4, 5
FIXED = 4
VMEM = 60 << 20
SHORT = pl.CostEstimate(flops=0, bytes_accessed=0, transcendentals=0)


def requantize_kernel(column_ref, w_ref, o_ref):
    ones = jnp.ones((ROW_TILE, GROUP), jnp.bfloat16)
    for start in range(0, w_ref.shape[0], GROUP):
        block = w_ref[start : start + GROUP, :]
        total = jnp.dot(ones, jnp.abs(block), preferred_element_type=jnp.float32)[:1]
        limit = (total * (clip_ratio / GROUP)).astype(jnp.bfloat16)
        o_ref[start : start + GROUP, :] = jnp.minimum(jnp.maximum(block, -limit), limit)


def requantize(weight, indices, own_width, width):
    rows = weight.shape[0]
    tile = min(rows, 4 * GROUP)
    return [
        pl.pallas_call(
            requantize_kernel,
            out_shape=jax.ShapeDtypeStruct((rows, width), jnp.bfloat16),
            grid_spec=pltpu.PrefetchScalarGridSpec(
                num_scalar_prefetch=1,
                grid=(rows // tile,),
                in_specs=[pl.BlockSpec((tile, width), lambda i, column: (i, column[0]))],
                out_specs=pl.BlockSpec((tile, width), lambda i, column: (i, 0)),
            ),
            compiler_params=pltpu.CompilerParams(vmem_limit_bytes=VMEM),
            cost_estimate=SHORT,
        )((index * own_width // width).reshape(1), weight)
        for index in indices
    ]


def project_kernel(layout, lhs_count, has_total, has_held, placed, where_ref, *refs):
    lhs = refs[:lhs_count]
    blocks = refs[lhs_count : lhs_count + len(layout)]
    rest = list(refs[lhs_count + len(layout) :])
    total_ref = rest.pop(0) if has_total else None
    if has_held:
        rest.pop(0)
    o_ref = rest.pop(0)
    segments = [(n, *segment) for n, (_, of_block) in enumerate(layout) for segment in of_block]

    def copy(i):
        n, _, start, depth = segments[i]
        out, sems = rest
        width = min(out.shape[1], o_ref.shape[1])
        rows = pl.ds(pl.multiple_of(where_ref[FIXED + len(layout) + 2 * i + 1], GROUP), depth)
        columns = pl.ds(pl.multiple_of(pl.program_id(0) * width, HD), width)
        source = blocks[n].at[pl.ds(start, depth)]
        if width < blocks[n].shape[1]:
            source = blocks[n].at[pl.ds(start, depth), pl.ds(pl.multiple_of(where_ref[2], HD), width)]
        return pltpu.make_async_copy(source, out.at[rows, columns], sems.at[i])

    def add(which):
        total = o_ref[...]
        for i in which:
            n, j, start, depth = segments[i]
            columns = pl.ds(pl.multiple_of(where_ref[FIXED + len(layout) + 2 * i], GROUP), depth)
            rows = blocks[n][start : start + depth, :]
            total += jnp.dot(lhs[j][:, columns], rows, preferred_element_type=jnp.float32)
        o_ref[...] = total

    def start(which):
        for i in which:
            copy(i).start()

    def wait(which):
        for i in which:
            copy(i).wait()

    groups = [(None, [i for i, segment in enumerate(segments) if not layout[segment[0]][0]])]
    for n, (gated, _) in enumerate(layout):
        if gated:
            groups.append((n, [i for i, segment in enumerate(segments) if segment[0] == n]))

    for n, which in groups:
        has = 1 if n is None else where_ref[FIXED + n]

        if placed and which:
            pl.when(where_ref[1] * has == 1)(functools.partial(start, which))

    o_ref[...] = total_ref[...] if has_total else jnp.zeros(o_ref.shape, jnp.float32)
    for n, which in groups:
        if which:
            has = 1 if n is None else where_ref[FIXED + n]
            pl.when(where_ref[0] * has == 1)(functools.partial(add, which))

    for n, which in groups:
        has = 1 if n is None else where_ref[FIXED + n]

        if placed and which:
            pl.when(where_ref[1] * has == 1)(functools.partial(wait, which))


def project(active, lhs, terms, total=None, placing=None, rollout=None):
    used = sorted({segment[0] for _, _, segments in terms for segment in segments})
    lhs = [lhs[j] for j in used]
    rows = lhs[0].shape[0]
    served = terms[0][0].shape[1]
    tile = min(served, 256)
    places, first_column, width = placing or (0, 0, 0)
    where = [active, places, first_column, active | places]
    where += [1 if has is None else has for _, has, _ in terms]
    for _, _, segments in terms:
        for _, offset, row, _, _ in segments:
            where += [offset, row]
    layout = [
        (has is not None, [(used.index(j), start, depth) for j, _, _, start, depth in segments])
        for _, has, segments in terms
    ]
    count = sum(len(segments) for _, segments in layout)
    added = () if total is None else (total,)
    held = () if rollout is None else (rollout,)
    column = lambda i, where: (0, i)

    def read(n):
        return lambda i, where: (0, i * where[3] * where[FIXED + n])

    anywhere = pl.BlockSpec(memory_space=pl.ANY)
    fresh_shape, fresh_spec = jax.ShapeDtypeStruct((rows, served), jnp.float32), pl.BlockSpec((rows, tile), column)
    placed = int(placing is not None)
    return pl.pallas_call(
        functools.partial(project_kernel, layout, len(lhs), bool(added), bool(held), placed),
        out_shape=[fresh_shape, jax.ShapeDtypeStruct((D, width), jnp.bfloat16)] if placing else fresh_shape,
        grid_spec=pltpu.PrefetchScalarGridSpec(
            num_scalar_prefetch=1,
            grid=(served // tile,),
            in_specs=[pl.BlockSpec(part.shape, lambda i, where: (0, 0)) for part in lhs]
            + [pl.BlockSpec((term[0].shape[0], tile), read(n)) for n, term in enumerate(terms)]
            + [fresh_spec for _ in added]
            + [anywhere for _ in held],
            out_specs=[fresh_spec, anywhere] if placing else fresh_spec,
            scratch_shapes=[pltpu.SemaphoreType.DMA((count,))] if placing else [],
        ),
        input_output_aliases={1 + len(lhs) + len(terms) + len(added): 1} if held else {},
        compiler_params=pltpu.CompilerParams(vmem_limit_bytes=VMEM),
        cost_estimate=SHORT,
    )(jnp.stack([jnp.asarray(v, jnp.int32) for v in where]), *lhs, *[term[0] for term in terms], *added, *held)


def attend_kernel(share, active_ref, bias_ref, x_ref, q_ref, c_ref, f_ref, held_ref, o_ref):
    heads = share * HALF
    scale = HD ** (-0.5)

    @pl.when((active_ref[0] == 0) & (pl.program_id(0) == 0))
    def _():
        o_ref[...] = held_ref[...]

    @pl.when(active_ref[0] == 1)
    def _():
        bias = jnp.concatenate([bias_ref[0]] * heads, axis=0)
        for g in range(q_ref.shape[1] // (heads * HD)):
            lanes = [slice((g * heads + i) * HD, (g * heads + i + 1) * HD) for i in range(heads)]
            query = jnp.concatenate([q_ref[:, lane] for lane in lanes], axis=0)
            at = g * share * PAIR
            keys = c_ref[:, :, at : at + HD].reshape(ROW_TILE * LMAX, HD)
            values = c_ref[:, :, at + HD : at + PAIR].reshape(ROW_TILE * LMAX, HD)
            fresh = f_ref[:, g * PAIR : (g + 1) * PAIR].astype(jnp.bfloat16).astype(jnp.float32)
            new_key = jnp.concatenate([fresh[:, :HD]] * heads, axis=0)
            new_value = jnp.concatenate([fresh[:, HD:]] * heads, axis=0)
            old = lax.dot_general(query, keys, (((1,), (1,)), ((), ())), preferred_element_type=jnp.float32)
            old = old * scale + bias
            new = jnp.sum(query.astype(jnp.float32) * new_key, axis=1, keepdims=True) * scale
            highest = jnp.maximum(jnp.max(old, axis=1, keepdims=True), new)
            old = jnp.exp(old - highest)
            new = jnp.exp(new - highest)
            inverse = 1.0 / (jnp.sum(old, axis=1, keepdims=True) + new)
            old = (old * inverse).astype(jnp.bfloat16)
            new = (new * inverse).astype(jnp.bfloat16).astype(jnp.float32)
            mixed = jnp.dot(old, values, preferred_element_type=jnp.float32) + new * new_value
            for i, lane in enumerate(lanes):
                total = x_ref[:, lane].astype(jnp.float32) + mixed[i * ROW_TILE : (i + 1) * ROW_TILE, :]
                o_ref[:, lane] = total.astype(jnp.bfloat16)


def seen_bias(lengths):
    column = jnp.arange(ROW_TILE * LMAX)
    own = jnp.arange(ROW_TILE)[:, None] == column[None, :] // LMAX
    seen = own[None] & ((column % LMAX)[None, None, :] < lengths.reshape(-1, ROW_TILE, 1))
    return jnp.where(seen, 0.0, -jnp.inf).astype(jnp.float32)


def attend(active, current, query, cache, bias, fresh, held):
    rows, width = query.shape
    share = min(2, width // (HALF * HD))
    wide = pl.BlockSpec((ROW_TILE, width), lambda i, active: (i * active[0], 0))
    return pl.pallas_call(
        functools.partial(attend_kernel, share),
        out_shape=jax.ShapeDtypeStruct((rows, width), jnp.bfloat16),
        grid_spec=pltpu.PrefetchScalarGridSpec(
            num_scalar_prefetch=1,
            grid=(rows // ROW_TILE,),
            in_specs=[
                pl.BlockSpec((1, *bias.shape[1:]), lambda i, active: (i * active[0], 0, 0)),
                wide,
                wide,
                pl.BlockSpec((ROW_TILE, LMAX, cache.shape[2]), lambda i, active: (i * active[0], 0, 0)),
                pl.BlockSpec((ROW_TILE, fresh.shape[1]), lambda i, active: (i * active[0], 0)),
                pl.BlockSpec((ROW_TILE, width), lambda i, active: (0, 0)),
            ],
            out_specs=wide,
        ),
        input_output_aliases={6: 0},
        compiler_params=pltpu.CompilerParams(vmem_limit_bytes=VMEM),
        cost_estimate=SHORT,
    )(active.reshape(1), bias, current, query, cache, fresh, held)


def together(*values):
    return lax.optimization_barrier(values)


def body(hidden_in, norm_gain, trainer_kv, queries, kv_cache, cache_lengths):
    sections, tensors, dps = (lax.axis_size(axis) for axis in ("section", "tensor", "dp"))
    section, tensor, dp = (lax.axis_index(axis) for axis in ("section", "tensor", "dp"))
    rows = hidden_in.shape[1]
    depth = trainer_kv.shape[1]
    own_width = 2 * KVH * HD // tensors
    served = max(own_width, PAIR)
    early, late = (1, 2), (0, 3)
    everyone = tuple(range(sections))
    is_early = ((section == 1) | (section == 2)).astype(jnp.int32)
    inner = ((dp == 1) | (dp == 2)).astype(jnp.int32)

    def over(axis, count, value, routes):
        pairs = [(a * count + i, b * count + j) for a, b, i, j in routes]
        return lax.ppermute(value, ("section", axis), pairs)

    def over_dp(value, at, target):
        return over("dp", dps, value, [(s, s, z, target[z]) for s in at for z in range(dps)])

    def over_tensor(value, at, flip, step=0):
        return over("tensor", tensors, value, [(s, s + step, t, t ^ flip) for s in at for t in range(tensors)])

    def flipped(b):
        return [z ^ b for z in range(dps)]

    def feature_block(value, b):
        return lax.dynamic_slice_in_dim(value, (dp ^ b) * depth, depth, 1)

    def normed_of(parts, inverse, gains):
        return [
            (part.astype(jnp.float32) * inverse[:, None] * gain.astype(jnp.float32)).astype(jnp.bfloat16)
            for part, gain in zip(parts, gains)
        ]

    def square_sum(part):
        wide = part.astype(jnp.float32)
        return jnp.sum(wide * wide, axis=1)

    bias = seen_bias(cache_lengths[0])
    turn = [(section == tick).astype(jnp.int32) for tick in range(sections)]

    def attended(tick, current, fresh, held):
        return attend(turn[tick], current, queries[0, 0], kv_cache[0, 0], bias, fresh, held)

    def hop(value, tick):
        return over_tensor(value, (tick - 1,), 0, 1)

    def both(part, tick):
        return [part] + [over_tensor(part, (tick,), j) for j in range(1, tensors)]

    def prepared(parts):
        inverse = lax.rsqrt(sum(square_sum(part) for part in parts) / D + epsilon)
        return normed_of(parts, inverse, gains)

    halves = [[(0, 0)], [(j, (j - 1) * depth) for j in range(1, tensors)], [(j, j * depth) for j in range(tensors)]]

    def far(at, blocks):
        return over("dp", dps, blocks[0], [(s, s, a, b) for s in at for a, b in ((0, 2), (3, 1))])

    def relayed(at, blocks):
        return over("dp", dps, blocks[3], [(s, s, a, b) for s in at for a, b in ((2, 3), (1, 0))])

    def around(at, blocks):
        return over_dp(jnp.where(inner == 1, blocks[3], blocks[0]), at, (2, 0, 3, 1))

    def terms_of(half, blocks, which, shift=0):
        terms = []
        for name in which:
            b, has = {FAR: (2, inner), RELAYED: (2, 1 - inner)}.get(name, (name, None))
            source = dp ^ b
            terms.append((blocks[name], has, [
                (j, source * depth + shift, ((tensor ^ j) * dps + source) * depth, start, depth)
                for j, start in halves[half]
            ]))
        return terms

    everything = (0, 1, 3, FAR, RELAYED)

    def placing(active):
        return (active, tensor * own_width % served, own_width)

    weight, hidden, first_kept = together(trainer_kv[0], hidden_in[0], requantize(trainer_kv[0], [tensor], own_width, served))

    squares = square_sum(hidden)
    for j in (2**i for i in range(tensors.bit_length() - 1)):
        squares = squares + over_tensor(squares, (0,), j)
    (normed,) = normed_of([hidden], lax.rsqrt(squares / D + epsilon), [norm_gain])
    first = [feature_block(normed, b) for b in range(dps)]
    weight, first = together(weight, first)
    kept = first_kept + requantize(weight, [tensor ^ j for j in range(1, tensors)], own_width, served)
    first[1:] = [over_dp(first[b], (0,), flipped(b)) for b in range(1, dps)]
    first, gain = together(first, norm_gain)
    gains = [gain] + [over_tensor(gain, everyone, j) for j in range(1, tensors)]

    def others(at, kept):
        received = [over_tensor(kept[j], at, j) for j in range(1, tensors)]
        return received[0] if len(received) == 1 else jnp.concatenate(received, axis=0)

    own = {0: kept[0], 3: over_dp(kept[0], early, flipped(3)), 1: over_dp(kept[0], early, flipped(1))}

    lhs = [jnp.concatenate(first, axis=0)]
    partial = [project(turn[0], lhs, [(kept[j], None, [(0, 0, 0, 0, depth)])]) for j in range(tensors)]
    partial, kept, gains = together(partial, kept, gains)
    rest = {0: others(early, kept)}
    total = partial[0]
    for j in range(1, tensors):
        total = total + over_tensor(partial[j].astype(jnp.bfloat16), (0,), j).astype(jnp.float32)
    total = total.reshape(dps, rows, served)
    step = 1
    while step < dps:
        send = jnp.stack([total[b] for b in range(total.shape[0]) if b & 1]).astype(jnp.bfloat16)
        keep = jnp.stack([total[b] for b in range(total.shape[0]) if not b & 1])
        total = keep + over_dp(send, (0,), flipped(step)).astype(jnp.float32)
        step *= 2
    fresh = total[0]
    result = attended(0, hidden, fresh, hidden)

    rest[3], rest[1] = over_dp(rest[0], early, flipped(3)), over_dp(rest[0], early, flipped(1))
    own, result, kept = together(own, result, kept)
    parts = both(result, 0)
    late_rest = others(late, kept)
    kept_back, rest[0] = together(own, rest[0])
    own[RELAYED], own[FAR] = relayed(early, kept_back), far(early, kept_back)
    own, rest = together(own, rest)
    rest[RELAYED], rest[FAR] = relayed(early, rest), far(early, rest)
    token = over("dp", dps, rest[3][:ROW_TILE, :HD], [(a, b, z, z) for a, b in ((1, 0), (2, 3)) for z in range(dps)])
    token, late_own, parts = together(token, kept[0], parts)
    whole = jnp.concatenate([late_own, late_rest], axis=0)
    shift = jnp.isnan(token[0, 0]).astype(jnp.int32)
    last = {0: whole, 3: over_dp(whole, late, flipped(3)), 1: over_dp(whole, late, flipped(1))}

    moved = [hop(part, 1) for part in parts]
    normed = prepared(moved)
    terms = terms_of(0, own, everything) + terms_of(1, rest, (0, 1, 3))
    fresh, rollout = project(turn[1], normed, terms, None, placing(is_early))
    fresh, rollout, rest = together(fresh, rollout, rest)
    fresh, rollout = project(turn[1], normed, terms_of(1, rest, (FAR, RELAYED)), fresh, placing(is_early), rollout)
    result = attended(1, moved[0], fresh, result)

    terms = terms_of(0, own, everything) + terms_of(1, rest, everything)
    moved, last = together(both(hop(result, 2), 2), last)
    last[RELAYED], last[FAR] = relayed(late, last), far(late, last)
    result = attended(2, moved[0], project(turn[2], prepared(moved), terms), result)
    moved = both(hop(result, 3), 3)
    normed = prepared(moved)
    fresh, rollout = project(turn[3], normed, terms_of(2, last, (0, 1, 3), shift), None, placing(1 - is_early), rollout)
    fresh, rollout, last = together(fresh, rollout, last)
    fresh, rollout = project(turn[3], normed, terms_of(2, last, (FAR, RELAYED)), fresh, placing(1 - is_early), rollout)
    result = attended(3, moved[0], fresh, result)
    return (rollout[None], result[None, None])


def solution(mesh):
    placed = (
        P(None, "dp", "tensor"),
        P("section", "tensor"),
        P("section", ("tensor", "dp"), None),
        P("section", None, "dp", "tensor"),
        P("section", None, "dp", None, "tensor"),
        P(None, "dp"),
    )
    return jax.shard_map(
        body,
        mesh=mesh,
        in_specs=placed,
        out_specs=(P("section", None, "tensor"), P("section", None, "dp", "tensor")),
        check_vma=False,
    )
```

```python
import functools

import jax
import jax.numpy as jnp
from jax import lax
from jax.experimental import pallas as pl
from jax.experimental.pallas import tpu as pltpu
from jax.sharding import PartitionSpec as P

D = 16384
KVH = 8
HD = 128
GQ = 16
GROUP = 128
LMAX = 16
HALF = GQ // 2
PAIR = 2 * HD
ROW_TILE = 16

epsilon = 1e-05
clip_ratio = 2.0
INNER, RELAYED = 4, 5
FIXED = 4
VMEM = 60 << 20
SHORT = pl.CostEstimate(flops=0, bytes_accessed=0, transcendentals=0)


def requantize_kernel(column_ref, w_ref, o_ref):
    ones = jnp.ones((ROW_TILE, GROUP), jnp.bfloat16)
    for start in range(0, w_ref.shape[0], GROUP):
        block = w_ref[start : start + GROUP, :]
        total = jnp.dot(ones, jnp.abs(block), preferred_element_type=jnp.float32)[:1]
        limit = (total * (clip_ratio / GROUP)).astype(jnp.bfloat16)
        o_ref[start : start + GROUP, :] = jnp.minimum(jnp.maximum(block, -limit), limit)


def requantize(weight, indices, own_width, width):
    rows = weight.shape[0]
    tile = min(rows, 4 * GROUP)
    return [
        pl.pallas_call(
            requantize_kernel,
            out_shape=jax.ShapeDtypeStruct((rows, width), jnp.bfloat16),
            grid_spec=pltpu.PrefetchScalarGridSpec(
                num_scalar_prefetch=1,
                grid=(rows // tile,),
                in_specs=[pl.BlockSpec((tile, width), lambda i, column: (i, column[0]))],
                out_specs=pl.BlockSpec((tile, width), lambda i, column: (i, 0)),
            ),
            compiler_params=pltpu.CompilerParams(vmem_limit_bytes=VMEM),
            cost_estimate=SHORT,
        )((index * own_width // width).reshape(1), weight)
        for index in indices
    ]


def project_kernel(layout, lhs_count, has_total, has_held, placed, where_ref, *refs):
    lhs = refs[:lhs_count]
    blocks = refs[lhs_count : lhs_count + len(layout)]
    rest = list(refs[lhs_count + len(layout) :])
    total_ref = rest.pop(0) if has_total else None
    if has_held:
        rest.pop(0)
    o_ref = rest.pop(0)
    segments = [(n, *segment) for n, (_, of_block) in enumerate(layout) for segment in of_block]

    def copy(i):
        n, _, start, depth = segments[i]
        out, sems = rest
        width = min(out.shape[1], o_ref.shape[1])
        rows = pl.ds(pl.multiple_of(where_ref[FIXED + len(layout) + 2 * i + 1], GROUP), depth)
        columns = pl.ds(pl.multiple_of(pl.program_id(0) * width, HD), width)
        source = blocks[n].at[pl.ds(start, depth)]
        if width < blocks[n].shape[1]:
            source = blocks[n].at[pl.ds(start, depth), pl.ds(pl.multiple_of(where_ref[2], HD), width)]
        return pltpu.make_async_copy(source, out.at[rows, columns], sems.at[i])

    def add(which):
        total = o_ref[...]
        for i in which:
            n, j, start, depth = segments[i]
            columns = pl.ds(pl.multiple_of(where_ref[FIXED + len(layout) + 2 * i], GROUP), depth)
            rows = blocks[n][start : start + depth, :]
            total += jnp.dot(lhs[j][:, columns], rows, preferred_element_type=jnp.float32)
        o_ref[...] = total

    def start(which):
        for i in which:
            copy(i).start()

    def wait(which):
        for i in which:
            copy(i).wait()

    groups = [(None, [i for i, segment in enumerate(segments) if not layout[segment[0]][0]])]
    for n, (gated, _) in enumerate(layout):
        if gated:
            groups.append((n, [i for i, segment in enumerate(segments) if segment[0] == n]))

    for n, which in groups:
        has = 1 if n is None else where_ref[FIXED + n]

        if placed and which:
            pl.when(where_ref[1] * has == 1)(functools.partial(start, which))

    o_ref[...] = total_ref[...] if has_total else jnp.zeros(o_ref.shape, jnp.float32)
    for n, which in groups:
        if which:
            has = 1 if n is None else where_ref[FIXED + n]
            pl.when(where_ref[0] * has == 1)(functools.partial(add, which))

    for n, which in groups:
        has = 1 if n is None else where_ref[FIXED + n]

        if placed and which:
            pl.when(where_ref[1] * has == 1)(functools.partial(wait, which))


def project(active, lhs, terms, total=None, placing=None, rollout=None):
    used = sorted({segment[0] for _, _, segments in terms for segment in segments})
    lhs = [lhs[j] for j in used]
    rows = lhs[0].shape[0]
    served = terms[0][0].shape[1]
    tile = min(served, 256)
    places, first_column, width = placing or (0, 0, 0)
    where = [active, places, first_column, active | places]
    where += [1 if has is None else has for _, has, _ in terms]
    for _, _, segments in terms:
        for _, offset, row, _, _ in segments:
            where += [offset, row]
    layout = [
        (has is not None, [(used.index(j), start, depth) for j, _, _, start, depth in segments])
        for _, has, segments in terms
    ]
    count = sum(len(segments) for _, segments in layout)
    added = () if total is None else (total,)
    held = () if rollout is None else (rollout,)
    column = lambda i, where: (0, i)

    def read(n):
        return lambda i, where: (0, i * where[3] * where[FIXED + n])

    anywhere = pl.BlockSpec(memory_space=pl.ANY)
    fresh_shape, fresh_spec = jax.ShapeDtypeStruct((rows, served), jnp.float32), pl.BlockSpec((rows, tile), column)
    placed = int(placing is not None)
    return pl.pallas_call(
        functools.partial(project_kernel, layout, len(lhs), bool(added), bool(held), placed),
        out_shape=[fresh_shape, jax.ShapeDtypeStruct((D, width), jnp.bfloat16)] if placing else fresh_shape,
        grid_spec=pltpu.PrefetchScalarGridSpec(
            num_scalar_prefetch=1,
            grid=(served // tile,),
            in_specs=[pl.BlockSpec(part.shape, lambda i, where: (0, 0)) for part in lhs]
            + [pl.BlockSpec((term[0].shape[0], tile), read(n)) for n, term in enumerate(terms)]
            + [fresh_spec for _ in added]
            + [anywhere for _ in held],
            out_specs=[fresh_spec, anywhere] if placing else fresh_spec,
            scratch_shapes=[pltpu.SemaphoreType.DMA((count,))] if placing else [],
        ),
        input_output_aliases={1 + len(lhs) + len(terms) + len(added): 1} if held else {},
        compiler_params=pltpu.CompilerParams(vmem_limit_bytes=VMEM),
        cost_estimate=SHORT,
    )(jnp.stack([jnp.asarray(v, jnp.int32) for v in where]), *lhs, *[term[0] for term in terms], *added, *held)


def attend_kernel(share, active_ref, bias_ref, x_ref, q_ref, c_ref, f_ref, held_ref, o_ref):
    heads = share * HALF
    scale = HD ** (-0.5)

    @pl.when((active_ref[0] == 0) & (pl.program_id(0) == 0))
    def _():
        o_ref[...] = held_ref[...]

    @pl.when(active_ref[0] == 1)
    def _():
        bias = jnp.concatenate([bias_ref[0]] * heads, axis=0)
        for g in range(q_ref.shape[1] // (heads * HD)):
            lanes = [slice((g * heads + i) * HD, (g * heads + i + 1) * HD) for i in range(heads)]
            query = jnp.concatenate([q_ref[:, lane] for lane in lanes], axis=0)
            at = g * share * PAIR
            keys = c_ref[:, :, at : at + HD].reshape(ROW_TILE * LMAX, HD)
            values = c_ref[:, :, at + HD : at + PAIR].reshape(ROW_TILE * LMAX, HD)
            fresh = f_ref[:, g * PAIR : (g + 1) * PAIR].astype(jnp.bfloat16).astype(jnp.float32)
            new_key = jnp.concatenate([fresh[:, :HD]] * heads, axis=0)
            new_value = jnp.concatenate([fresh[:, HD:]] * heads, axis=0)
            old = lax.dot_general(query, keys, (((1,), (1,)), ((), ())), preferred_element_type=jnp.float32)
            old = old * scale + bias
            new = jnp.sum(query.astype(jnp.float32) * new_key, axis=1, keepdims=True) * scale
            highest = jnp.maximum(jnp.max(old, axis=1, keepdims=True), new)
            old = jnp.exp(old - highest)
            new = jnp.exp(new - highest)
            inverse = 1.0 / (jnp.sum(old, axis=1, keepdims=True) + new)
            old = (old * inverse).astype(jnp.bfloat16)
            new = (new * inverse).astype(jnp.bfloat16).astype(jnp.float32)
            mixed = jnp.dot(old, values, preferred_element_type=jnp.float32) + new * new_value
            for i, lane in enumerate(lanes):
                total = x_ref[:, lane].astype(jnp.float32) + mixed[i * ROW_TILE : (i + 1) * ROW_TILE, :]
                o_ref[:, lane] = total.astype(jnp.bfloat16)


def seen_bias(lengths):
    column = jnp.arange(ROW_TILE * LMAX)
    own = jnp.arange(ROW_TILE)[:, None] == column[None, :] // LMAX
    seen = own[None] & ((column % LMAX)[None, None, :] < lengths.reshape(-1, ROW_TILE, 1))
    return jnp.where(seen, 0.0, -jnp.inf).astype(jnp.float32)


def attend(active, current, query, cache, bias, fresh, held):
    rows, width = query.shape
    share = min(2, width // (HALF * HD))
    wide = pl.BlockSpec((ROW_TILE, width), lambda i, active: (i * active[0], 0))
    return pl.pallas_call(
        functools.partial(attend_kernel, share),
        out_shape=jax.ShapeDtypeStruct((rows, width), jnp.bfloat16),
        grid_spec=pltpu.PrefetchScalarGridSpec(
            num_scalar_prefetch=1,
            grid=(rows // ROW_TILE,),
            in_specs=[
                pl.BlockSpec((1, *bias.shape[1:]), lambda i, active: (i * active[0], 0, 0)),
                wide,
                wide,
                pl.BlockSpec((ROW_TILE, LMAX, cache.shape[2]), lambda i, active: (i * active[0], 0, 0)),
                pl.BlockSpec((ROW_TILE, fresh.shape[1]), lambda i, active: (i * active[0], 0)),
                pl.BlockSpec((ROW_TILE, width), lambda i, active: (0, 0)),
            ],
            out_specs=wide,
        ),
        input_output_aliases={6: 0},
        compiler_params=pltpu.CompilerParams(vmem_limit_bytes=VMEM),
        cost_estimate=SHORT,
    )(active.reshape(1), bias, current, query, cache, fresh, held)


def together(*values):
    return lax.optimization_barrier(values)


def body(hidden_in, norm_gain, trainer_kv, queries, kv_cache, cache_lengths):
    sections, tensors, dps = (lax.axis_size(axis) for axis in ("section", "tensor", "dp"))
    section, tensor, dp = (lax.axis_index(axis) for axis in ("section", "tensor", "dp"))
    rows = hidden_in.shape[1]
    depth = trainer_kv.shape[1]
    own_width = 2 * KVH * HD // tensors
    served = max(own_width, PAIR)
    early, late = (1, 2), (0, 3)
    everyone = tuple(range(sections))
    is_early = ((section == 1) | (section == 2)).astype(jnp.int32)
    inner = ((dp == 1) | (dp == 2)).astype(jnp.int32)

    def over(axis, count, value, routes):
        pairs = [(a * count + i, b * count + j) for a, b, i, j in routes]
        return lax.ppermute(value, ("section", axis), pairs)

    def over_dp(value, at, target):
        return over("dp", dps, value, [(s, s, z, target[z]) for s in at for z in range(dps)])

    def over_tensor(value, at, flip, step=0):
        return over("tensor", tensors, value, [(s, s + step, t, t ^ flip) for s in at for t in range(tensors)])

    def flipped(b):
        return [z ^ b for z in range(dps)]

    def feature_block(value, b):
        return lax.dynamic_slice_in_dim(value, (dp ^ b) * depth, depth, 1)

    def normed_of(parts, inverse, gains):
        return [
            (part.astype(jnp.float32) * inverse[:, None] * gain.astype(jnp.float32)).astype(jnp.bfloat16)
            for part, gain in zip(parts, gains)
        ]

    def square_sum(part):
        wide = part.astype(jnp.float32)
        return jnp.sum(wide * wide, axis=1)

    bias = seen_bias(cache_lengths[0])
    turn = [(section == tick).astype(jnp.int32) for tick in range(sections)]

    def attended(tick, current, fresh, held):
        return attend(turn[tick], current, queries[0, 0], kv_cache[0, 0], bias, fresh, held)

    def hop(value, tick):
        return over_tensor(value, (tick - 1,), 0, 1)

    def both(part, tick):
        return [part] + [over_tensor(part, (tick,), j) for j in range(1, tensors)]

    def prepared(parts):
        inverse = lax.rsqrt(sum(square_sum(part) for part in parts) / D + epsilon)
        return normed_of(parts, inverse, gains)

    halves = [[(0, 0)], [(j, (j - 1) * depth) for j in range(1, tensors)], [(j, j * depth) for j in range(tensors)]]

    def across(at, blocks):
        return over("dp", dps, blocks[0], [(s, s, a, b) for s in at for a, b in ((1, 2), (2, 1))])

    def relayed(at, blocks):
        return over("dp", dps, blocks[2], [(s, s, a, b) for s in at for a, b in ((2, 3), (1, 0))])

    def terms_of(half, blocks, which, shift=0):
        terms = []
        for name in which:
            b, has = {INNER: (3, inner), RELAYED: (3, 1 - inner)}.get(name, (name, None))
            source = dp ^ b
            terms.append((blocks[name], has, [
                (j, source * depth + shift, ((tensor ^ j) * dps + source) * depth, start, depth)
                for j, start in halves[half]
            ]))
        return terms

    everything = (0, 1, 2, INNER, RELAYED)

    def placing(active):
        return (active, tensor * own_width % served, own_width)

    weight, hidden, first_kept = together(trainer_kv[0], hidden_in[0], requantize(trainer_kv[0], [tensor], own_width, served))

    squares = square_sum(hidden)
    for j in (2**i for i in range(tensors.bit_length() - 1)):
        squares = squares + over_tensor(squares, (0,), j)
    (normed,) = normed_of([hidden], lax.rsqrt(squares / D + epsilon), [norm_gain])
    first = [feature_block(normed, b) for b in range(dps)]
    weight, first = together(weight, first)
    kept = first_kept + requantize(weight, [tensor ^ j for j in range(1, tensors)], own_width, served)
    first[1:] = [over_dp(first[b], (0,), flipped(b)) for b in range(1, dps)]
    first, gain = together(first, norm_gain)
    gains = [gain] + [over_tensor(gain, everyone, j) for j in range(1, tensors)]

    def others(at, kept):
        received = [over_tensor(kept[j], at, j) for j in range(1, tensors)]
        return received[0] if len(received) == 1 else jnp.concatenate(received, axis=0)

    own = {0: kept[0], 2: over_dp(kept[0], early, flipped(2)), 1: over_dp(kept[0], early, flipped(1))}

    lhs = [jnp.concatenate(first, axis=0)]
    partial = [project(turn[0], lhs, [(kept[j], None, [(0, 0, 0, 0, depth)])]) for j in range(tensors)]
    partial, kept, gains = together(partial, kept, gains)
    rest = {0: others(early, kept)}
    total = partial[0]
    for j in range(1, tensors):
        total = total + over_tensor(partial[j].astype(jnp.bfloat16), (0,), j).astype(jnp.float32)
    total = total.reshape(dps, rows, served)
    step = 1
    while step < dps:
        send = jnp.stack([total[b] for b in range(total.shape[0]) if b & 1]).astype(jnp.bfloat16)
        keep = jnp.stack([total[b] for b in range(total.shape[0]) if not b & 1])
        total = keep + over_dp(send, (0,), flipped(step)).astype(jnp.float32)
        step *= 2
    fresh = total[0]
    result = attended(0, hidden, fresh, hidden)

    rest[2], rest[1] = over_dp(rest[0], early, flipped(2)), over_dp(rest[0], early, flipped(1))
    own, result, kept = together(own, result, kept)
    parts = both(result, 0)
    late_rest = others(late, kept)
    kept_back, rest[0] = together(own, rest[0])
    own[RELAYED], own[INNER] = relayed(early, kept_back), across(early, kept_back)
    own, rest = together(own, rest)
    rest[RELAYED], rest[INNER] = relayed(early, rest), across(early, rest)
    token = over("dp", dps, rest[2][:ROW_TILE, :HD], [(a, b, z, z) for a, b in ((1, 0), (2, 3)) for z in range(dps)])
    token, late_own, parts = together(token, kept[0], parts)
    whole = jnp.concatenate([late_own, late_rest], axis=0)
    shift = jnp.isnan(token[0, 0]).astype(jnp.int32)
    last = {0: whole, 2: over_dp(whole, late, flipped(2)), 1: over_dp(whole, late, flipped(1))}

    moved = [hop(part, 1) for part in parts]
    normed = prepared(moved)
    terms = terms_of(0, own, everything) + terms_of(1, rest, (0, 1, 2))
    fresh, rollout = project(turn[1], normed, terms, None, placing(is_early))
    fresh, rollout, rest = together(fresh, rollout, rest)
    fresh, rollout = project(turn[1], normed, terms_of(1, rest, (INNER, RELAYED)), fresh, placing(is_early), rollout)
    result = attended(1, moved[0], fresh, result)

    terms = terms_of(0, own, everything) + terms_of(1, rest, everything)
    moved, last = together(both(hop(result, 2), 2), last)
    last[RELAYED], last[INNER] = relayed(late, last), across(late, last)
    result = attended(2, moved[0], project(turn[2], prepared(moved), terms), result)
    moved = both(hop(result, 3), 3)
    normed = prepared(moved)
    fresh, rollout = project(turn[3], normed, terms_of(2, last, (0, 1, 2), shift), None, placing(1 - is_early), rollout)
    fresh, rollout, last = together(fresh, rollout, last)
    fresh, rollout = project(turn[3], normed, terms_of(2, last, (INNER, RELAYED)), fresh, placing(1 - is_early), rollout)
    result = attended(3, moved[0], fresh, result)
    return (rollout[None], result[None, None])


def solution(mesh):
    placed = (
        P(None, "dp", "tensor"),
        P("section", "tensor"),
        P("section", ("tensor", "dp"), None),
        P("section", None, "dp", "tensor"),
        P("section", None, "dp", None, "tensor"),
        P(None, "dp"),
    )
    return jax.shard_map(
        body,
        mesh=mesh,
        in_specs=placed,
        out_specs=(P("section", None, "tensor"), P("section", None, "dp", "tensor")),
        check_vma=False,
    )
```

```python
import functools

import jax
import jax.numpy as jnp
from jax import lax
from jax.experimental import pallas as pl
from jax.experimental.pallas import tpu as pltpu
from jax.sharding import PartitionSpec as P

D = 16384
KVH = 8
HD = 128
GQ = 16
GROUP = 128
LMAX = 16
HALF = GQ // 2
PAIR = 2 * HD
ROW_TILE = 16

epsilon = 1e-05
clip_ratio = 2.0
INNER, RELAYED = 4, 5
FIXED = 4
VMEM = 60 << 20
SHORT = pl.CostEstimate(flops=0, bytes_accessed=0, transcendentals=0)


def requantize_kernel(column_ref, w_ref, o_ref):
    ones = jnp.ones((ROW_TILE, GROUP), jnp.bfloat16)
    for start in range(0, w_ref.shape[0], GROUP):
        block = w_ref[start : start + GROUP, :]
        total = jnp.dot(ones, jnp.abs(block), preferred_element_type=jnp.float32)[:1]
        limit = (total * (clip_ratio / GROUP)).astype(jnp.bfloat16)
        o_ref[start : start + GROUP, :] = jnp.minimum(jnp.maximum(block, -limit), limit)


def requantize(weight, indices, own_width, width):
    rows = weight.shape[0]
    tile = min(rows, 4 * GROUP)
    return [
        pl.pallas_call(
            requantize_kernel,
            out_shape=jax.ShapeDtypeStruct((rows, width), jnp.bfloat16),
            grid_spec=pltpu.PrefetchScalarGridSpec(
                num_scalar_prefetch=1,
                grid=(rows // tile,),
                in_specs=[pl.BlockSpec((tile, width), lambda i, column: (i, column[0]))],
                out_specs=pl.BlockSpec((tile, width), lambda i, column: (i, 0)),
            ),
            compiler_params=pltpu.CompilerParams(vmem_limit_bytes=VMEM),
            cost_estimate=SHORT,
        )((index * own_width // width).reshape(1), weight)
        for index in indices
    ]


def project_kernel(layout, lhs_count, has_total, has_held, placed, where_ref, *refs):
    lhs = refs[:lhs_count]
    blocks = refs[lhs_count : lhs_count + len(layout)]
    rest = list(refs[lhs_count + len(layout) :])
    total_ref = rest.pop(0) if has_total else None
    if has_held:
        rest.pop(0)
    o_ref = rest.pop(0)
    segments = [(n, *segment) for n, (_, of_block) in enumerate(layout) for segment in of_block]

    def copy(i):
        n, _, start, depth = segments[i]
        out, sems = rest
        width = min(out.shape[1], o_ref.shape[1])
        rows = pl.ds(pl.multiple_of(where_ref[FIXED + len(layout) + 2 * i + 1], GROUP), depth)
        columns = pl.ds(pl.multiple_of(pl.program_id(0) * width, HD), width)
        source = blocks[n].at[pl.ds(start, depth)]
        if width < blocks[n].shape[1]:
            source = blocks[n].at[pl.ds(start, depth), pl.ds(pl.multiple_of(where_ref[2], HD), width)]
        return pltpu.make_async_copy(source, out.at[rows, columns], sems.at[i])

    def add(which):
        total = o_ref[...]
        for i in which:
            n, j, start, depth = segments[i]
            columns = pl.ds(pl.multiple_of(where_ref[FIXED + len(layout) + 2 * i], GROUP), depth)
            rows = blocks[n][start : start + depth, :]
            total += jnp.dot(lhs[j][:, columns], rows, preferred_element_type=jnp.float32)
        o_ref[...] = total

    def start(which):
        for i in which:
            copy(i).start()

    def wait(which):
        for i in which:
            copy(i).wait()

    groups = [(None, [i for i, segment in enumerate(segments) if not layout[segment[0]][0]])]
    for n, (gated, _) in enumerate(layout):
        if gated:
            groups.append((n, [i for i, segment in enumerate(segments) if segment[0] == n]))

    for n, which in groups:
        has = 1 if n is None else where_ref[FIXED + n]

        if placed and which:
            pl.when(where_ref[1] * has == 1)(functools.partial(start, which))

    o_ref[...] = total_ref[...] if has_total else jnp.zeros(o_ref.shape, jnp.float32)
    for n, which in groups:
        if which:
            has = 1 if n is None else where_ref[FIXED + n]
            pl.when(where_ref[0] * has == 1)(functools.partial(add, which))

    for n, which in groups:
        has = 1 if n is None else where_ref[FIXED + n]

        if placed and which:
            pl.when(where_ref[1] * has == 1)(functools.partial(wait, which))


def project(active, lhs, terms, total=None, placing=None, rollout=None):
    used = sorted({segment[0] for _, _, segments in terms for segment in segments})
    lhs = [lhs[j] for j in used]
    rows = lhs[0].shape[0]
    served = terms[0][0].shape[1]
    tile = min(served, 256)
    places, first_column, width = placing or (0, 0, 0)
    where = [active, places, first_column, active | places]
    where += [1 if has is None else has for _, has, _ in terms]
    for _, _, segments in terms:
        for _, offset, row, _, _ in segments:
            where += [offset, row]
    layout = [
        (has is not None, [(used.index(j), start, depth) for j, _, _, start, depth in segments])
        for _, has, segments in terms
    ]
    count = sum(len(segments) for _, segments in layout)
    added = () if total is None else (total,)
    held = () if rollout is None else (rollout,)
    column = lambda i, where: (0, i)

    def read(n):
        return lambda i, where: (0, i * where[3] * where[FIXED + n])

    anywhere = pl.BlockSpec(memory_space=pl.ANY)
    fresh_shape, fresh_spec = jax.ShapeDtypeStruct((rows, served), jnp.float32), pl.BlockSpec((rows, tile), column)
    placed = int(placing is not None)
    return pl.pallas_call(
        functools.partial(project_kernel, layout, len(lhs), bool(added), bool(held), placed),
        out_shape=[fresh_shape, jax.ShapeDtypeStruct((D, width), jnp.bfloat16)] if placing else fresh_shape,
        grid_spec=pltpu.PrefetchScalarGridSpec(
            num_scalar_prefetch=1,
            grid=(served // tile,),
            in_specs=[pl.BlockSpec(part.shape, lambda i, where: (0, 0)) for part in lhs]
            + [pl.BlockSpec((term[0].shape[0], tile), read(n)) for n, term in enumerate(terms)]
            + [fresh_spec for _ in added]
            + [anywhere for _ in held],
            out_specs=[fresh_spec, anywhere] if placing else fresh_spec,
            scratch_shapes=[pltpu.SemaphoreType.DMA((count,))] if placing else [],
        ),
        input_output_aliases={1 + len(lhs) + len(terms) + len(added): 1} if held else {},
        compiler_params=pltpu.CompilerParams(vmem_limit_bytes=VMEM),
        cost_estimate=SHORT,
    )(jnp.stack([jnp.asarray(v, jnp.int32) for v in where]), *lhs, *[term[0] for term in terms], *added, *held)


def attend_kernel(share, active_ref, bias_ref, x_ref, q_ref, c_ref, f_ref, held_ref, o_ref):
    heads = share * HALF
    scale = HD ** (-0.5)

    @pl.when((active_ref[0] == 0) & (pl.program_id(0) == 0))
    def _():
        o_ref[...] = held_ref[...]

    @pl.when(active_ref[0] == 1)
    def _():
        bias = jnp.concatenate([bias_ref[0]] * heads, axis=0)
        for g in range(q_ref.shape[1] // (heads * HD)):
            lanes = [slice((g * heads + i) * HD, (g * heads + i + 1) * HD) for i in range(heads)]
            query = jnp.concatenate([q_ref[:, lane] for lane in lanes], axis=0)
            at = g * share * PAIR
            keys = c_ref[:, :, at : at + HD].reshape(ROW_TILE * LMAX, HD)
            values = c_ref[:, :, at + HD : at + PAIR].reshape(ROW_TILE * LMAX, HD)
            fresh = f_ref[:, g * PAIR : (g + 1) * PAIR].astype(jnp.bfloat16).astype(jnp.float32)
            new_key = jnp.concatenate([fresh[:, :HD]] * heads, axis=0)
            new_value = jnp.concatenate([fresh[:, HD:]] * heads, axis=0)
            old = lax.dot_general(query, keys, (((1,), (1,)), ((), ())), preferred_element_type=jnp.float32)
            old = old * scale + bias
            new = jnp.sum(query.astype(jnp.float32) * new_key, axis=1, keepdims=True) * scale
            highest = jnp.maximum(jnp.max(old, axis=1, keepdims=True), new)
            old = jnp.exp(old - highest)
            new = jnp.exp(new - highest)
            inverse = 1.0 / (jnp.sum(old, axis=1, keepdims=True) + new)
            old = (old * inverse).astype(jnp.bfloat16)
            new = (new * inverse).astype(jnp.bfloat16).astype(jnp.float32)
            mixed = jnp.dot(old, values, preferred_element_type=jnp.float32) + new * new_value
            for i, lane in enumerate(lanes):
                total = x_ref[:, lane].astype(jnp.float32) + mixed[i * ROW_TILE : (i + 1) * ROW_TILE, :]
                o_ref[:, lane] = total.astype(jnp.bfloat16)


def seen_bias(lengths):
    column = jnp.arange(ROW_TILE * LMAX)
    own = jnp.arange(ROW_TILE)[:, None] == column[None, :] // LMAX
    seen = own[None] & ((column % LMAX)[None, None, :] < lengths.reshape(-1, ROW_TILE, 1))
    return jnp.where(seen, 0.0, -jnp.inf).astype(jnp.float32)


def attend(active, current, query, cache, bias, fresh, held):
    rows, width = query.shape
    share = min(2, width // (HALF * HD))
    wide = pl.BlockSpec((ROW_TILE, width), lambda i, active: (i * active[0], 0))
    return pl.pallas_call(
        functools.partial(attend_kernel, share),
        out_shape=jax.ShapeDtypeStruct((rows, width), jnp.bfloat16),
        grid_spec=pltpu.PrefetchScalarGridSpec(
            num_scalar_prefetch=1,
            grid=(rows // ROW_TILE,),
            in_specs=[
                pl.BlockSpec((1, *bias.shape[1:]), lambda i, active: (i * active[0], 0, 0)),
                wide,
                wide,
                pl.BlockSpec((ROW_TILE, LMAX, cache.shape[2]), lambda i, active: (i * active[0], 0, 0)),
                pl.BlockSpec((ROW_TILE, fresh.shape[1]), lambda i, active: (i * active[0], 0)),
                pl.BlockSpec((ROW_TILE, width), lambda i, active: (0, 0)),
            ],
            out_specs=wide,
        ),
        input_output_aliases={6: 0},
        compiler_params=pltpu.CompilerParams(vmem_limit_bytes=VMEM),
        cost_estimate=SHORT,
    )(active.reshape(1), bias, current, query, cache, fresh, held)


def together(*values):
    return lax.optimization_barrier(values)


def body(hidden_in, norm_gain, trainer_kv, queries, kv_cache, cache_lengths):
    sections, tensors, dps = (lax.axis_size(axis) for axis in ("section", "tensor", "dp"))
    section, tensor, dp = (lax.axis_index(axis) for axis in ("section", "tensor", "dp"))
    rows = hidden_in.shape[1]
    depth = trainer_kv.shape[1]
    own_width = 2 * KVH * HD // tensors
    served = max(own_width, PAIR)
    early, late = (1, 2), (0, 3)
    everyone = tuple(range(sections))
    is_early = ((section == 1) | (section == 2)).astype(jnp.int32)
    inner = ((dp == 1) | (dp == 2)).astype(jnp.int32)

    def over(axis, count, value, routes):
        pairs = [(a * count + i, b * count + j) for a, b, i, j in routes]
        return lax.ppermute(value, ("section", axis), pairs)

    def over_dp(value, at, target):
        return over("dp", dps, value, [(s, s, z, target[z]) for s in at for z in range(dps)])

    def over_tensor(value, at, flip, step=0):
        return over("tensor", tensors, value, [(s, s + step, t, t ^ flip) for s in at for t in range(tensors)])

    def flipped(b):
        return [z ^ b for z in range(dps)]

    def feature_block(value, b):
        return lax.dynamic_slice_in_dim(value, (dp ^ b) * depth, depth, 1)

    def normed_of(parts, inverse, gains):
        return [
            (part.astype(jnp.float32) * inverse[:, None] * gain.astype(jnp.float32)).astype(jnp.bfloat16)
            for part, gain in zip(parts, gains)
        ]

    def square_sum(part):
        wide = part.astype(jnp.float32)
        return jnp.sum(wide * wide, axis=1)

    bias = seen_bias(cache_lengths[0])
    turn = [(section == tick).astype(jnp.int32) for tick in range(sections)]

    def attended(tick, current, fresh, held):
        return attend(turn[tick], current, queries[0, 0], kv_cache[0, 0], bias, fresh, held)

    def hop(value, tick):
        return over_tensor(value, (tick - 1,), 0, 1)

    def both(part, tick):
        return [part] + [over_tensor(part, (tick,), j) for j in range(1, tensors)]

    def prepared(parts):
        inverse = lax.rsqrt(sum(square_sum(part) for part in parts) / D + epsilon)
        return normed_of(parts, inverse, gains)

    halves = [[(0, 0)], [(j, (j - 1) * depth) for j in range(1, tensors)], [(j, j * depth) for j in range(tensors)]]

    def across(at, blocks):
        return over("dp", dps, blocks[0], [(s, s, a, b) for s in at for a, b in ((1, 2), (2, 1))])

    def relayed(at, blocks):
        return over("dp", dps, blocks[2], [(s, s, a, b) for s in at for a, b in ((2, 3), (1, 0))])

    def terms_of(half, blocks, which, shift=0):
        terms = []
        for name in which:
            b, has = {INNER: (3, inner), RELAYED: (3, 1 - inner)}.get(name, (name, None))
            source = dp ^ b
            terms.append((blocks[name], has, [
                (j, source * depth + shift, ((tensor ^ j) * dps + source) * depth, start, depth)
                for j, start in halves[half]
            ]))
        return terms

    everything = (0, 1, 2, INNER, RELAYED)

    def placing(active):
        return (active, tensor * own_width % served, own_width)

    weight, hidden, first_kept = together(trainer_kv[0], hidden_in[0], requantize(trainer_kv[0], [tensor], own_width, served))

    squares = square_sum(hidden)
    for j in (2**i for i in range(tensors.bit_length() - 1)):
        squares = squares + over_tensor(squares, (0,), j)
    (normed,) = normed_of([hidden], lax.rsqrt(squares / D + epsilon), [norm_gain])
    first = [feature_block(normed, b) for b in range(dps)]
    weight, first = together(weight, first)
    kept = first_kept + requantize(weight, [tensor ^ j for j in range(1, tensors)], own_width, served)
    first[1:] = [over_dp(first[b], (0,), flipped(b)) for b in range(1, dps)]
    first, gain = together(first, norm_gain)
    gains = [gain] + [over_tensor(gain, everyone, j) for j in range(1, tensors)]

    def others(at, kept):
        received = [over_tensor(kept[j], at, j) for j in range(1, tensors)]
        return received[0] if len(received) == 1 else jnp.concatenate(received, axis=0)

    own = {0: kept[0], 2: over_dp(kept[0], early, flipped(2)), 1: over_dp(kept[0], early, flipped(1))}

    lhs = [jnp.concatenate(first, axis=0)]
    partial = [project(turn[0], lhs, [(kept[j], None, [(0, 0, 0, 0, depth)])]) for j in range(tensors)]
    partial, kept, gains = together(partial, kept, gains)
    rest = {0: others(early, kept)}
    total = partial[0]
    for j in range(1, tensors):
        total = total + over_tensor(partial[j].astype(jnp.bfloat16), (0,), j).astype(jnp.float32)
    total = total.reshape(dps, rows, served)
    step = 1
    while step < dps:
        send = jnp.stack([total[b] for b in range(total.shape[0]) if b & 1]).astype(jnp.bfloat16)
        keep = jnp.stack([total[b] for b in range(total.shape[0]) if not b & 1])
        total = keep + over_dp(send, (0,), flipped(step)).astype(jnp.float32)
        step *= 2
    fresh = total[0]
    result = attended(0, hidden, fresh, hidden)

    rest[2], rest[1] = over_dp(rest[0], early, flipped(2)), over_dp(rest[0], early, flipped(1))
    own, result, kept = together(own, result, kept)
    parts = both(result, 0)
    late_rest = others(late, kept)
    kept_back, rest[0] = together(own, rest[0])
    own[INNER], own[RELAYED] = across(early, kept_back), relayed(early, kept_back)
    swapped = own.pop(INNER)
    own, rest = together(own, rest)
    own[INNER], rest = together(swapped, rest)
    rest[RELAYED], rest[INNER] = relayed(early, rest), across(early, rest)
    token = over("dp", dps, rest[2][:ROW_TILE, :HD], [(a, b, z, z) for a, b in ((1, 0), (2, 3)) for z in range(dps)])
    token, late_own, parts = together(token, kept[0], parts)
    whole = jnp.concatenate([late_own, late_rest], axis=0)
    shift = jnp.isnan(token[0, 0]).astype(jnp.int32)
    last = {0: whole, 2: over_dp(whole, late, flipped(2)), 1: over_dp(whole, late, flipped(1))}

    moved = [hop(part, 1) for part in parts]
    normed = prepared(moved)
    terms = terms_of(0, own, everything) + terms_of(1, rest, (0, 1, 2))
    fresh, rollout = project(turn[1], normed, terms, None, placing(is_early))
    swapped = rest.pop(INNER)
    fresh, rollout, rest = together(fresh, rollout, rest)
    fresh, rest[INNER] = together(fresh, swapped)
    fresh, rollout = project(turn[1], normed, terms_of(1, rest, (INNER, RELAYED)), fresh, placing(is_early), rollout)
    result = attended(1, moved[0], fresh, result)

    terms = terms_of(0, own, everything) + terms_of(1, rest, everything)
    moved = both(hop(result, 2), 2)
    result = attended(2, moved[0], project(turn[2], prepared(moved), terms), result)
    result, last = together(result, last)
    last[INNER], last[RELAYED] = across(late, last), relayed(late, last)
    moved = both(hop(result, 3), 3)
    normed = prepared(moved)
    fresh, rollout = project(turn[3], normed, terms_of(2, last, (0, 1, 2), shift), None, placing(1 - is_early), rollout)
    swapped = last.pop(INNER)
    fresh, rollout, last = together(fresh, rollout, last)
    fresh, last[INNER] = together(fresh, swapped)
    fresh, rollout = project(turn[3], normed, terms_of(2, last, (INNER, RELAYED)), fresh, placing(1 - is_early), rollout)
    result = attended(3, moved[0], fresh, result)
    return (rollout[None], result[None, None])


def solution(mesh):
    placed = (
        P(None, "dp", "tensor"),
        P("section", "tensor"),
        P("section", ("tensor", "dp"), None),
        P("section", None, "dp", "tensor"),
        P("section", None, "dp", None, "tensor"),
        P(None, "dp"),
    )
    return jax.shard_map(
        body,
        mesh=mesh,
        in_specs=placed,
        out_specs=(P("section", None, "tensor"), P("section", None, "dp", "tensor")),
        check_vma=False,
    )
```

```python
import functools

import jax
import jax.numpy as jnp
from jax import lax
from jax.experimental import pallas as pl
from jax.experimental.pallas import tpu as pltpu
from jax.sharding import PartitionSpec as P

D = 16384
KVH = 8
HD = 128
GQ = 16
GROUP = 128
LMAX = 16
HALF = GQ // 2
PAIR = 2 * HD
ROW_TILE = 16

epsilon = 1e-05
clip_ratio = 2.0
FIXED = 4
VMEM = 60 << 20
SHORT = pl.CostEstimate(flops=0, bytes_accessed=0, transcendentals=0)


def requantize_kernel(column_ref, w_ref, o_ref):
    ones = jnp.ones((ROW_TILE, GROUP), jnp.bfloat16)
    for start in range(0, w_ref.shape[0], GROUP):
        block = w_ref[start : start + GROUP, :]
        total = jnp.dot(ones, jnp.abs(block), preferred_element_type=jnp.float32)[:1]
        limit = (total * (clip_ratio / GROUP)).astype(jnp.bfloat16)
        o_ref[start : start + GROUP, :] = jnp.minimum(jnp.maximum(block, -limit), limit)


def requantize(weight, indices, own_width, width):
    rows = weight.shape[0]
    tile = min(rows, 4 * GROUP)
    return [
        pl.pallas_call(
            requantize_kernel,
            out_shape=jax.ShapeDtypeStruct((rows, width), jnp.bfloat16),
            grid_spec=pltpu.PrefetchScalarGridSpec(
                num_scalar_prefetch=1,
                grid=(rows // tile,),
                in_specs=[pl.BlockSpec((tile, width), lambda i, column: (i, column[0]))],
                out_specs=pl.BlockSpec((tile, width), lambda i, column: (i, 0)),
            ),
            compiler_params=pltpu.CompilerParams(vmem_limit_bytes=VMEM),
            cost_estimate=SHORT,
        )((index * own_width // width).reshape(1), weight)
        for index in indices
    ]


def project_kernel(layout, lhs_count, has_total, has_held, placed, where_ref, *refs):
    lhs = refs[:lhs_count]
    blocks = refs[lhs_count : lhs_count + len(layout)]
    rest = list(refs[lhs_count + len(layout) :])
    total_ref = rest.pop(0) if has_total else None
    if has_held:
        rest.pop(0)
    o_ref = rest.pop(0)
    segments = [(block, *segment) for block, of_block in zip(blocks, layout) for segment in of_block]

    def copies():
        out, sems = rest
        width = min(out.shape[1], o_ref.shape[1])
        for i, (block, _, start, depth) in enumerate(segments):
            rows = pl.ds(pl.multiple_of(where_ref[FIXED + 2 * i + 1], GROUP), depth)
            columns = pl.ds(pl.multiple_of(pl.program_id(0) * width, HD), width)
            source = block.at[pl.ds(start, depth)]
            if width < block.shape[1]:
                source = block.at[pl.ds(start, depth), pl.ds(pl.multiple_of(where_ref[2], HD), width)]
            yield pltpu.make_async_copy(source, out.at[rows, columns], sems.at[i])

    if placed:

        @pl.when(where_ref[1] == 1)
        def _():
            for copy in copies():
                copy.start()

    @pl.when(where_ref[0] == 1)
    def _():
        total = total_ref[...] if has_total else None
        for i, (block, j, start, depth) in enumerate(segments):
            columns = pl.ds(pl.multiple_of(where_ref[FIXED + 2 * i], GROUP), depth)
            term = jnp.dot(
                lhs[j][:, columns], block[start : start + depth, :], preferred_element_type=jnp.float32
            )
            total = term if total is None else total + term
        o_ref[...] = total

    @pl.when(where_ref[0] == 0)
    def _():
        o_ref[...] = jnp.zeros(o_ref.shape, jnp.float32)

    if placed:

        @pl.when(where_ref[1] == 1)
        def _():
            for copy in copies():
                copy.wait()


def project(active, lhs, terms, total=None, placing=None, rollout=None):
    used = sorted({segment[0] for _, segments in terms for segment in segments})
    lhs = [lhs[j] for j in used]
    rows = lhs[0].shape[0]
    served = terms[0][0].shape[1]
    tile = min(served, 256)
    places, first_column, width = placing or (0, 0, 0)
    where = [active, places, first_column, active | places]
    for _, segments in terms:
        for _, offset, row, _, _ in segments:
            where += [offset, row]
    layout = [[(used.index(j), start, depth) for j, _, _, start, depth in segments] for _, segments in terms]
    count = sum(len(segments) for segments in layout)
    added = () if total is None else (total,)
    held = () if rollout is None else (rollout,)
    column = lambda i, where: (0, i)
    read = lambda i, where: (0, i * where[3])
    anywhere = pl.BlockSpec(memory_space=pl.ANY)
    fresh_shape, fresh_spec = jax.ShapeDtypeStruct((rows, served), jnp.float32), pl.BlockSpec((rows, tile), column)
    return pl.pallas_call(
        functools.partial(project_kernel, layout, len(lhs), bool(added), bool(held), placing is not None),
        out_shape=[fresh_shape, jax.ShapeDtypeStruct((D, width), jnp.bfloat16)] if placing else fresh_shape,
        grid_spec=pltpu.PrefetchScalarGridSpec(
            num_scalar_prefetch=1,
            grid=(served // tile,),
            in_specs=[pl.BlockSpec(part.shape, lambda i, where: (0, 0)) for part in lhs]
            + [pl.BlockSpec((block.shape[0], tile), read) for block, _ in terms]
            + [fresh_spec for _ in added]
            + [anywhere for _ in held],
            out_specs=[fresh_spec, anywhere] if placing else fresh_spec,
            scratch_shapes=[pltpu.SemaphoreType.DMA((count,))] if placing else [],
        ),
        input_output_aliases={1 + len(lhs) + len(terms) + len(added): 1} if held else {},
        compiler_params=pltpu.CompilerParams(vmem_limit_bytes=VMEM),
        cost_estimate=SHORT,
    )(jnp.stack([jnp.asarray(v, jnp.int32) for v in where]), *lhs, *[block for block, _ in terms], *added, *held)


def attend_kernel(share, active_ref, bias_ref, x_ref, q_ref, c_ref, f_ref, held_ref, o_ref):
    heads = share * HALF
    scale = HD ** (-0.5)

    @pl.when((active_ref[0] == 0) & (pl.program_id(0) == 0))
    def _():
        o_ref[...] = held_ref[...]

    @pl.when(active_ref[0] == 1)
    def _():
        bias = jnp.concatenate([bias_ref[0]] * heads, axis=0)
        for g in range(q_ref.shape[1] // (heads * HD)):
            lanes = [slice((g * heads + i) * HD, (g * heads + i + 1) * HD) for i in range(heads)]
            query = jnp.concatenate([q_ref[:, lane] for lane in lanes], axis=0)
            at = g * share * PAIR
            keys = c_ref[:, :, at : at + HD].reshape(ROW_TILE * LMAX, HD)
            values = c_ref[:, :, at + HD : at + PAIR].reshape(ROW_TILE * LMAX, HD)
            fresh = f_ref[:, g * PAIR : (g + 1) * PAIR].astype(jnp.bfloat16).astype(jnp.float32)
            new_key = jnp.concatenate([fresh[:, :HD]] * heads, axis=0)
            new_value = jnp.concatenate([fresh[:, HD:]] * heads, axis=0)
            old = lax.dot_general(query, keys, (((1,), (1,)), ((), ())), preferred_element_type=jnp.float32)
            old = old * scale + bias
            new = jnp.sum(query.astype(jnp.float32) * new_key, axis=1, keepdims=True) * scale
            highest = jnp.maximum(jnp.max(old, axis=1, keepdims=True), new)
            old = jnp.exp(old - highest)
            new = jnp.exp(new - highest)
            inverse = 1.0 / (jnp.sum(old, axis=1, keepdims=True) + new)
            old = (old * inverse).astype(jnp.bfloat16)
            new = (new * inverse).astype(jnp.bfloat16).astype(jnp.float32)
            mixed = jnp.dot(old, values, preferred_element_type=jnp.float32) + new * new_value
            for i, lane in enumerate(lanes):
                total = x_ref[:, lane].astype(jnp.float32) + mixed[i * ROW_TILE : (i + 1) * ROW_TILE, :]
                o_ref[:, lane] = total.astype(jnp.bfloat16)


def seen_bias(lengths):
    column = jnp.arange(ROW_TILE * LMAX)
    own = jnp.arange(ROW_TILE)[:, None] == column[None, :] // LMAX
    seen = own[None] & ((column % LMAX)[None, None, :] < lengths.reshape(-1, ROW_TILE, 1))
    return jnp.where(seen, 0.0, -jnp.inf).astype(jnp.float32)


def attend(active, current, query, cache, bias, fresh, held):
    rows, width = query.shape
    share = min(2, width // (HALF * HD))
    wide = pl.BlockSpec((ROW_TILE, width), lambda i, active: (i * active[0], 0))
    return pl.pallas_call(
        functools.partial(attend_kernel, share),
        out_shape=jax.ShapeDtypeStruct((rows, width), jnp.bfloat16),
        grid_spec=pltpu.PrefetchScalarGridSpec(
            num_scalar_prefetch=1,
            grid=(rows // ROW_TILE,),
            in_specs=[
                pl.BlockSpec((1, *bias.shape[1:]), lambda i, active: (i * active[0], 0, 0)),
                wide,
                wide,
                pl.BlockSpec((ROW_TILE, LMAX, cache.shape[2]), lambda i, active: (i * active[0], 0, 0)),
                pl.BlockSpec((ROW_TILE, fresh.shape[1]), lambda i, active: (i * active[0], 0)),
                pl.BlockSpec((ROW_TILE, width), lambda i, active: (0, 0)),
            ],
            out_specs=wide,
        ),
        input_output_aliases={6: 0},
        compiler_params=pltpu.CompilerParams(vmem_limit_bytes=VMEM),
        cost_estimate=SHORT,
    )(active.reshape(1), bias, current, query, cache, fresh, held)


def together(*values):
    return lax.optimization_barrier(values)


def body(hidden_in, norm_gain, trainer_kv, queries, kv_cache, cache_lengths):
    sections, tensors, dps = (lax.axis_size(axis) for axis in ("section", "tensor", "dp"))
    section, tensor, dp = (lax.axis_index(axis) for axis in ("section", "tensor", "dp"))
    rows = hidden_in.shape[1]
    depth = trainer_kv.shape[1]
    own_width = 2 * KVH * HD // tensors
    served = max(own_width, PAIR)
    early, late = (1, 2), (0, 3)
    everyone = tuple(range(sections))
    is_early = ((section == 1) | (section == 2)).astype(jnp.int32)

    def over(axis, count, value, routes):
        pairs = [(a * count + i, b * count + j) for a, b, i, j in routes]
        return lax.ppermute(value, ("section", axis), pairs)

    def over_dp(value, at, target):
        return over("dp", dps, value, [(s, s, z, target[z]) for s in at for z in range(dps)])

    def over_tensor(value, at, flip, step=0):
        return over("tensor", tensors, value, [(s, s + step, t, t ^ flip) for s in at for t in range(tensors)])

    def flipped(b):
        return [z ^ b for z in range(dps)]

    def feature_block(value, b):
        return lax.dynamic_slice_in_dim(value, (dp ^ b) * depth, depth, 1)

    def normed_of(parts, inverse, gains):
        return [
            (part.astype(jnp.float32) * inverse[:, None] * gain.astype(jnp.float32)).astype(jnp.bfloat16)
            for part, gain in zip(parts, gains)
        ]

    def square_sum(part):
        wide = part.astype(jnp.float32)
        return jnp.sum(wide * wide, axis=1)

    bias = seen_bias(cache_lengths[0])
    turn = [(section == tick).astype(jnp.int32) for tick in range(sections)]

    def attended(tick, current, fresh, held):
        return attend(turn[tick], current, queries[0, 0], kv_cache[0, 0], bias, fresh, held)

    def hop(value, tick):
        return over_tensor(value, (tick - 1,), 0, 1)

    def both(part, tick):
        return [part] + [over_tensor(part, (tick,), j) for j in range(1, tensors)]

    def prepared(parts):
        inverse = lax.rsqrt(sum(square_sum(part) for part in parts) / D + epsilon)
        return normed_of(parts, inverse, gains)

    halves = [[(0, 0)], [(j, (j - 1) * depth) for j in range(1, tensors)], [(j, j * depth) for j in range(tensors)]]

    def straight(at, block):
        return {0: block, 2: over_dp(block, at, flipped(2)), 1: over_dp(block, at, flipped(1))}

    def handed_on(at, blocks):
        return over_dp(blocks[2], at, flipped(1))

    def terms_of(half, blocks, which, shift=0):
        terms = []
        for b in which:
            source = dp ^ b
            terms.append((blocks[b], [
                (j, source * depth + shift, ((tensor ^ j) * dps + source) * depth, start, depth)
                for j, start in halves[half]
            ]))
        return terms

    def placing(active):
        return (active, tensor * own_width % served, own_width)

    weight, hidden, first_kept = together(trainer_kv[0], hidden_in[0], requantize(trainer_kv[0], [tensor], own_width, served))

    squares = square_sum(hidden)
    for j in (2**i for i in range(tensors.bit_length() - 1)):
        squares = squares + over_tensor(squares, (0,), j)
    (normed,) = normed_of([hidden], lax.rsqrt(squares / D + epsilon), [norm_gain])
    first = [feature_block(normed, b) for b in range(dps)]
    weight, first = together(weight, first)
    kept = first_kept + requantize(weight, [tensor ^ j for j in range(1, tensors)], own_width, served)
    first[1:] = [over_dp(first[b], (0,), flipped(b)) for b in range(1, dps)]
    first, gain = together(first, norm_gain)
    gains = [gain] + [over_tensor(gain, everyone, j) for j in range(1, tensors)]

    def others(at, kept):
        received = [over_tensor(kept[j], at, j) for j in range(1, tensors)]
        return received[0] if len(received) == 1 else jnp.concatenate(received, axis=0)

    own = straight(early, kept[0])

    lhs = [jnp.concatenate(first, axis=0)]
    partial = [project(turn[0], lhs, [(kept[j], [(0, 0, 0, 0, depth)])]) for j in range(tensors)]
    partial, kept, gains = together(partial, kept, gains)
    rest = others(early, kept)
    total = partial[0]
    for j in range(1, tensors):
        total = total + over_tensor(partial[j].astype(jnp.bfloat16), (0,), j).astype(jnp.float32)
    total = total.reshape(dps, rows, served)
    step = 1
    while step < dps:
        send = jnp.stack([total[b] for b in range(total.shape[0]) if b & 1]).astype(jnp.bfloat16)
        keep = jnp.stack([total[b] for b in range(total.shape[0]) if not b & 1])
        total = keep + over_dp(send, (0,), flipped(step)).astype(jnp.float32)
        step *= 2
    fresh = total[0]
    result = attended(0, hidden, fresh, hidden)

    rest = straight(early, rest)
    own, result, kept = together(own, result, kept)
    parts = both(result, 0)
    late_rest = others(late, kept)
    own[3] = handed_on(early, own)
    own, rest = together(own, rest)
    rest[3] = handed_on(early, rest)
    token = over("dp", dps, rest[2][:ROW_TILE, :HD], [(a, b, z, z) for a, b in ((1, 0), (2, 3)) for z in range(dps)])
    token, late_own, parts = together(token, kept[0], parts)
    whole = jnp.concatenate([late_own, late_rest], axis=0)
    shift = jnp.isnan(token[0, 0]).astype(jnp.int32)
    last = straight(late, whole)

    moved = [hop(part, 1) for part in parts]
    normed = prepared(moved)
    terms = terms_of(0, own, range(dps)) + terms_of(1, rest, (0, 1, 2))
    fresh, rollout = project(turn[1], normed, terms, None, placing(is_early))
    fresh, rollout, rest = together(fresh, rollout, rest)
    fresh, rollout = project(turn[1], normed, terms_of(1, rest, (3,)), fresh, placing(is_early), rollout)
    result = attended(1, moved[0], fresh, result)

    terms = terms_of(0, own, range(dps)) + terms_of(1, rest, range(dps))
    moved = both(hop(result, 2), 2)
    result = attended(2, moved[0], project(turn[2], prepared(moved), terms), result)
    result, last = together(result, last)
    last[3] = handed_on(late, last)
    moved = both(hop(result, 3), 3)
    normed = prepared(moved)
    fresh, rollout = project(turn[3], normed, terms_of(2, last, (0, 1, 2), shift), None, placing(1 - is_early), rollout)
    fresh, rollout, last = together(fresh, rollout, last)
    fresh, rollout = project(turn[3], normed, terms_of(2, last, (3,)), fresh, placing(1 - is_early), rollout)
    result = attended(3, moved[0], fresh, result)
    return (rollout[None], result[None, None])


def solution(mesh):
    placed = (
        P(None, "dp", "tensor"),
        P("section", "tensor"),
        P("section", ("tensor", "dp"), None),
        P("section", None, "dp", "tensor"),
        P("section", None, "dp", None, "tensor"),
        P(None, "dp"),
    )
    return jax.shard_map(
        body,
        mesh=mesh,
        in_specs=placed,
        out_specs=(P("section", None, "tensor"), P("section", None, "dp", "tensor")),
        check_vma=False,
    )
```

```python
import functools

import jax
import jax.numpy as jnp
from jax import lax
from jax.experimental import pallas as pl
from jax.experimental.pallas import tpu as pltpu
from jax.sharding import PartitionSpec as P

D = 16384
KVH = 8
HD = 128
GQ = 16
GROUP = 128
LMAX = 16
HALF = GQ // 2
PAIR = 2 * HD
ROW_TILE = 16

epsilon = 1e-05
clip_ratio = 2.0
FIXED = 4
VMEM = 60 << 20
SHORT = pl.CostEstimate(flops=0, bytes_accessed=0, transcendentals=0)


def requantize_kernel(column_ref, w_ref, o_ref):
    ones = jnp.ones((ROW_TILE, GROUP), jnp.bfloat16)
    for start in range(0, w_ref.shape[0], GROUP):
        block = w_ref[start : start + GROUP, :]
        total = jnp.dot(ones, jnp.abs(block), preferred_element_type=jnp.float32)[:1]
        limit = (total * (clip_ratio / GROUP)).astype(jnp.bfloat16)
        o_ref[start : start + GROUP, :] = jnp.minimum(jnp.maximum(block, -limit), limit)


def requantize(weight, indices, own_width, width):
    rows = weight.shape[0]
    tile = min(rows, 4 * GROUP)
    return [
        pl.pallas_call(
            requantize_kernel,
            out_shape=jax.ShapeDtypeStruct((rows, width), jnp.bfloat16),
            grid_spec=pltpu.PrefetchScalarGridSpec(
                num_scalar_prefetch=1,
                grid=(rows // tile,),
                in_specs=[pl.BlockSpec((tile, width), lambda i, column: (i, column[0]))],
                out_specs=pl.BlockSpec((tile, width), lambda i, column: (i, 0)),
            ),
            compiler_params=pltpu.CompilerParams(vmem_limit_bytes=VMEM),
            cost_estimate=SHORT,
        )((index * own_width // width).reshape(1), weight)
        for index in indices
    ]


def project_kernel(layout, lhs_count, has_total, has_held, placed, where_ref, *refs):
    lhs = refs[:lhs_count]
    blocks = refs[lhs_count : lhs_count + len(layout)]
    rest = list(refs[lhs_count + len(layout) :])
    total_ref = rest.pop(0) if has_total else None
    if has_held:
        rest.pop(0)
    o_ref = rest.pop(0)
    segments = [(block, *segment) for block, of_block in zip(blocks, layout) for segment in of_block]

    def copies():
        out, sems = rest
        width = min(out.shape[1], o_ref.shape[1])
        for i, (block, _, start, depth) in enumerate(segments):
            rows = pl.ds(pl.multiple_of(where_ref[FIXED + 2 * i + 1], GROUP), depth)
            columns = pl.ds(pl.multiple_of(pl.program_id(0) * width, HD), width)
            source = block.at[pl.ds(start, depth)]
            if width < block.shape[1]:
                source = block.at[pl.ds(start, depth), pl.ds(pl.multiple_of(where_ref[2], HD), width)]
            yield pltpu.make_async_copy(source, out.at[rows, columns], sems.at[i])

    if placed:

        @pl.when(where_ref[1] == 1)
        def _():
            for copy in copies():
                copy.start()

    @pl.when(where_ref[0] == 1)
    def _():
        total = total_ref[...] if has_total else None
        for i, (block, j, start, depth) in enumerate(segments):
            columns = pl.ds(pl.multiple_of(where_ref[FIXED + 2 * i], GROUP), depth)
            term = jnp.dot(
                lhs[j][:, columns], block[start : start + depth, :], preferred_element_type=jnp.float32
            )
            total = term if total is None else total + term
        o_ref[...] = total

    @pl.when(where_ref[0] == 0)
    def _():
        o_ref[...] = jnp.zeros(o_ref.shape, jnp.float32)

    if placed:

        @pl.when(where_ref[1] == 1)
        def _():
            for copy in copies():
                copy.wait()


def project(active, lhs, terms, total=None, placing=None, rollout=None):
    used = sorted({segment[0] for _, segments in terms for segment in segments})
    lhs = [lhs[j] for j in used]
    rows = lhs[0].shape[0]
    served = terms[0][0].shape[1]
    tile = min(served, 256)
    places, first_column, width = placing or (0, 0, 0)
    where = [active, places, first_column, active | places]
    for _, segments in terms:
        for _, offset, row, _, _ in segments:
            where += [offset, row]
    layout = [[(used.index(j), start, depth) for j, _, _, start, depth in segments] for _, segments in terms]
    count = sum(len(segments) for segments in layout)
    added = () if total is None else (total,)
    held = () if rollout is None else (rollout,)
    column = lambda i, where: (0, i)
    read = lambda i, where: (0, i * where[3])
    anywhere = pl.BlockSpec(memory_space=pl.ANY)
    fresh_shape, fresh_spec = jax.ShapeDtypeStruct((rows, served), jnp.float32), pl.BlockSpec((rows, tile), column)
    return pl.pallas_call(
        functools.partial(project_kernel, layout, len(lhs), bool(added), bool(held), placing is not None),
        out_shape=[fresh_shape, jax.ShapeDtypeStruct((D, width), jnp.bfloat16)] if placing else fresh_shape,
        grid_spec=pltpu.PrefetchScalarGridSpec(
            num_scalar_prefetch=1,
            grid=(served // tile,),
            in_specs=[pl.BlockSpec(part.shape, lambda i, where: (0, 0)) for part in lhs]
            + [pl.BlockSpec((block.shape[0], tile), read) for block, _ in terms]
            + [fresh_spec for _ in added]
            + [anywhere for _ in held],
            out_specs=[fresh_spec, anywhere] if placing else fresh_spec,
            scratch_shapes=[pltpu.SemaphoreType.DMA((count,))] if placing else [],
        ),
        input_output_aliases={1 + len(lhs) + len(terms) + len(added): 1} if held else {},
        compiler_params=pltpu.CompilerParams(vmem_limit_bytes=VMEM),
        cost_estimate=SHORT,
    )(jnp.stack([jnp.asarray(v, jnp.int32) for v in where]), *lhs, *[block for block, _ in terms], *added, *held)


def attend_kernel(share, active_ref, bias_ref, x_ref, q_ref, c_ref, f_ref, held_ref, o_ref):
    heads = share * HALF
    scale = HD ** (-0.5)

    @pl.when((active_ref[0] == 0) & (pl.program_id(0) == 0))
    def _():
        o_ref[...] = held_ref[...]

    @pl.when(active_ref[0] == 1)
    def _():
        bias = jnp.concatenate([bias_ref[0]] * heads, axis=0)
        for g in range(q_ref.shape[1] // (heads * HD)):
            lanes = [slice((g * heads + i) * HD, (g * heads + i + 1) * HD) for i in range(heads)]
            query = jnp.concatenate([q_ref[:, lane] for lane in lanes], axis=0)
            at = g * share * PAIR
            keys = c_ref[:, :, at : at + HD].reshape(ROW_TILE * LMAX, HD)
            values = c_ref[:, :, at + HD : at + PAIR].reshape(ROW_TILE * LMAX, HD)
            fresh = f_ref[:, g * PAIR : (g + 1) * PAIR].astype(jnp.bfloat16).astype(jnp.float32)
            new_key = jnp.concatenate([fresh[:, :HD]] * heads, axis=0)
            new_value = jnp.concatenate([fresh[:, HD:]] * heads, axis=0)
            old = lax.dot_general(query, keys, (((1,), (1,)), ((), ())), preferred_element_type=jnp.float32)
            old = old * scale + bias
            new = jnp.sum(query.astype(jnp.float32) * new_key, axis=1, keepdims=True) * scale
            highest = jnp.maximum(jnp.max(old, axis=1, keepdims=True), new)
            old = jnp.exp(old - highest)
            new = jnp.exp(new - highest)
            inverse = 1.0 / (jnp.sum(old, axis=1, keepdims=True) + new)
            old = (old * inverse).astype(jnp.bfloat16)
            new = (new * inverse).astype(jnp.bfloat16).astype(jnp.float32)
            mixed = jnp.dot(old, values, preferred_element_type=jnp.float32) + new * new_value
            for i, lane in enumerate(lanes):
                total = x_ref[:, lane].astype(jnp.float32) + mixed[i * ROW_TILE : (i + 1) * ROW_TILE, :]
                o_ref[:, lane] = total.astype(jnp.bfloat16)


def seen_bias(lengths):
    column = jnp.arange(ROW_TILE * LMAX)
    own = jnp.arange(ROW_TILE)[:, None] == column[None, :] // LMAX
    seen = own[None] & ((column % LMAX)[None, None, :] < lengths.reshape(-1, ROW_TILE, 1))
    return jnp.where(seen, 0.0, -jnp.inf).astype(jnp.float32)


def attend(active, current, query, cache, bias, fresh, held):
    rows, width = query.shape
    share = min(2, width // (HALF * HD))
    wide = pl.BlockSpec((ROW_TILE, width), lambda i, active: (i * active[0], 0))
    return pl.pallas_call(
        functools.partial(attend_kernel, share),
        out_shape=jax.ShapeDtypeStruct((rows, width), jnp.bfloat16),
        grid_spec=pltpu.PrefetchScalarGridSpec(
            num_scalar_prefetch=1,
            grid=(rows // ROW_TILE,),
            in_specs=[
                pl.BlockSpec((1, *bias.shape[1:]), lambda i, active: (i * active[0], 0, 0)),
                wide,
                wide,
                pl.BlockSpec((ROW_TILE, LMAX, cache.shape[2]), lambda i, active: (i * active[0], 0, 0)),
                pl.BlockSpec((ROW_TILE, fresh.shape[1]), lambda i, active: (i * active[0], 0)),
                pl.BlockSpec((ROW_TILE, width), lambda i, active: (0, 0)),
            ],
            out_specs=wide,
        ),
        input_output_aliases={6: 0},
        compiler_params=pltpu.CompilerParams(vmem_limit_bytes=VMEM),
        cost_estimate=SHORT,
    )(active.reshape(1), bias, current, query, cache, fresh, held)


def together(*values):
    return lax.optimization_barrier(values)


def body(hidden_in, norm_gain, trainer_kv, queries, kv_cache, cache_lengths):
    sections, tensors, dps = (lax.axis_size(axis) for axis in ("section", "tensor", "dp"))
    section, tensor, dp = (lax.axis_index(axis) for axis in ("section", "tensor", "dp"))
    rows = hidden_in.shape[1]
    depth = trainer_kv.shape[1]
    own_width = 2 * KVH * HD // tensors
    served = max(own_width, PAIR)
    early, late = (1, 2), (0, 3)
    everyone = tuple(range(sections))
    is_early = ((section == 1) | (section == 2)).astype(jnp.int32)

    def over(axis, count, value, routes):
        pairs = [(a * count + i, b * count + j) for a, b, i, j in routes]
        return lax.ppermute(value, ("section", axis), pairs)

    def over_dp(value, at, target):
        return over("dp", dps, value, [(s, s, z, target[z]) for s in at for z in range(dps)])

    def over_tensor(value, at, flip, step=0):
        return over("tensor", tensors, value, [(s, s + step, t, t ^ flip) for s in at for t in range(tensors)])

    def flipped(b):
        return [z ^ b for z in range(dps)]

    def feature_block(value, b):
        return lax.dynamic_slice_in_dim(value, (dp ^ b) * depth, depth, 1)

    def normed_of(parts, inverse, gains):
        return [
            (part.astype(jnp.float32) * inverse[:, None] * gain.astype(jnp.float32)).astype(jnp.bfloat16)
            for part, gain in zip(parts, gains)
        ]

    def square_sum(part):
        wide = part.astype(jnp.float32)
        return jnp.sum(wide * wide, axis=1)

    bias = seen_bias(cache_lengths[0])
    turn = [(section == tick).astype(jnp.int32) for tick in range(sections)]

    def attended(tick, current, fresh, held):
        return attend(turn[tick], current, queries[0, 0], kv_cache[0, 0], bias, fresh, held)

    def hop(value, tick):
        return over_tensor(value, (tick - 1,), 0, 1)

    def both(part, tick):
        return [part] + [over_tensor(part, (tick,), j) for j in range(1, tensors)]

    def prepared(parts):
        inverse = lax.rsqrt(sum(square_sum(part) for part in parts) / D + epsilon)
        return normed_of(parts, inverse, gains)

    halves = [[(0, 0)], [(j, (j - 1) * depth) for j in range(1, tensors)], [(j, j * depth) for j in range(tensors)]]

    def straight(at, block):
        return {0: block, 2: over_dp(block, at, flipped(2)), 1: over_dp(block, at, flipped(1))}

    def handed_on(at, blocks):
        return over_dp(blocks[2], at, flipped(1))

    def terms_of(half, blocks, which, shift=0):
        terms = []
        for b in which:
            source = dp ^ b
            terms.append((blocks[b], [
                (j, source * depth + shift, ((tensor ^ j) * dps + source) * depth, start, depth)
                for j, start in halves[half]
            ]))
        return terms

    def placing(active):
        return (active, tensor * own_width % served, own_width)

    weight, hidden, first_kept = together(trainer_kv[0], hidden_in[0], requantize(trainer_kv[0], [tensor], own_width, served))

    squares = square_sum(hidden)
    for j in (2**i for i in range(tensors.bit_length() - 1)):
        squares = squares + over_tensor(squares, (0,), j)
    (normed,) = normed_of([hidden], lax.rsqrt(squares / D + epsilon), [norm_gain])
    first = [feature_block(normed, b) for b in range(dps)]
    weight, first = together(weight, first)
    kept = first_kept + requantize(weight, [tensor ^ j for j in range(1, tensors)], own_width, served)
    first[1:] = [over_dp(first[b], (0,), flipped(b)) for b in range(1, dps)]
    first, gain = together(first, norm_gain)
    gains = [gain] + [over_tensor(gain, everyone, j) for j in range(1, tensors)]

    def others(at, kept):
        received = [over_tensor(kept[j], at, j) for j in range(1, tensors)]
        return received[0] if len(received) == 1 else jnp.concatenate(received, axis=0)

    own = straight(early, kept[0])

    lhs = [jnp.concatenate(first, axis=0)]
    partial = [project(turn[0], lhs, [(kept[j], [(0, 0, 0, 0, depth)])]) for j in range(tensors)]
    partial, kept, gains = together(partial, kept, gains)
    rest = others(early, kept)
    total = partial[0]
    for j in range(1, tensors):
        total = total + over_tensor(partial[j].astype(jnp.bfloat16), (0,), j).astype(jnp.float32)
    total = total.reshape(dps, rows, served)
    step = 1
    while step < dps:
        send = jnp.stack([total[b] for b in range(total.shape[0]) if b & 1]).astype(jnp.bfloat16)
        keep = jnp.stack([total[b] for b in range(total.shape[0]) if not b & 1])
        total = keep + over_dp(send, (0,), flipped(step)).astype(jnp.float32)
        step *= 2
    fresh = total[0]
    result = attended(0, hidden, fresh, hidden)

    rest = straight(early, rest)
    own, result, kept = together(own, result, kept)
    parts = both(result, 0)
    late_rest = others(late, kept)
    own[3] = handed_on(early, own)
    own, rest = together(own, rest)
    rest[3] = handed_on(early, rest)
    moved = [hop(part, 1) for part in parts]
    normed = prepared(moved)
    terms = terms_of(0, own, range(dps)) + terms_of(1, rest, (0, 1, 2))
    fresh, rollout = project(turn[1], normed, terms, None, placing(is_early))

    token, fresh = together(rest[2][:ROW_TILE, :HD], fresh)
    token = over("dp", dps, token, [(a, b, z, z) for a, b in ((1, 0), (2, 3)) for z in range(dps)])
    token, late_own, fresh = together(token, kept[0], fresh)
    whole = jnp.concatenate([late_own, late_rest], axis=0)
    shift = jnp.isnan(token[0, 0]).astype(jnp.int32)
    last = straight(late, whole)

    fresh, rollout, rest = together(fresh, rollout, rest)
    fresh, rollout = project(turn[1], normed, terms_of(1, rest, (3,)), fresh, placing(is_early), rollout)
    result = attended(1, moved[0], fresh, result)

    terms = terms_of(0, own, range(dps)) + terms_of(1, rest, range(dps))
    moved = both(hop(result, 2), 2)
    result = attended(2, moved[0], project(turn[2], prepared(moved), terms), result)
    result, last = together(result, last)
    last[3] = handed_on(late, last)
    moved = both(hop(result, 3), 3)
    normed = prepared(moved)
    fresh, rollout = project(turn[3], normed, terms_of(2, last, (0, 1, 2), shift), None, placing(1 - is_early), rollout)
    fresh, rollout, last = together(fresh, rollout, last)
    fresh, rollout = project(turn[3], normed, terms_of(2, last, (3,)), fresh, placing(1 - is_early), rollout)
    result = attended(3, moved[0], fresh, result)
    return (rollout[None], result[None, None])


def solution(mesh):
    placed = (
        P(None, "dp", "tensor"),
        P("section", "tensor"),
        P("section", ("tensor", "dp"), None),
        P("section", None, "dp", "tensor"),
        P("section", None, "dp", None, "tensor"),
        P(None, "dp"),
    )
    return jax.shard_map(
        body,
        mesh=mesh,
        in_specs=placed,
        out_specs=(P("section", None, "tensor"), P("section", None, "dp", "tensor")),
        check_vma=False,
    )
```

```python
import functools

import jax
import jax.numpy as jnp
from jax import lax
from jax.experimental import pallas as pl
from jax.experimental.pallas import tpu as pltpu
from jax.sharding import PartitionSpec as P

D = 16384
KVH = 8
HD = 128
GQ = 16
GROUP = 128
LMAX = 16
HALF = GQ // 2
PAIR = 2 * HD
ROW_TILE = 16

epsilon = 1e-05
clip_ratio = 2.0
FIXED = 4
VMEM = 60 << 20
SHORT = pl.CostEstimate(flops=0, bytes_accessed=0, transcendentals=0)


def requantize_kernel(column_ref, w_ref, o_ref):
    ones = jnp.ones((ROW_TILE, GROUP), jnp.bfloat16)
    for start in range(0, w_ref.shape[0], GROUP):
        block = w_ref[start : start + GROUP, :]
        total = jnp.dot(ones, jnp.abs(block), preferred_element_type=jnp.float32)[:1]
        limit = (total * (clip_ratio / GROUP)).astype(jnp.bfloat16)
        o_ref[start : start + GROUP, :] = jnp.minimum(jnp.maximum(block, -limit), limit)


def requantize(weight, indices, own_width, width):
    rows = weight.shape[0]
    tile = min(rows, 4 * GROUP)
    return [
        pl.pallas_call(
            requantize_kernel,
            out_shape=jax.ShapeDtypeStruct((rows, width), jnp.bfloat16),
            grid_spec=pltpu.PrefetchScalarGridSpec(
                num_scalar_prefetch=1,
                grid=(rows // tile,),
                in_specs=[pl.BlockSpec((tile, width), lambda i, column: (i, column[0]))],
                out_specs=pl.BlockSpec((tile, width), lambda i, column: (i, 0)),
            ),
            compiler_params=pltpu.CompilerParams(vmem_limit_bytes=VMEM),
            cost_estimate=SHORT,
        )((index * own_width // width).reshape(1), weight)
        for index in indices
    ]


def project_kernel(layout, lhs_count, has_total, has_held, placed, where_ref, *refs):
    lhs = refs[:lhs_count]
    blocks = refs[lhs_count : lhs_count + len(layout)]
    rest = list(refs[lhs_count + len(layout) :])
    total_ref = rest.pop(0) if has_total else None
    if has_held:
        rest.pop(0)
    o_ref = rest.pop(0)
    segments = [(block, *segment) for block, of_block in zip(blocks, layout) for segment in of_block]

    def copies():
        out, sems = rest
        width = min(out.shape[1], o_ref.shape[1])
        for i, (block, _, start, depth) in enumerate(segments):
            rows = pl.ds(pl.multiple_of(where_ref[FIXED + 2 * i + 1], GROUP), depth)
            columns = pl.ds(pl.multiple_of(pl.program_id(0) * width, HD), width)
            source = block.at[pl.ds(start, depth)]
            if width < block.shape[1]:
                source = block.at[pl.ds(start, depth), pl.ds(pl.multiple_of(where_ref[2], HD), width)]
            yield pltpu.make_async_copy(source, out.at[rows, columns], sems.at[i])

    if placed:

        @pl.when(where_ref[1] == 1)
        def _():
            for copy in copies():
                copy.start()

    @pl.when(where_ref[0] == 1)
    def _():
        total = total_ref[...] if has_total else None
        for i, (block, j, start, depth) in enumerate(segments):
            columns = pl.ds(pl.multiple_of(where_ref[FIXED + 2 * i], GROUP), depth)
            term = jnp.dot(
                lhs[j][:, columns], block[start : start + depth, :], preferred_element_type=jnp.float32
            )
            total = term if total is None else total + term
        o_ref[...] = total

    @pl.when(where_ref[0] == 0)
    def _():
        o_ref[...] = jnp.zeros(o_ref.shape, jnp.float32)

    if placed:

        @pl.when(where_ref[1] == 1)
        def _():
            for copy in copies():
                copy.wait()


def project(active, lhs, terms, total=None, placing=None, rollout=None):
    used = sorted({segment[0] for _, segments in terms for segment in segments})
    lhs = [lhs[j] for j in used]
    rows = lhs[0].shape[0]
    served = terms[0][0].shape[1]
    tile = min(served, 256)
    places, first_column, width = placing or (0, 0, 0)
    where = [active, places, first_column, active | places]
    for _, segments in terms:
        for _, offset, row, _, _ in segments:
            where += [offset, row]
    layout = [[(used.index(j), start, depth) for j, _, _, start, depth in segments] for _, segments in terms]
    count = sum(len(segments) for segments in layout)
    added = () if total is None else (total,)
    held = () if rollout is None else (rollout,)
    column = lambda i, where: (0, i)
    read = lambda i, where: (0, i * where[3])
    anywhere = pl.BlockSpec(memory_space=pl.ANY)
    fresh_shape, fresh_spec = jax.ShapeDtypeStruct((rows, served), jnp.float32), pl.BlockSpec((rows, tile), column)
    return pl.pallas_call(
        functools.partial(project_kernel, layout, len(lhs), bool(added), bool(held), placing is not None),
        out_shape=[fresh_shape, jax.ShapeDtypeStruct((D, width), jnp.bfloat16)] if placing else fresh_shape,
        grid_spec=pltpu.PrefetchScalarGridSpec(
            num_scalar_prefetch=1,
            grid=(served // tile,),
            in_specs=[pl.BlockSpec(part.shape, lambda i, where: (0, 0)) for part in lhs]
            + [pl.BlockSpec((block.shape[0], tile), read) for block, _ in terms]
            + [fresh_spec for _ in added]
            + [anywhere for _ in held],
            out_specs=[fresh_spec, anywhere] if placing else fresh_spec,
            scratch_shapes=[pltpu.SemaphoreType.DMA((count,))] if placing else [],
        ),
        input_output_aliases={1 + len(lhs) + len(terms) + len(added): 1} if held else {},
        compiler_params=pltpu.CompilerParams(vmem_limit_bytes=VMEM),
        cost_estimate=SHORT,
    )(jnp.stack([jnp.asarray(v, jnp.int32) for v in where]), *lhs, *[block for block, _ in terms], *added, *held)


def attend_kernel(share, active_ref, bias_ref, x_ref, q_ref, c_ref, f_ref, held_ref, o_ref):
    heads = share * HALF
    scale = HD ** (-0.5)

    @pl.when((active_ref[0] == 0) & (pl.program_id(0) == 0))
    def _():
        o_ref[...] = held_ref[...]

    @pl.when(active_ref[0] == 1)
    def _():
        bias = jnp.concatenate([bias_ref[0]] * heads, axis=0)
        for g in range(q_ref.shape[1] // (heads * HD)):
            lanes = [slice((g * heads + i) * HD, (g * heads + i + 1) * HD) for i in range(heads)]
            query = jnp.concatenate([q_ref[:, lane] for lane in lanes], axis=0)
            at = g * share * PAIR
            keys = c_ref[:, :, at : at + HD].reshape(ROW_TILE * LMAX, HD)
            values = c_ref[:, :, at + HD : at + PAIR].reshape(ROW_TILE * LMAX, HD)
            fresh = f_ref[:, g * PAIR : (g + 1) * PAIR].astype(jnp.bfloat16).astype(jnp.float32)
            new_key = jnp.concatenate([fresh[:, :HD]] * heads, axis=0)
            new_value = jnp.concatenate([fresh[:, HD:]] * heads, axis=0)
            old = lax.dot_general(query, keys, (((1,), (1,)), ((), ())), preferred_element_type=jnp.float32)
            old = old * scale + bias
            new = jnp.sum(query.astype(jnp.float32) * new_key, axis=1, keepdims=True) * scale
            highest = jnp.maximum(jnp.max(old, axis=1, keepdims=True), new)
            old = jnp.exp(old - highest)
            new = jnp.exp(new - highest)
            inverse = 1.0 / (jnp.sum(old, axis=1, keepdims=True) + new)
            old = (old * inverse).astype(jnp.bfloat16)
            new = (new * inverse).astype(jnp.bfloat16).astype(jnp.float32)
            mixed = jnp.dot(old, values, preferred_element_type=jnp.float32) + new * new_value
            for i, lane in enumerate(lanes):
                total = x_ref[:, lane].astype(jnp.float32) + mixed[i * ROW_TILE : (i + 1) * ROW_TILE, :]
                o_ref[:, lane] = total.astype(jnp.bfloat16)


def seen_bias(lengths):
    column = jnp.arange(ROW_TILE * LMAX)
    own = jnp.arange(ROW_TILE)[:, None] == column[None, :] // LMAX
    seen = own[None] & ((column % LMAX)[None, None, :] < lengths.reshape(-1, ROW_TILE, 1))
    return jnp.where(seen, 0.0, -jnp.inf).astype(jnp.float32)


def attend(active, current, query, cache, bias, fresh, held):
    rows, width = query.shape
    share = min(2, width // (HALF * HD))
    wide = pl.BlockSpec((ROW_TILE, width), lambda i, active: (i * active[0], 0))
    return pl.pallas_call(
        functools.partial(attend_kernel, share),
        out_shape=jax.ShapeDtypeStruct((rows, width), jnp.bfloat16),
        grid_spec=pltpu.PrefetchScalarGridSpec(
            num_scalar_prefetch=1,
            grid=(rows // ROW_TILE,),
            in_specs=[
                pl.BlockSpec((1, *bias.shape[1:]), lambda i, active: (i * active[0], 0, 0)),
                wide,
                wide,
                pl.BlockSpec((ROW_TILE, LMAX, cache.shape[2]), lambda i, active: (i * active[0], 0, 0)),
                pl.BlockSpec((ROW_TILE, fresh.shape[1]), lambda i, active: (i * active[0], 0)),
                pl.BlockSpec((ROW_TILE, width), lambda i, active: (0, 0)),
            ],
            out_specs=wide,
        ),
        input_output_aliases={6: 0},
        compiler_params=pltpu.CompilerParams(vmem_limit_bytes=VMEM),
        cost_estimate=SHORT,
    )(active.reshape(1), bias, current, query, cache, fresh, held)


def together(*values):
    return lax.optimization_barrier(values)


def body(hidden_in, norm_gain, trainer_kv, queries, kv_cache, cache_lengths):
    sections, tensors, dps = (lax.axis_size(axis) for axis in ("section", "tensor", "dp"))
    section, tensor, dp = (lax.axis_index(axis) for axis in ("section", "tensor", "dp"))
    rows = hidden_in.shape[1]
    depth = trainer_kv.shape[1]
    own_width = 2 * KVH * HD // tensors
    served = max(own_width, PAIR)
    early, late = (1, 2), (0, 3)
    everyone = tuple(range(sections))
    is_early = ((section == 1) | (section == 2)).astype(jnp.int32)

    def over(axis, count, value, routes):
        pairs = [(a * count + i, b * count + j) for a, b, i, j in routes]
        return lax.ppermute(value, ("section", axis), pairs)

    def over_dp(value, at, target):
        return over("dp", dps, value, [(s, s, z, target[z]) for s in at for z in range(dps)])

    def over_tensor(value, at, flip, step=0):
        return over("tensor", tensors, value, [(s, s + step, t, t ^ flip) for s in at for t in range(tensors)])

    def flipped(b):
        return [z ^ b for z in range(dps)]

    def feature_block(value, b):
        return lax.dynamic_slice_in_dim(value, (dp ^ b) * depth, depth, 1)

    def normed_of(parts, inverse, gains):
        return [
            (part.astype(jnp.float32) * inverse[:, None] * gain.astype(jnp.float32)).astype(jnp.bfloat16)
            for part, gain in zip(parts, gains)
        ]

    def square_sum(part):
        wide = part.astype(jnp.float32)
        return jnp.sum(wide * wide, axis=1)

    bias = seen_bias(cache_lengths[0])
    turn = [(section == tick).astype(jnp.int32) for tick in range(sections)]

    def attended(tick, current, fresh, held):
        return attend(turn[tick], current, queries[0, 0], kv_cache[0, 0], bias, fresh, held)

    def hop(value, tick):
        return over_tensor(value, (tick - 1,), 0, 1)

    def both(part, tick):
        return [part] + [over_tensor(part, (tick,), j) for j in range(1, tensors)]

    def prepared(parts):
        inverse = lax.rsqrt(sum(square_sum(part) for part in parts) / D + epsilon)
        return normed_of(parts, inverse, gains)

    halves = [[(0, 0)], [(j, (j - 1) * depth) for j in range(1, tensors)], [(j, j * depth) for j in range(tensors)]]

    def straight(at, block):
        return {0: block, 2: over_dp(block, at, flipped(2)), 1: over_dp(block, at, flipped(1))}

    def handed_on(at, blocks):
        return over_dp(blocks[2], at, flipped(1))

    def terms_of(half, blocks, which, shift=0):
        terms = []
        for b in which:
            source = dp ^ b
            terms.append((blocks[b], [
                (j, source * depth + shift, ((tensor ^ j) * dps + source) * depth, start, depth)
                for j, start in halves[half]
            ]))
        return terms

    def placing(active):
        return (active, tensor * own_width % served, own_width)

    weight, hidden, first_kept = together(trainer_kv[0], hidden_in[0], requantize(trainer_kv[0], [tensor], own_width, served))

    squares = square_sum(hidden)
    for j in (2**i for i in range(tensors.bit_length() - 1)):
        squares = squares + over_tensor(squares, (0,), j)
    (normed,) = normed_of([hidden], lax.rsqrt(squares / D + epsilon), [norm_gain])
    first = [feature_block(normed, b) for b in range(dps)]
    weight, first = together(weight, first)
    kept = first_kept + requantize(weight, [tensor ^ j for j in range(1, tensors)], own_width, served)
    first[1:] = [over_dp(first[b], (0,), flipped(b)) for b in range(1, dps)]
    first, gain = together(first, norm_gain)
    gains = [gain] + [over_tensor(gain, everyone, j) for j in range(1, tensors)]

    def others(at, kept):
        received = [over_tensor(kept[j], at, j) for j in range(1, tensors)]
        return received[0] if len(received) == 1 else jnp.concatenate(received, axis=0)

    own = {0: kept[0], 1: over_dp(kept[0], early, flipped(1))}
    later, kept[1:] = together(kept[0], kept[1:])
    own[2] = over_dp(later, early, flipped(2))

    lhs = [jnp.concatenate(first, axis=0)]
    partial = [project(turn[0], lhs, [(kept[j], [(0, 0, 0, 0, depth)])]) for j in range(tensors)]
    partial, kept, gains = together(partial, kept, gains)
    rest = others(early, kept)
    total = partial[0]
    for j in range(1, tensors):
        total = total + over_tensor(partial[j].astype(jnp.bfloat16), (0,), j).astype(jnp.float32)
    total = total.reshape(dps, rows, served)
    step = 1
    while step < dps:
        send = jnp.stack([total[b] for b in range(total.shape[0]) if b & 1]).astype(jnp.bfloat16)
        keep = jnp.stack([total[b] for b in range(total.shape[0]) if not b & 1])
        total = keep + over_dp(send, (0,), flipped(step)).astype(jnp.float32)
        step *= 2
    fresh = total[0]
    result = attended(0, hidden, fresh, hidden)

    rest = straight(early, rest)
    own[1], result = together(own[1], result)
    own, result, kept = together(own, result, kept)
    parts = both(result, 0)
    late_rest = others(late, kept)
    own[3] = handed_on(early, own)
    own, rest = together(own, rest)
    rest[3] = handed_on(early, rest)
    moved = [hop(part, 1) for part in parts]
    normed = prepared(moved)
    terms = terms_of(0, own, range(dps)) + terms_of(1, rest, (0, 1, 2))
    fresh, rollout = project(turn[1], normed, terms, None, placing(is_early))

    token, fresh = together(rest[2][:ROW_TILE, :HD], fresh)
    token = over("dp", dps, token, [(a, b, z, z) for a, b in ((1, 0), (2, 3)) for z in range(dps)])
    token, whole, fresh = together(token, jnp.concatenate([kept[0], late_rest], axis=0), fresh)
    shift = jnp.isnan(token[0, 0]).astype(jnp.int32)
    last = straight(late, whole)

    fresh, rollout, rest = together(fresh, rollout, rest)
    fresh, rollout = project(turn[1], normed, terms_of(1, rest, (3,)), fresh, placing(is_early), rollout)
    result = attended(1, moved[0], fresh, result)

    terms = terms_of(0, own, range(dps)) + terms_of(1, rest, range(dps))
    moved = both(hop(result, 2), 2)
    result = attended(2, moved[0], project(turn[2], prepared(moved), terms), result)
    result, last = together(result, last)
    last[3] = handed_on(late, last)
    moved = both(hop(result, 3), 3)
    normed = prepared(moved)
    fresh, rollout = project(turn[3], normed, terms_of(2, last, (0, 1, 2), shift), None, placing(1 - is_early), rollout)
    fresh, rollout, last = together(fresh, rollout, last)
    fresh, rollout = project(turn[3], normed, terms_of(2, last, (3,)), fresh, placing(1 - is_early), rollout)
    result = attended(3, moved[0], fresh, result)
    return (rollout[None], result[None, None])


def solution(mesh):
    placed = (
        P(None, "dp", "tensor"),
        P("section", "tensor"),
        P("section", ("tensor", "dp"), None),
        P("section", None, "dp", "tensor"),
        P("section", None, "dp", None, "tensor"),
        P(None, "dp"),
    )
    return jax.shard_map(
        body,
        mesh=mesh,
        in_specs=placed,
        out_specs=(P("section", None, "tensor"), P("section", None, "dp", "tensor")),
        check_vma=False,
    )
```

```python
import functools

import jax
import jax.numpy as jnp
from jax import lax
from jax.experimental import pallas as pl
from jax.experimental.pallas import tpu as pltpu
from jax.sharding import PartitionSpec as P

D = 16384
KVH = 8
HD = 128
GQ = 16
GROUP = 128
LMAX = 16
HALF = GQ // 2
PAIR = 2 * HD
ROW_TILE = 16

epsilon = 1e-05
clip_ratio = 2.0
FIXED = 4
VMEM = 60 << 20
SHORT = pl.CostEstimate(flops=0, bytes_accessed=0, transcendentals=0)


def requantize_kernel(column_ref, w_ref, o_ref):
    ones = jnp.ones((ROW_TILE, GROUP), jnp.bfloat16)
    for start in range(0, w_ref.shape[0], GROUP):
        block = w_ref[start : start + GROUP, :]
        total = jnp.dot(ones, jnp.abs(block), preferred_element_type=jnp.float32)[:1]
        limit = (total * (clip_ratio / GROUP)).astype(jnp.bfloat16)
        o_ref[start : start + GROUP, :] = jnp.minimum(jnp.maximum(block, -limit), limit)


def requantize(weight, indices, own_width, width):
    rows = weight.shape[0]
    tile = min(rows, 4 * GROUP)
    return [
        pl.pallas_call(
            requantize_kernel,
            out_shape=jax.ShapeDtypeStruct((rows, width), jnp.bfloat16),
            grid_spec=pltpu.PrefetchScalarGridSpec(
                num_scalar_prefetch=1,
                grid=(rows // tile,),
                in_specs=[pl.BlockSpec((tile, width), lambda i, column: (i, column[0]))],
                out_specs=pl.BlockSpec((tile, width), lambda i, column: (i, 0)),
            ),
            compiler_params=pltpu.CompilerParams(vmem_limit_bytes=VMEM),
            cost_estimate=SHORT,
        )((index * own_width // width).reshape(1), weight)
        for index in indices
    ]


def project_kernel(layout, lhs_count, has_total, has_held, placed, where_ref, *refs):
    lhs = refs[:lhs_count]
    blocks = refs[lhs_count : lhs_count + len(layout)]
    rest = list(refs[lhs_count + len(layout) :])
    total_ref = rest.pop(0) if has_total else None
    if has_held:
        rest.pop(0)
    o_ref = rest.pop(0)
    segments = [(block, *segment) for block, of_block in zip(blocks, layout) for segment in of_block]

    def copies():
        out, sems = rest
        width = min(out.shape[1], o_ref.shape[1])
        for i, (block, _, start, depth) in enumerate(segments):
            rows = pl.ds(pl.multiple_of(where_ref[FIXED + 2 * i + 1], GROUP), depth)
            columns = pl.ds(pl.multiple_of(pl.program_id(0) * width, HD), width)
            source = block.at[pl.ds(start, depth)]
            if width < block.shape[1]:
                source = block.at[pl.ds(start, depth), pl.ds(pl.multiple_of(where_ref[2], HD), width)]
            yield pltpu.make_async_copy(source, out.at[rows, columns], sems.at[i])

    if placed:

        @pl.when(where_ref[1] == 1)
        def _():
            for copy in copies():
                copy.start()

    @pl.when(where_ref[0] == 1)
    def _():
        total = total_ref[...] if has_total else None
        for i, (block, j, start, depth) in enumerate(segments):
            columns = pl.ds(pl.multiple_of(where_ref[FIXED + 2 * i], GROUP), depth)
            term = jnp.dot(
                lhs[j][:, columns], block[start : start + depth, :], preferred_element_type=jnp.float32
            )
            total = term if total is None else total + term
        o_ref[...] = total

    @pl.when(where_ref[0] == 0)
    def _():
        o_ref[...] = jnp.zeros(o_ref.shape, jnp.float32)

    if placed:

        @pl.when(where_ref[1] == 1)
        def _():
            for copy in copies():
                copy.wait()


def project(active, lhs, terms, total=None, placing=None, rollout=None):
    used = sorted({segment[0] for _, segments in terms for segment in segments})
    lhs = [lhs[j] for j in used]
    rows = lhs[0].shape[0]
    served = terms[0][0].shape[1]
    tile = min(served, 256)
    places, first_column, width = placing or (0, 0, 0)
    where = [active, places, first_column, active | places]
    for _, segments in terms:
        for _, offset, row, _, _ in segments:
            where += [offset, row]
    layout = [[(used.index(j), start, depth) for j, _, _, start, depth in segments] for _, segments in terms]
    count = sum(len(segments) for segments in layout)
    added = () if total is None else (total,)
    held = () if rollout is None else (rollout,)
    column = lambda i, where: (0, i)
    read = lambda i, where: (0, i * where[3])
    anywhere = pl.BlockSpec(memory_space=pl.ANY)
    fresh_shape, fresh_spec = jax.ShapeDtypeStruct((rows, served), jnp.float32), pl.BlockSpec((rows, tile), column)
    return pl.pallas_call(
        functools.partial(project_kernel, layout, len(lhs), bool(added), bool(held), placing is not None),
        out_shape=[fresh_shape, jax.ShapeDtypeStruct((D, width), jnp.bfloat16)] if placing else fresh_shape,
        grid_spec=pltpu.PrefetchScalarGridSpec(
            num_scalar_prefetch=1,
            grid=(served // tile,),
            in_specs=[pl.BlockSpec(part.shape, lambda i, where: (0, 0)) for part in lhs]
            + [pl.BlockSpec((block.shape[0], tile), read) for block, _ in terms]
            + [fresh_spec for _ in added]
            + [anywhere for _ in held],
            out_specs=[fresh_spec, anywhere] if placing else fresh_spec,
            scratch_shapes=[pltpu.SemaphoreType.DMA((count,))] if placing else [],
        ),
        input_output_aliases={1 + len(lhs) + len(terms) + len(added): 1} if held else {},
        compiler_params=pltpu.CompilerParams(vmem_limit_bytes=VMEM),
        cost_estimate=SHORT,
    )(jnp.stack([jnp.asarray(v, jnp.int32) for v in where]), *lhs, *[block for block, _ in terms], *added, *held)


def attend_kernel(share, active_ref, bias_ref, x_ref, q_ref, c_ref, f_ref, held_ref, o_ref):
    heads = share * HALF
    scale = HD ** (-0.5)

    @pl.when((active_ref[0] == 0) & (pl.program_id(0) == 0))
    def _():
        o_ref[...] = held_ref[...]

    @pl.when(active_ref[0] == 1)
    def _():
        bias = jnp.concatenate([bias_ref[0]] * heads, axis=0)
        for g in range(q_ref.shape[1] // (heads * HD)):
            lanes = [slice((g * heads + i) * HD, (g * heads + i + 1) * HD) for i in range(heads)]
            query = jnp.concatenate([q_ref[:, lane] for lane in lanes], axis=0)
            at = g * share * PAIR
            keys = c_ref[:, :, at : at + HD].reshape(ROW_TILE * LMAX, HD)
            values = c_ref[:, :, at + HD : at + PAIR].reshape(ROW_TILE * LMAX, HD)
            fresh = f_ref[:, g * PAIR : (g + 1) * PAIR].astype(jnp.bfloat16).astype(jnp.float32)
            new_key = jnp.concatenate([fresh[:, :HD]] * heads, axis=0)
            new_value = jnp.concatenate([fresh[:, HD:]] * heads, axis=0)
            old = lax.dot_general(query, keys, (((1,), (1,)), ((), ())), preferred_element_type=jnp.float32)
            old = old * scale + bias
            new = jnp.sum(query.astype(jnp.float32) * new_key, axis=1, keepdims=True) * scale
            highest = jnp.maximum(jnp.max(old, axis=1, keepdims=True), new)
            old = jnp.exp(old - highest)
            new = jnp.exp(new - highest)
            inverse = 1.0 / (jnp.sum(old, axis=1, keepdims=True) + new)
            old = (old * inverse).astype(jnp.bfloat16)
            new = (new * inverse).astype(jnp.bfloat16).astype(jnp.float32)
            mixed = jnp.dot(old, values, preferred_element_type=jnp.float32) + new * new_value
            for i, lane in enumerate(lanes):
                total = x_ref[:, lane].astype(jnp.float32) + mixed[i * ROW_TILE : (i + 1) * ROW_TILE, :]
                o_ref[:, lane] = total.astype(jnp.bfloat16)


def seen_bias(lengths):
    column = jnp.arange(ROW_TILE * LMAX)
    own = jnp.arange(ROW_TILE)[:, None] == column[None, :] // LMAX
    seen = own[None] & ((column % LMAX)[None, None, :] < lengths.reshape(-1, ROW_TILE, 1))
    return jnp.where(seen, 0.0, -jnp.inf).astype(jnp.float32)


def attend(active, current, query, cache, bias, fresh, held):
    rows, width = query.shape
    share = min(2, width // (HALF * HD))
    wide = pl.BlockSpec((ROW_TILE, width), lambda i, active: (i * active[0], 0))
    return pl.pallas_call(
        functools.partial(attend_kernel, share),
        out_shape=jax.ShapeDtypeStruct((rows, width), jnp.bfloat16),
        grid_spec=pltpu.PrefetchScalarGridSpec(
            num_scalar_prefetch=1,
            grid=(rows // ROW_TILE,),
            in_specs=[
                pl.BlockSpec((1, *bias.shape[1:]), lambda i, active: (i * active[0], 0, 0)),
                wide,
                wide,
                pl.BlockSpec((ROW_TILE, LMAX, cache.shape[2]), lambda i, active: (i * active[0], 0, 0)),
                pl.BlockSpec((ROW_TILE, fresh.shape[1]), lambda i, active: (i * active[0], 0)),
                pl.BlockSpec((ROW_TILE, width), lambda i, active: (0, 0)),
            ],
            out_specs=wide,
        ),
        input_output_aliases={6: 0},
        compiler_params=pltpu.CompilerParams(vmem_limit_bytes=VMEM),
        cost_estimate=SHORT,
    )(active.reshape(1), bias, current, query, cache, fresh, held)


def together(*values):
    return lax.optimization_barrier(values)


def body(hidden_in, norm_gain, trainer_kv, queries, kv_cache, cache_lengths):
    sections, tensors, dps = (lax.axis_size(axis) for axis in ("section", "tensor", "dp"))
    section, tensor, dp = (lax.axis_index(axis) for axis in ("section", "tensor", "dp"))
    rows = hidden_in.shape[1]
    depth = trainer_kv.shape[1]
    own_width = 2 * KVH * HD // tensors
    served = max(own_width, PAIR)
    early, late = (1, 2), (0, 3)
    everyone = tuple(range(sections))
    is_early = ((section == 1) | (section == 2)).astype(jnp.int32)

    def over(axis, count, value, routes):
        pairs = [(a * count + i, b * count + j) for a, b, i, j in routes]
        return lax.ppermute(value, ("section", axis), pairs)

    def over_dp(value, at, target):
        return over("dp", dps, value, [(s, s, z, target[z]) for s in at for z in range(dps)])

    def over_tensor(value, at, flip, step=0):
        return over("tensor", tensors, value, [(s, s + step, t, t ^ flip) for s in at for t in range(tensors)])

    def flipped(b):
        return [z ^ b for z in range(dps)]

    def feature_block(value, b):
        return lax.dynamic_slice_in_dim(value, (dp ^ b) * depth, depth, 1)

    def normed_of(parts, inverse, gains):
        return [
            (part.astype(jnp.float32) * inverse[:, None] * gain.astype(jnp.float32)).astype(jnp.bfloat16)
            for part, gain in zip(parts, gains)
        ]

    def square_sum(part):
        wide = part.astype(jnp.float32)
        return jnp.sum(wide * wide, axis=1)

    bias = seen_bias(cache_lengths[0])
    turn = [(section == tick).astype(jnp.int32) for tick in range(sections)]

    def attended(tick, current, fresh, held):
        return attend(turn[tick], current, queries[0, 0], kv_cache[0, 0], bias, fresh, held)

    def hop(value, tick):
        return over_tensor(value, (tick - 1,), 0, 1)

    def both(part, tick):
        return [part] + [over_tensor(part, (tick,), j) for j in range(1, tensors)]

    def prepared(parts):
        inverse = lax.rsqrt(sum(square_sum(part) for part in parts) / D + epsilon)
        return normed_of(parts, inverse, gains)

    halves = [[(0, 0)], [(j, (j - 1) * depth) for j in range(1, tensors)], [(j, j * depth) for j in range(tensors)]]

    def straight(at, block):
        return {0: block, 2: over_dp(block, at, flipped(2)), 1: over_dp(block, at, flipped(1))}

    def handed_on(at, blocks):
        return over_dp(blocks[2], at, flipped(1))

    def terms_of(half, blocks, which, shift=0):
        terms = []
        for b in which:
            source = dp ^ b
            terms.append((blocks[b], [
                (j, source * depth + shift, ((tensor ^ j) * dps + source) * depth, start, depth)
                for j, start in halves[half]
            ]))
        return terms

    def placing(active):
        return (active, tensor * own_width % served, own_width)

    weight, hidden, first_kept = together(trainer_kv[0], hidden_in[0], requantize(trainer_kv[0], [tensor], own_width, served))

    squares = square_sum(hidden)
    for j in (2**i for i in range(tensors.bit_length() - 1)):
        squares = squares + over_tensor(squares, (0,), j)
    (normed,) = normed_of([hidden], lax.rsqrt(squares / D + epsilon), [norm_gain])
    first = [feature_block(normed, b) for b in range(dps)]
    weight, first, later = together(weight, first, first_kept[0])
    kept = first_kept + requantize(weight, [tensor ^ j for j in range(1, tensors)], own_width, served)
    first[1:] = [over_dp(first[b], (0,), flipped(b)) for b in range(1, dps)]
    first, gain = together(first, norm_gain)
    gains = [gain] + [over_tensor(gain, everyone, j) for j in range(1, tensors)]

    def others(at, kept):
        received = [over_tensor(kept[j], at, j) for j in range(1, tensors)]
        return received[0] if len(received) == 1 else jnp.concatenate(received, axis=0)

    own = {0: kept[0], 1: over_dp(kept[0], early, flipped(1))}
    own[2] = over_dp(later, early, flipped(2))

    lhs = [jnp.concatenate(first, axis=0)]
    partial = [project(turn[0], lhs, [(kept[j], [(0, 0, 0, 0, depth)])]) for j in range(tensors)]
    partial, kept, gains = together(partial, kept, gains)
    rest = others(early, kept)
    total = partial[0]
    for j in range(1, tensors):
        total = total + over_tensor(partial[j].astype(jnp.bfloat16), (0,), j).astype(jnp.float32)
    total = total.reshape(dps, rows, served)
    step = 1
    while step < dps:
        send = jnp.stack([total[b] for b in range(total.shape[0]) if b & 1]).astype(jnp.bfloat16)
        keep = jnp.stack([total[b] for b in range(total.shape[0]) if not b & 1])
        total = keep + over_dp(send, (0,), flipped(step)).astype(jnp.float32)
        step *= 2
    fresh = total[0]
    result = attended(0, hidden, fresh, hidden)

    rest = straight(early, rest)
    own[1], result = together(own[1], result)
    own, result, kept = together(own, result, kept)
    parts = both(result, 0)
    late_rest = others(late, kept)
    own[3] = handed_on(early, own)
    own, rest = together(own, rest)
    rest[3] = handed_on(early, rest)
    moved = [hop(part, 1) for part in parts]
    normed = prepared(moved)
    terms = terms_of(0, own, range(dps)) + terms_of(1, rest, (0, 1, 2))
    fresh, rollout = project(turn[1], normed, terms, None, placing(is_early))

    token, fresh = together(rest[2][:ROW_TILE, :HD], fresh)
    token = over("dp", dps, token, [(a, b, z, z) for a, b in ((1, 0), (2, 3)) for z in range(dps)])
    token, whole, fresh = together(token, jnp.concatenate([kept[0], late_rest], axis=0), fresh)
    shift = jnp.isnan(token[0, 0]).astype(jnp.int32)
    last = straight(late, whole)

    fresh, rollout, rest = together(fresh, rollout, rest)
    fresh, rollout = project(turn[1], normed, terms_of(1, rest, (3,)), fresh, placing(is_early), rollout)
    result = attended(1, moved[0], fresh, result)

    terms = terms_of(0, own, range(dps)) + terms_of(1, rest, range(dps))
    moved = both(hop(result, 2), 2)
    result = attended(2, moved[0], project(turn[2], prepared(moved), terms), result)
    result, last = together(result, last)
    last[3] = handed_on(late, last)
    moved = both(hop(result, 3), 3)
    normed = prepared(moved)
    fresh, rollout = project(turn[3], normed, terms_of(2, last, (0, 1, 2), shift), None, placing(1 - is_early), rollout)
    fresh, rollout, last = together(fresh, rollout, last)
    fresh, rollout = project(turn[3], normed, terms_of(2, last, (3,)), fresh, placing(1 - is_early), rollout)
    result = attended(3, moved[0], fresh, result)
    return (rollout[None], result[None, None])


def solution(mesh):
    placed = (
        P(None, "dp", "tensor"),
        P("section", "tensor"),
        P("section", ("tensor", "dp"), None),
        P("section", None, "dp", "tensor"),
        P("section", None, "dp", None, "tensor"),
        P(None, "dp"),
    )
    return jax.shard_map(
        body,
        mesh=mesh,
        in_specs=placed,
        out_specs=(P("section", None, "tensor"), P("section", None, "dp", "tensor")),
        check_vma=False,
    )
```
